32 devices in a mesh: member: 2 (over y), gx: 4 (over z), gy: 2 (over x), tracer: 2 (over core).
Axes of the slice: x: 2, y: 2, z: 4, core: 2. Of those that a mesh axis runs over, the one named last changes fastest.
Arguments:
- tracers: bfloat16 [128, 32, 512], P(('member', 'tracer'), 'gx', 'gy'), parts along dimension 0, may hold values from 0.5 to 2
- cotangent: bfloat16 [128, 32, 512], P(('member', 'tracer'), 'gx', 'gy'), parts along dimension 0, may hold values from -6 to 6
- winds: float32 [8, 32, 512], P('member', 'gx', 'gy'), parts along dimension 0, may hold values from -1 to 1
- levels: int32 [128], P(('member', 'tracer')), parts along dimension 0, may hold values from 0 to 1
- conv1: float32 [32, 36], replicated, may hold values from -1 to 1
- bias1: float32 [32], replicated, may hold values from -0.5 to 0.5
- conv2: float32 [32, 288], replicated, may hold values from -0.375 to 0.375
- bias2: float32 [32], replicated, may hold values from -0.5 to 0.5
- head: float32 [18, 32], replicated, may hold values from -1 to 1
Outputs:
- tracer_grad: bfloat16 [128, 32, 512], P(('member', 'tracer'), 'gx', 'gy'), parts along dimension 0
- wind_grad: float32 [8, 32, 512], P('member', 'gx', 'gy'), parts along dimension 0
- conv1_grad: float32 [64, 36], P('member'), parts along dimension 0
- bias1_grad: float32 [64], P('member'), parts along dimension 0
- conv2_grad: float32 [64, 288], P('member'), parts along dimension 0
- bias2_grad: float32 [64], P('member'), parts along dimension 0
- head_grad: float32 [36, 32], P('member'), parts along dimension 0
The draws below stay inside these ranges and needn't reach their ends.
There are 2 independent parts, one for each index of `member`. The reference program is written for one: setup_inputs(seed, part) draws one part's arguments, and reference() takes and returns one part's arrays. A program takes and returns all parts, laid end to end along the dimension named above; an argument that names none is the same for every part. Nothing has to cross between parts.
All inputs are finite; a program needn't handle non-finite values.
Results may differ from the reference program's by a relative error of at most 0.001.
Values may be sent and summed in bfloat16 or wider, within the bound.
No kernel may reach another device: no remote copies, remote signals or barrier semaphores. Data moves between devices by JAX's collectives and lax.ppermute only.
A program may use at most 64 MiB of HBM per device.

```python
import math
import jax
import jax.numpy as jnp
from jax import lax

CH = 32
LEVELS = 2
COEF = 18
WIND = 4
TRACERS = 64
NX = 32
NY = 512


def set_ends(entries, key, low, top_value):
    longest = entries.shape.index(max(entries.shape))
    spots = []
    for shift in (0, 1):
        where = [jax.random.randint(jax.random.fold_in(key, axis), (), 0, length) for axis, length in enumerate(entries.shape)]
        where[longest] = (where[longest] + shift) % entries.shape[longest]
        spots.append(tuple(where))
    return entries.at[spots[0]].set(low).at[spots[1]].set(top_value)


def shard_levels(rng, extent, pieces, low, high):
    factor_of = 1.0
    for position, shards_of in pieces:
        heights = jax.random.uniform(jax.random.fold_in(jax.random.fold_in(rng, 6), position), (shards_of,), jnp.float32, low / len(pieces), high / len(pieces))
        factor_of = factor_of * jnp.repeat(jnp.exp(heights), extent[position] // shards_of).reshape((-1,) + (1,) * (len(extent) - 1 - position))
    return factor_of


def scatter_about(rng, shape, deviation, reach, split=(), kind=jnp.bfloat16):
    entries = deviation * jax.random.normal(rng, shape, jnp.float32)
    if split:
        entries = entries * shard_levels(rng, shape, split, -0.22, 0.18)
    return jnp.clip(entries, -reach, reach).astype(kind)


def setup_inputs(seed: int = 0, part: int = 0) -> dict:
    streams_of = jax.random.split(jax.random.key(seed), 10)
    part_splits = jax.random.split(jax.random.fold_in(streams_of[9], part), 10)
    return {
        "tracers": jnp.clip(jnp.exp(math.log(2.0) - 1.3862944 * jax.random.uniform(part_splits[0], (TRACERS, NX, NY), jnp.float32) ** shard_levels(part_splits[0], (TRACERS, NX, NY), ((0, 2), (1, 4), (2, 2)), -0.2, 0.2)), 0.5, 2.0).astype(jnp.bfloat16),
        "cotangent": scatter_about(part_splits[1], (TRACERS, NX, NY), 1.0, 6.0, ((0, 2), (1, 4), (2, 2))),
        "winds": jnp.clip(jax.random.uniform(part_splits[2], (WIND, NX, NY), jnp.float32, -1.0, 1.0) * shard_levels(part_splits[2], (WIND, NX, NY), ((1, 4), (2, 2)), -0.4, 0.0), -1.0, 1.0),
        "levels": set_ends(jax.random.randint(part_splits[3], (TRACERS,), 0, LEVELS), jax.random.fold_in(part_splits[3], 1), 0, LEVELS - 1).astype(jnp.int32),
        "conv1": scatter_about(streams_of[4], (CH, WIND * 9), (WIND * 9) ** -0.5, 1.0, (), jnp.float32),
        "bias1": jnp.clip(jax.random.uniform(streams_of[5], (CH,), jnp.float32, -0.5, 0.5), -0.5, 0.5),
        "conv2": scatter_about(streams_of[6], (CH, CH * 9), (CH * 9) ** -0.5, 0.375, (), jnp.float32),
        "bias2": jnp.clip(jax.random.uniform(streams_of[7], (CH,), jnp.float32, -0.5, 0.5), -0.5, 0.5),
        "head": scatter_about(streams_of[8], (COEF, CH), CH ** -0.5, 1.0, (), jnp.float32),
    }


COURANT = 0.5
CORRECTION = 0.2
OFFSETS = tuple(((step_x, step_y) for step_x in (-1, 0, 1) for step_y in (-1, 0, 1)))

def shifted(field, step_x, step_y):
    moved = jnp.roll(field, -step_x, axis=-2)
    if step_y == 1:
        return jnp.concatenate([moved[..., 1:], jnp.zeros_like(moved[..., :1])], axis=-1)
    if step_y == -1:
        return jnp.concatenate([jnp.zeros_like(moved[..., :1]), moved[..., :-1]], axis=-1)
    return moved

def lax_wendroff(courant):
    return jnp.stack([0.5 * courant + 0.5 * courant * courant, 1.0 - courant * courant, 0.5 * courant * courant - 0.5 * courant], axis=1)

def coef_cells(winds, hidden, head):
    paired = winds.reshape((LEVELS, 2) + winds.shape[1:]) * COURANT
    along_x = lax_wendroff(paired[:, 0])
    along_y = lax_wendroff(paired[:, 1])
    base = (along_x[:, :, None] * along_y[:, None, :]).reshape((LEVELS, 9) + winds.shape[1:])
    raw = jnp.einsum('kc,cxy->kxy', head, hidden, precision=lax.Precision.HIGHEST)
    raw = raw.reshape((LEVELS, 9) + winds.shape[1:])
    return base + CORRECTION * (raw - lax.optimization_barrier(jnp.mean(raw, axis=1, keepdims=True)))

def convolve(field, weights, biases):
    kernel = weights.reshape(weights.shape[0], field.shape[0], 9)
    total = jnp.zeros((weights.shape[0],) + field.shape[1:], jnp.float32) + biases[:, None, None]
    for offset, (step_x, step_y) in enumerate(OFFSETS):
        total = total + jnp.einsum('oi,ixy->oxy', kernel[:, :, offset], shifted(field, step_x, step_y), precision=lax.Precision.HIGHEST)
    return total

def coefficients(winds, conv1, bias1, conv2, bias2, head):
    first = jnp.tanh(convolve(winds, conv1, bias1))
    second = jnp.tanh(convolve(first, conv2, bias2))
    return coef_cells(winds, second, head)

def reference(tracers, cotangent, winds, levels, conv1, bias1, conv2, bias2, head):
    coefs, pullback = jax.vjp(coefficients, winds, conv1, bias1, conv2, bias2, head)

    def accumulate(running, entry):
        field, adjoint, level = entry
        marker = (jnp.arange(LEVELS, dtype=jnp.int32) == level).astype(jnp.float32)
        field = field.astype(jnp.float32)
        adjoint = adjoint.astype(jnp.float32)
        products = jnp.stack([adjoint * shifted(field, step_x, step_y) for step_x, step_y in OFFSETS], 0)
        return (running + marker[:, None, None, None] * products[None], None)
    coef_grad, unused = lax.scan(accumulate, jnp.zeros(coefs.shape, jnp.float32), (tracers, cotangent, levels))

    def backward_one(entry):
        adjoint, level = entry
        chosen = lax.dynamic_index_in_dim(coefs, level, 0, keepdims=False)
        adjoint = adjoint.astype(jnp.float32)
        total = jnp.zeros(adjoint.shape, jnp.float32)
        for offset, (step_x, step_y) in enumerate(OFFSETS):
            total = total + shifted(chosen[offset] * adjoint, -step_x, -step_y)
        return total.astype(jnp.bfloat16)
    tracer_grad = lax.map(backward_one, (cotangent, levels))
    wind_grad, conv1_grad, bias1_grad, conv2_grad, bias2_grad, head_grad = pullback(coef_grad)
    return (tracer_grad, wind_grad, conv1_grad, bias1_grad, conv2_grad, bias2_grad, head_grad)
```

```python
import functools

import jax
import jax.numpy as jnp
from jax import lax
from jax.experimental import pallas as pl
from jax.experimental.pallas import tpu as pltpu
from jax.sharding import PartitionSpec as P

LEVELS = 2
CH = 32
COURANT = 0.5
CORRECTION = 0.2
STEPS = (-1, 0, 1)
HALO = 4
LANES = 128
F32 = jnp.float32
BF16 = jnp.bfloat16
NT = (((1,), (1,)), ((), ()))


def pieces(array, count):
    parts = []
    for _ in range(count):
        part = lax.reduce_precision(array, 8, 7)
        parts.append(part)
        array = array - part
    return parts


def halves(value):
    high = value.astype(BF16)
    return high, (value - high.astype(F32)).astype(BF16)


def dot3(weights, high, low):
    rows = weights.shape[0] // 2
    both = jnp.dot(weights, high, preferred_element_type=F32)
    rest = jnp.dot(weights[:rows], low, preferred_element_type=F32)
    return both[:rows] + both[rows:] + rest


def dot3_nt(a_high, a_low, b_high, b_low):
    out = lax.dot_general(a_high, b_high, NT, preferred_element_type=F32)
    out = out + lax.dot_general(a_high, b_low, NT, preferred_element_type=F32)
    return out + lax.dot_general(a_low, b_high, NT, preferred_element_type=F32)


def turn(value, step, axis):
    shift = (-step) % value.shape[axis]
    return pltpu.roll(value, shift, axis) if shift else value


def load_field(index, main_ref, below_ref, above_ref):
    strip = jnp.concatenate([below_ref[index].astype(F32), above_ref[index].astype(F32)], axis=0)
    return jnp.concatenate([main_ref[index].astype(F32), strip], axis=0)


def grad_kernel(levels_ref, main_ref, below_ref, above_ref, out_ref, moved_ref, cot_ref):
    count = levels_ref.shape[0]

    def fill(t, carry):
        field = load_field(t, main_ref, below_ref, above_ref)
        for b in range(3):
            moved_ref[b, t] = turn(field, STEPS[b], 1)
        cot_ref[t] = load_field(count + t, main_ref, below_ref, above_ref)
        return carry

    lax.fori_loop(0, count, fill, 0, unroll=4)
    for a in range(3):
        for b in range(3):

            def step(t, sums):
                product = cot_ref[t] * turn(moved_ref[b, t], STEPS[a], 0)
                upper = levels_ref[t].astype(F32)
                return sums[0] + product, sums[1] + upper * product

            zero = jnp.zeros(out_ref.shape[1:], F32)
            total, second = lax.fori_loop(0, count, step, (zero, zero), unroll=4)
            out_ref[3 * a + b] = total - second
            out_ref[9 + 3 * a + b] = second


def put_moved(high_ref, low_ref, row, value, sign):
    width = value.shape[1]
    for b in range(3):
        high, low = halves(turn(value, sign * STEPS[b], 1))
        high_ref[b * CH : (b + 1) * CH, row * width : (row + 1) * width] = high
        low_ref[b * CH : (b + 1) * CH, row * width : (row + 1) * width] = low


def put_winds(wind_ref, stack_ref, first_row, rows):
    width = wind_ref.shape[2]
    count = wind_ref.shape[0]
    for row in range(rows):
        value = wind_ref[:, first_row + row, :]
        for b in range(3):
            stack_ref[b * count : (b + 1) * count, row * width : (row + 1) * width] = turn(value, STEPS[b], 1)


def forward_kernel(wind_ref, inside_ref, w1_ref, b1_ref, w2_ref, b2_ref, head_ref, first_ref, second_ref, corr_ref, stack_ref, high_ref, low_ref):
    rows, width = wind_ref.shape[1:]
    stack_ref[...] = jnp.zeros(stack_ref.shape, F32)
    put_winds(wind_ref, stack_ref, 0, rows)
    bias1, bias2 = b1_ref[...], b2_ref[...]
    inside = jnp.concatenate([inside_ref[...]] * 2, axis=1)
    for row in range(0, rows - 2, 2):
        total = jnp.zeros((CH, 2 * width), F32) + bias1
        for a in range(3):
            high, low = halves(stack_ref[:, (row + a) * width : (row + a + 2) * width])
            total = total + dot3(w1_ref[a], high, low)
        value = jnp.tanh(total) * inside
        first_ref[:, row * width : (row + 2) * width] = value
        for part in range(2):
            put_moved(high_ref, low_ref, row + part, value[:, part * width : (part + 1) * width], 1)
    for row in range(0, rows - 4, 2):
        total = jnp.zeros((CH, 2 * width), F32) + bias2
        for a in range(3):
            where = slice((row + a) * width, (row + a + 2) * width)
            total = total + dot3(w2_ref[a], high_ref[:, where], low_ref[:, where])
        value = jnp.tanh(total)
        second_ref[:, row * width : (row + 2) * width] = value
        high, low = halves(value)
        corr = dot3(head_ref[...], high, low)
        for part in range(2):
            corr_ref[:, 2 + row + part, :] = corr[: corr_ref.shape[0], part * width : (part + 1) * width]


def backward_kernel(
    mine_ref, other_ref, wind_ref, inside_ref, first_ref, second_ref, headt_ref, w2b_ref, w1b_ref,
    wgrad_ref, par_ref,
    sum_ref, g_ref, d2_high, d2_low, own2_high, own2_low, act_high, act_low, d1_high, d1_low, own1_high, own1_low, wind_stack, net_ref,
):
    cells = g_ref.shape[1]
    width = wind_ref.shape[2]
    cols = wgrad_ref.shape[2]
    ring = cells // width
    tile = ring - 4
    sum_ref[...] = mine_ref[...] + other_ref[...]
    wrap = sum_ref.shape[1]
    nine = sum_ref.shape[0]
    g_ref[...] = jnp.zeros(g_ref.shape, F32)
    for row in range(ring):
        g_ref[:nine, row * width : (row + 1) * width] = sum_ref[:, (row - 2) % wrap, :]
    own = lax.broadcasted_iota(jnp.int32, (1, width), 1) < cols
    inside = inside_ref[...]
    for ref in (own2_high, own2_low, own1_high, own1_low):
        ref[...] = jnp.zeros(ref.shape, BF16)
    wind_stack[...] = jnp.zeros(wind_stack.shape, F32)
    put_winds(wind_ref, wind_stack, 3, tile + 2)
    wind_stack[12:13, :] = jnp.ones((1, wind_stack.shape[1]), F32)
    act_high[3 * CH :, :] = jnp.ones((act_high.shape[0] - 3 * CH, act_high.shape[1]), BF16)
    act_low[3 * CH :, :] = jnp.zeros((act_high.shape[0] - 3 * CH, act_high.shape[1]), BF16)

    def put_own(high_ref, low_ref, x, value):
        high, low = halves(jnp.where(own, value, 0.0))
        for a in range(3):
            high_ref[a * CH : (a + 1) * CH, (x + a) * width : (x + a + 1) * width] = high
            low_ref[a * CH : (a + 1) * CH, (x + a) * width : (x + a + 1) * width] = low

    for row in range(0, ring, 2):
        where = slice(row * width, (row + 2) * width)
        high, low = halves(g_ref[:, where])
        hidden = dot3(headt_ref[...], high, low)
        second = second_ref[:, where]
        delta = hidden * (1.0 - second * second)
        for part in range(2):
            value = delta[:, part * width : (part + 1) * width]
            put_moved(d2_high, d2_low, row + part, value, -1)
            x = row + part - 2
            if 0 <= x < tile:
                put_own(own2_high, own2_low, x, value)
    for row in range(tile + 2):
        put_moved(act_high, act_low, row, first_ref[:, (row + 2) * width : (row + 3) * width], 1)
    limit = act_high.shape[0]
    out2 = dot3_nt(act_high[...], act_low[...], own2_high[...], own2_low[...])
    par_ref[:limit, : 3 * CH] = out2
    inside2 = jnp.concatenate([inside] * 2, axis=1)
    for row in range(0, tile + 2, 2):
        total = jnp.zeros((CH, 2 * width), F32)
        for a in range(3):
            start = row + 1 - STEPS[a]
            where = slice(start * width, (start + 2) * width)
            total = total + dot3(w2b_ref[a], d2_high[:, where], d2_low[:, where])
        first = first_ref[:, (row + 2) * width : (row + 4) * width]
        delta = total * (1.0 - first * first) * inside2
        for part in range(2):
            value = delta[:, part * width : (part + 1) * width]
            put_moved(d1_high, d1_low, row + part, value, -1)
            x = row + part - 1
            if 0 <= x < tile:
                put_own(own1_high, own1_low, x, value)
    high, low = halves(wind_stack[...])
    par_ref[limit : limit + 16, : 3 * CH] = dot3_nt(high, low, own1_high[...], own1_low[...])
    mid = slice(2 * width, (2 + tile) * width)
    own_rows = jnp.concatenate([own] * tile, axis=1)
    g_high, g_low = halves(jnp.where(own_rows, g_ref[:, mid], 0.0))
    s_high, s_low = halves(second_ref[:, mid])
    raw = dot3_nt(g_high, g_low, s_high, s_low)
    place = lax.broadcasted_iota(jnp.int32, raw.shape, 0)
    mean0 = jnp.sum(jnp.where(place < 9, raw, 0.0), axis=0, keepdims=True) / 9.0
    mean1 = jnp.sum(jnp.where((place >= 9) & (place < 18), raw, 0.0), axis=0, keepdims=True) / 9.0
    par_ref[limit + 16 : limit + 16 + CH, :CH] = CORRECTION * (raw - jnp.where(place < 9, mean0, mean1))
    for row in range(0, tile, 2):
        total = jnp.zeros((16, 2 * width), F32)
        for a in range(3):
            start = row + 1 - STEPS[a]
            where = slice(start * width, (start + 2) * width)
            total = total + dot3(w1b_ref[a], d1_high[:, where], d1_low[:, where])
        for part in range(2):
            net_ref[:, row + part, :] = total[:4, part * width : part * width + cols]
    for level in range(LEVELS):
        cx = COURANT * wind_ref[2 * level, HALO : HALO + tile, :cols]
        cy = COURANT * wind_ref[2 * level + 1, HALO : HALO + tile, :cols]
        px, py = lax_wendroff(cx), lax_wendroff(cy)
        dx, dy = (0.5 + cx, -2.0 * cx, cx - 0.5), (0.5 + cy, -2.0 * cy, cy - 0.5)
        gx_sum = jnp.zeros((tile, cols), F32)
        gy_sum = jnp.zeros((tile, cols), F32)
        for a in range(3):
            for b in range(3):
                grad = sum_ref[9 * level + 3 * a + b, :tile, :cols]
                gx_sum = gx_sum + grad * (dx[a] * py[b])
                gy_sum = gy_sum + grad * (px[a] * dy[b])
        wgrad_ref[2 * level] = COURANT * gx_sum + net_ref[2 * level]
        wgrad_ref[2 * level + 1] = COURANT * gy_sum + net_ref[2 * level + 1]


def lax_wendroff(courant):
    return (
        0.5 * courant + 0.5 * courant * courant,
        1.0 - courant * courant,
        0.5 * courant * courant - 0.5 * courant,
    )


def tracer_kernel(levels_ref, wind_ref, corr_ref, main_ref, below_ref, above_ref, out_ref, coef_ref):
    count, tile, cols = out_ref.shape
    for level in range(LEVELS):
        px = lax_wendroff(COURANT * wind_ref[2 * level])
        py = lax_wendroff(COURANT * wind_ref[2 * level + 1])
        for a in range(3):
            for b in range(3):
                coef = corr_ref[9 * level + 3 * a + b] + px[a] * py[b]
                coef = turn(turn(coef, -STEPS[b], 1), HALO - STEPS[a], 0)
                coef_ref[level, 3 * a + b] = coef[:tile, :cols]

    def step(t, carry):
        level = levels_ref[t]
        field = load_field(count + t, main_ref, below_ref, above_ref)
        total = jnp.zeros((tile, cols), F32)
        for b in range(3):
            moved = turn(field, -STEPS[b], 1)
            for a in range(3):
                total = total + coef_ref[level, 3 * a + b] * turn(moved, -STEPS[a], 0)[:tile, :cols]
        out_ref[t] = total.astype(BF16)
        return carry

    lax.fori_loop(0, count, step, 0, unroll=4)


def call(kernel, outs, scratch, smem, operands, flops):
    specs = [pl.BlockSpec(memory_space=pltpu.SMEM if i < smem else pltpu.VMEM) for i in range(len(operands))]
    whole = pl.BlockSpec(memory_space=pltpu.VMEM)
    return pl.pallas_call(
        kernel,
        out_shape=outs,
        in_specs=specs,
        out_specs=[whole] * len(outs) if isinstance(outs, (list, tuple)) else whole,
        scratch_shapes=scratch,
        compiler_params=pltpu.CompilerParams(vmem_limit_bytes=40 * 1024 * 1024),
        cost_estimate=pl.CostEstimate(flops=flops, bytes_accessed=2_000_000, transcendentals=0),
    )(*operands)


def stacked(weights):
    return jnp.concatenate(pieces(weights, 2), axis=-2).astype(BF16)


def pad_to(array, rows, cols):
    widths = [(0, 0)] * (array.ndim - 2) + [(0, rows - array.shape[-2]), (0, cols - array.shape[-1])]
    return jnp.pad(array, widths)


def ring_pairs(size, wrap):
    up = [(i, (i + 1) % size) for i in range(size if wrap else size - 1)]
    return up, [(j, i) for i, j in up]


def sum_over(value, axis):
    size = lax.axis_size(axis)
    if size & (size - 1):
        return lax.psum(value, axis)
    step = 1
    while step < size:
        value = value + lax.ppermute(value, axis, [(i, i ^ step) for i in range(size)])
        step *= 2
    return value


def body(tracers, cotangent, winds, levels, conv1, bias1, conv2, bias2, head):
    count, tile, cols = tracers.shape
    n_wind = winds.shape[0]
    width = cols + LANES
    rows = tile + 2 * HALO
    gy, gy_size = lax.axis_index("gy"), lax.axis_size("gy")
    field = jnp.concatenate([tracers, cotangent] + [p.astype(BF16) for p in pieces(winds, 3)], axis=0)
    head_cols, tail_cols = field[..., :LANES], field[..., cols - LANES :]
    lane = lax.broadcasted_iota(jnp.int32, (1, 1, LANES), 2)
    up, down = ring_pairs(gy_size, False)
    if gy_size == 2:
        got = lax.ppermute(jnp.where(gy == 0, tail_cols, head_cols), "gy", up + down)
        side = jnp.where(jnp.where(gy == 0, lane < HALO, lane >= LANES - HALO), got, 0)
    else:
        right = lax.ppermute(head_cols, "gy", down)
        left = lax.ppermute(tail_cols, "gy", up)
        side = jnp.where(lane < HALO, right, jnp.where(lane >= LANES - HALO, left, 0))
    side = side.astype(BF16)
    main = jnp.concatenate([field, side], axis=2)
    up, down = ring_pairs(lax.axis_size("gx"), True)
    above = lax.ppermute(main[:, tile - HALO :], "gx", up)
    below = lax.ppermute(main[:, :HALO], "gx", down)

    def wind_of(part):
        split = part[2 * count :].astype(F32)
        return split[:n_wind] + split[n_wind : 2 * n_wind] + split[2 * n_wind :]

    wind_ext = jnp.concatenate([wind_of(above), wind_of(main), wind_of(below)], axis=1)
    place = lax.broadcasted_iota(jnp.int32, (1, width), 1)
    has_right, has_left = gy < gy_size - 1, gy > 0
    inside = jnp.where(place < cols, True, jnp.where(place < cols + LANES // 2, has_right, has_left)).astype(F32)

    split1 = conv1.reshape(CH, n_wind, 3, 3)
    split2 = conv2.reshape(CH, CH, 3, 3)
    w1 = stacked(pad_to(split1.transpose(2, 0, 3, 1).reshape(3, CH, 3 * n_wind), CH, 16))
    w2 = stacked(split2.transpose(2, 0, 3, 1).reshape(3, CH, 3 * CH))
    w2b = stacked(split2.transpose(2, 1, 3, 0).reshape(3, CH, 3 * CH))
    w1b = stacked(pad_to(split1.transpose(2, 1, 3, 0).reshape(3, n_wind, 3 * CH), 16, 3 * CH))
    by_level = head.reshape(LEVELS, 9, CH)
    centred = (CORRECTION * (by_level - jnp.mean(by_level, axis=1, keepdims=True))).reshape(9 * LEVELS, CH)
    head_w = stacked(pad_to(centred, CH, CH))
    head_t = stacked(pad_to(centred.T, CH, CH))

    vmem = pltpu.VMEM
    mine = call(
        grad_kernel,
        jax.ShapeDtypeStruct((9 * LEVELS, rows, width), F32),
        [vmem((3, count, rows, width), F32), vmem((count, rows, width), F32)],
        1,
        (levels, main, below, above),
        2_000_000,
    )
    pairs = [(i, i ^ 1) for i in range(lax.axis_size("tracer"))]
    other = lax.ppermute(mine, "tracer", pairs)
    first, second, corr = call(
        forward_kernel,
        [
            jax.ShapeDtypeStruct((CH, (rows - 2) * width), F32),
            jax.ShapeDtypeStruct((CH, (rows - 4) * width), F32),
            jax.ShapeDtypeStruct((9 * LEVELS, rows, width), F32),
        ],
        [vmem((16, rows * width), F32)] + [vmem((3 * CH, (rows - 2) * width), BF16)] * 2,
        0,
        (wind_ext, inside, w1, bias1[:, None], w2, bias2[:, None], head_w),
        2_000_000,
    )
    ring, own = (tile + 4) * width, (tile + 2) * width
    wind_grad, params = call(
        backward_kernel,
        [jax.ShapeDtypeStruct((n_wind, tile, cols), F32), jax.ShapeDtypeStruct((160, LANES), F32)],
        [vmem((9 * LEVELS, rows, width), F32), vmem((CH, ring), F32)]
        + [vmem((3 * CH, ring), BF16)] * 2
        + [vmem((3 * CH, own), BF16)] * 2
        + [vmem((3 * CH + 16, own), BF16)] * 2
        + [vmem((3 * CH, own), BF16)] * 4
        + [vmem((16, own), F32), vmem((n_wind, tile, cols), F32)],
        0,
        (mine, other, wind_ext, inside, first, second, head_t, w2b, w1b),
        2_000_000,
    )
    params = sum_over(sum_over(params, "gy"), "gx")
    tracer_grad = call(
        tracer_kernel,
        jax.ShapeDtypeStruct((count, tile, cols), BF16),
        [vmem((LEVELS, 9, tile, cols), F32)],
        1,
        (levels, wind_ext, corr, main, below, above),
        2_000_000,
    )
    conv2_grad = params[: 3 * CH, : 3 * CH].reshape(3, CH, 3, CH).transpose(3, 1, 2, 0).reshape(CH, 9 * CH)
    bias2_grad = params[3 * CH, CH : 2 * CH]
    low = params[3 * CH + 16 : 3 * CH + 32, : 3 * CH]
    conv1_grad = low[: 3 * n_wind].reshape(3, n_wind, 3, CH).transpose(3, 1, 2, 0).reshape(CH, 9 * n_wind)
    bias1_grad = low[3 * n_wind, CH : 2 * CH]
    head_grad = params[3 * CH + 32 : 3 * CH + 32 + 9 * LEVELS, :CH]
    return (tracer_grad, wind_grad, conv1_grad, bias1_grad, conv2_grad, bias2_grad, head_grad)


def solution(mesh):
    return jax.shard_map(
        body,
        mesh=mesh,
        in_specs=(
            P(("member", "tracer"), "gx", "gy"),
            P(("member", "tracer"), "gx", "gy"),
            P("member", "gx", "gy"),
            P(("member", "tracer")),
            P(),
            P(),
            P(),
            P(),
            P(),
        ),
        out_specs=(
            P(("member", "tracer"), "gx", "gy"),
            P("member", "gx", "gy"),
            P("member", None),
            P("member"),
            P("member", None),
            P("member"),
            P("member", None),
        ),
        check_vma=False,
    )
```

```python
import functools

import jax
import jax.numpy as jnp
from jax import lax
from jax.experimental import pallas as pl
from jax.experimental.pallas import tpu as pltpu
from jax.sharding import PartitionSpec as P

LEVELS = 2
CH = 32
COURANT = 0.5
CORRECTION = 0.2
STEPS = (-1, 0, 1)
HALO = 4
LANES = 128
GROUP = LANES // (2 * HALO)
F32 = jnp.float32
BF16 = jnp.bfloat16
NT = (((1,), (1,)), ((), ()))


def pieces(array, count):
    parts = []
    for _ in range(count):
        part = lax.reduce_precision(array, 8, 7)
        parts.append(part)
        array = array - part
    return parts


def halves(value):
    high = value.astype(BF16)
    return high, (value - high.astype(F32)).astype(BF16)


def dot3(weights, high, low):
    rows = weights.shape[0] // 2
    both = jnp.dot(weights, high, preferred_element_type=F32)
    rest = jnp.dot(weights[:rows], low, preferred_element_type=F32)
    return both[:rows] + both[rows:] + rest


def dot3_nt(a_high, a_low, b_high, b_low):
    out = lax.dot_general(a_high, b_high, NT, preferred_element_type=F32)
    out = out + lax.dot_general(a_high, b_low, NT, preferred_element_type=F32)
    return out + lax.dot_general(a_low, b_high, NT, preferred_element_type=F32)


def turn(value, step, axis):
    shift = (-step) % value.shape[axis]
    return pltpu.roll(value, shift, axis) if shift else value


def side_mask():
    lane = lax.broadcasted_iota(jnp.int32, (1, LANES), 1)
    return (lane < HALO) | (lane >= LANES - HALO)


def rows_of(below, above):
    return jnp.concatenate([below.astype(F32), above.astype(F32)], axis=0)


def sides_of(group, side_ref, below_ref, above_ref, channels):
    index = channels + group % 3
    where = slice(group // 3 * LANES, (group // 3 + 1) * LANES)
    return side_ref[group].astype(F32), rows_of(below_ref[index, :, where], above_ref[index, :, where])


def placed(side, j):
    return jnp.where(side_mask(), pltpu.roll(side, LANES - HALO - 2 * HALO * j, 1), 0.0)


def load_field(index, main, below_ref, above_ref, sides, j):
    top = jnp.concatenate([main.astype(F32), placed(sides[0], j)], axis=1)
    strip = jnp.concatenate([rows_of(below_ref[index], above_ref[index]), placed(sides[1], j)], axis=1)
    return jnp.concatenate([top, strip], axis=0)


def pack_kernel(tracer_ref, cot_ref, wind_ref, out_ref):
    count = tracer_ref.shape[0]
    cols = tracer_ref.shape[2]
    lane = lax.broadcasted_iota(jnp.int32, (1, LANES), 1)
    mask = side_mask()

    def lifted(head, tail, j):
        both = jnp.where(lane < HALO, head, tail)
        return pltpu.roll(jnp.where(mask, both, 0.0), HALO + 2 * HALO * j, 1)

    group = 0
    for ref in (tracer_ref, cot_ref):
        for start in range(0, count, GROUP):
            total = jnp.zeros(out_ref.shape[1:], F32)
            for j in range(GROUP):
                head = ref[start + j, :, :LANES].astype(F32)
                tail = ref[start + j, :, cols - LANES :].astype(F32)
                total = total + lifted(head, tail, j)
            out_ref[group] = total.astype(BF16)
            group += 1
    total = jnp.zeros(out_ref.shape[1:], F32)
    for i in range(wind_ref.shape[0]):
        head, tail = wind_ref[i, :, :LANES], wind_ref[i, :, cols - LANES :]
        for part in range(3):
            high_head, high_tail = head.astype(BF16).astype(F32), tail.astype(BF16).astype(F32)
            total = total + lifted(high_head, high_tail, part * wind_ref.shape[0] + i)
            head, tail = head - high_head, tail - high_tail
    out_ref[group] = total.astype(BF16)
    out_ref[group + 1] = jnp.zeros(out_ref.shape[1:], BF16)


def grad_kernel(levels_ref, tracer_ref, cot_ref, side_ref, below_ref, above_ref, out_ref, moved_ref, held_ref):
    count = levels_ref.shape[0]
    channels = below_ref.shape[0] - 3
    groups = count // GROUP
    for group in range(groups):
        near = sides_of(group, side_ref, below_ref, above_ref, channels)
        far = sides_of(groups + group, side_ref, below_ref, above_ref, channels)

        def fill(j, carry):
            t = group * GROUP + j
            field = load_field(t, tracer_ref[t], below_ref, above_ref, near, j)
            for b in range(3):
                moved_ref[b, t] = turn(field, STEPS[b], 1)
            held_ref[t] = load_field(count + t, cot_ref[t], below_ref, above_ref, far, j)
            return carry

        lax.fori_loop(0, GROUP, fill, 0, unroll=4)
    for a in range(3):
        for b in range(3):

            def step(t, sums):
                product = held_ref[t] * turn(moved_ref[b, t], STEPS[a], 0)
                upper = levels_ref[t].astype(F32)
                return sums[0] + product, sums[1] + upper * product

            zero = jnp.zeros(out_ref.shape[1:], F32)
            total, second = lax.fori_loop(0, count, step, (zero, zero), unroll=4)
            out_ref[3 * a + b] = total - second
            out_ref[9 + 3 * a + b] = second


def put_moved(high_ref, low_ref, row, value, sign):
    width = value.shape[1]
    for b in range(3):
        high, low = halves(turn(value, sign * STEPS[b], 1))
        high_ref[b * CH : (b + 1) * CH, row * width : (row + 1) * width] = high
        low_ref[b * CH : (b + 1) * CH, row * width : (row + 1) * width] = low


def put_winds(wind_ref, stack_ref, first_row, rows):
    width = wind_ref.shape[2]
    count = wind_ref.shape[0]
    for row in range(rows):
        value = wind_ref[:, first_row + row, :]
        for b in range(3):
            stack_ref[b * count : (b + 1) * count, row * width : (row + 1) * width] = turn(value, STEPS[b], 1)


def forward_kernel(
    own_ref, side_ref, below_ref, above_ref, inside_ref, w1_ref, b1_ref, w2_ref, b2_ref, head_ref,
    first_ref, second_ref, corr_ref, wind_ref,
    stack_ref, high_ref, low_ref,
):
    count, rows, width = wind_ref.shape
    tile, cols = own_ref.shape[1:]
    channels = below_ref.shape[0] - 3
    side, side_rows = sides_of((channels - 3 * count) // GROUP, side_ref, below_ref, above_ref, channels)
    for i in range(count):
        wind_ref[i, HALO : HALO + tile, :cols] = own_ref[i]
        wide = [jnp.zeros((tile, LANES), F32), jnp.zeros((tile, LANES), F32)]
        strip = jnp.zeros((2 * HALO, cols), F32)
        for part in range(3):
            j = part * count + i
            wide[0] = wide[0] + placed(side, j)
            wide[1] = wide[1] + placed(side_rows, j)
            index = channels - 3 * count + j
            strip = strip + rows_of(below_ref[index], above_ref[index])
        wind_ref[i, HALO : HALO + tile, cols:] = wide[0]
        for value, where in ((strip, slice(0, cols)), (wide[1], slice(cols, width))):
            wind_ref[i, HALO + tile :, where] = value[:HALO]
            wind_ref[i, :HALO, where] = value[HALO:]
    stack_ref[...] = jnp.zeros(stack_ref.shape, F32)
    put_winds(wind_ref, stack_ref, 0, rows)
    bias1, bias2 = b1_ref[...], b2_ref[...]
    inside = jnp.concatenate([inside_ref[...]] * 2, axis=1)
    for row in range(0, rows - 2, 2):
        total = jnp.zeros((CH, 2 * width), F32) + bias1
        for a in range(3):
            high, low = halves(stack_ref[:, (row + a) * width : (row + a + 2) * width])
            total = total + dot3(w1_ref[a], high, low)
        value = jnp.tanh(total) * inside
        first_ref[:, row * width : (row + 2) * width] = value
        for part in range(2):
            put_moved(high_ref, low_ref, row + part, value[:, part * width : (part + 1) * width], 1)
    for row in range(0, rows - 4, 2):
        total = jnp.zeros((CH, 2 * width), F32) + bias2
        for a in range(3):
            where = slice((row + a) * width, (row + a + 2) * width)
            total = total + dot3(w2_ref[a], high_ref[:, where], low_ref[:, where])
        value = jnp.tanh(total)
        second_ref[:, row * width : (row + 2) * width] = value
        high, low = halves(value)
        corr = dot3(head_ref[...], high, low)
        for part in range(2):
            corr_ref[:, 2 + row + part, :] = corr[: corr_ref.shape[0], part * width : (part + 1) * width]


def backward_kernel(
    mine_ref, other_ref, wind_ref, inside_ref, first_ref, second_ref, headt_ref, w2b_ref,
    par_ref, d1_ref,
    sum_ref, g_ref, d2_high, d2_low, own2_high, own2_low, act_high, act_low, own1_high, own1_low, wind_stack,
):
    cells = g_ref.shape[1]
    width = wind_ref.shape[2]
    cols = width - LANES
    ring = cells // width
    tile = ring - 4
    sum_ref[...] = mine_ref[...] + other_ref[...]
    wrap = sum_ref.shape[1]
    nine = sum_ref.shape[0]
    g_ref[...] = jnp.zeros(g_ref.shape, F32)
    for row in range(ring):
        g_ref[:nine, row * width : (row + 1) * width] = sum_ref[:, (row - 2) % wrap, :]
    own = lax.broadcasted_iota(jnp.int32, (1, width), 1) < cols
    inside = inside_ref[...]
    for ref in (own2_high, own2_low, own1_high, own1_low):
        ref[...] = jnp.zeros(ref.shape, BF16)
    wind_stack[...] = jnp.zeros(wind_stack.shape, F32)
    put_winds(wind_ref, wind_stack, 3, tile + 2)
    wind_stack[12:13, :] = jnp.ones((1, wind_stack.shape[1]), F32)
    bias2 = jnp.zeros((CH, width), F32)

    def put_own(high_ref, low_ref, x, value):
        high, low = halves(jnp.where(own, value, 0.0))
        for a in range(3):
            high_ref[a * CH : (a + 1) * CH, (x + a) * width : (x + a + 1) * width] = high
            low_ref[a * CH : (a + 1) * CH, (x + a) * width : (x + a + 1) * width] = low

    for row in range(0, ring, 2):
        where = slice(row * width, (row + 2) * width)
        high, low = halves(g_ref[:, where])
        hidden = dot3(headt_ref[...], high, low)
        second = second_ref[:, where]
        delta = hidden * (1.0 - second * second)
        for part in range(2):
            value = delta[:, part * width : (part + 1) * width]
            put_moved(d2_high, d2_low, row + part, value, -1)
            x = row + part - 2
            if 0 <= x < tile:
                put_own(own2_high, own2_low, x, value)
                bias2 = bias2 + jnp.where(own, value, 0.0)
    for row in range(tile + 2):
        put_moved(act_high, act_low, row, first_ref[:, (row + 2) * width : (row + 3) * width], 1)
    par_ref[...] = jnp.zeros(par_ref.shape, F32)
    par_ref[:, : 3 * CH] = dot3_nt(act_high[...], act_low[...], own2_high[...], own2_low[...])
    par_ref[:CH, 3 * CH + 16 : 3 * CH + 17] = jnp.sum(bias2, axis=1, keepdims=True)
    inside2 = jnp.concatenate([inside] * 2, axis=1)
    for row in range(0, tile + 2, 2):
        total = jnp.zeros((CH, 2 * width), F32)
        for a in range(3):
            start = row + 1 - STEPS[a]
            where = slice(start * width, (start + 2) * width)
            total = total + dot3(w2b_ref[a], d2_high[:, where], d2_low[:, where])
        first = first_ref[:, (row + 2) * width : (row + 4) * width]
        delta = total * (1.0 - first * first) * inside2
        d1_ref[:, row * width : (row + 2) * width] = delta
        for part in range(2):
            value = delta[:, part * width : (part + 1) * width]
            x = row + part - 1
            if 0 <= x < tile:
                put_own(own1_high, own1_low, x, value)
    high, low = halves(wind_stack[...])
    par_ref[:, 3 * CH : 3 * CH + 16] = dot3_nt(own1_high[...], own1_low[...], high, low)
    mid = slice(2 * width, (2 + tile) * width)
    own_rows = jnp.concatenate([own] * tile, axis=1)
    g_high, g_low = halves(jnp.where(own_rows, g_ref[:, mid], 0.0))
    s_high, s_low = halves(second_ref[:, mid])
    raw = dot3_nt(s_high, s_low, g_high, g_low)
    for level in range(LEVELS):
        rows = slice((level + 1) * CH, (level + 2) * CH)
        par_ref[rows, 3 * CH + 16 : 3 * CH + 25] = raw[:, 9 * level : 9 * level + 9]


def wind_kernel(mine_ref, other_ref, wind_ref, d1_ref, w1b_ref, wgrad_ref, d1_high, d1_low, net_ref):
    tile, cols = wgrad_ref.shape[1:]
    width = wind_ref.shape[2]
    for row in range(tile + 2):
        put_moved(d1_high, d1_low, row, d1_ref[:, row * width : (row + 1) * width], -1)
    for row in range(0, tile, 2):
        total = jnp.zeros((16, 2 * width), F32)
        for a in range(3):
            start = row + 1 - STEPS[a]
            where = slice(start * width, (start + 2) * width)
            total = total + dot3(w1b_ref[a], d1_high[:, where], d1_low[:, where])
        for part in range(2):
            net_ref[:, row + part, :] = total[:4, part * width : part * width + cols]
    for level in range(LEVELS):
        cx = COURANT * wind_ref[2 * level, HALO : HALO + tile, :cols]
        cy = COURANT * wind_ref[2 * level + 1, HALO : HALO + tile, :cols]
        px, py = lax_wendroff(cx), lax_wendroff(cy)
        dx, dy = (0.5 + cx, -2.0 * cx, cx - 0.5), (0.5 + cy, -2.0 * cy, cy - 0.5)
        gx_sum = jnp.zeros((tile, cols), F32)
        gy_sum = jnp.zeros((tile, cols), F32)
        for a in range(3):
            for b in range(3):
                k = 9 * level + 3 * a + b
                grad = mine_ref[k, :tile, :cols] + other_ref[k, :tile, :cols]
                gx_sum = gx_sum + grad * (dx[a] * py[b])
                gy_sum = gy_sum + grad * (px[a] * dy[b])
        wgrad_ref[2 * level] = COURANT * gx_sum + net_ref[2 * level]
        wgrad_ref[2 * level + 1] = COURANT * gy_sum + net_ref[2 * level + 1]


def final_kernel(mine_ref, other_ref, c1_ref, b1_ref, c2_ref, b2_ref, head_ref):
    total = mine_ref[...] + other_ref[...]
    across = jnp.concatenate([total, jnp.zeros((LANES - total.shape[0], LANES), F32)], axis=0).T
    size2, size1 = c2_ref.shape[1], c1_ref.shape[1]
    n_wind = size1 // 9
    split, rest = [], total
    turned, rest_t = [], across[: 3 * CH, : 3 * CH]
    for _ in range(3):
        high = rest.astype(BF16)
        split.append(high)
        rest = rest - high.astype(F32)
        high = rest_t.astype(BF16)
        turned.append(high)
        rest_t = rest_t - high.astype(F32)
    source = lax.broadcasted_iota(jnp.int32, (3 * CH, size2), 0)
    target = lax.broadcasted_iota(jnp.int32, (3 * CH, size2), 1)
    source1 = lax.broadcasted_iota(jnp.int32, (LANES, size1), 0) - 3 * CH
    target1 = lax.broadcasted_iota(jnp.int32, (LANES, size1), 1)
    out2 = jnp.zeros((CH, size2), F32)
    out1 = jnp.zeros((CH, size1), F32)
    for a in range(3):
        rows = slice(a * CH, (a + 1) * CH)
        pick2 = jnp.zeros((3 * CH, size2), F32)
        pick1 = jnp.zeros((LANES, size1), F32)
        for b in range(3):
            shift = 3 * a + b
            lies = (source >= b * CH) & (source < (b + 1) * CH)
            pick2 = jnp.where(lies & (target == 9 * (source - b * CH) + shift), 1.0, pick2)
            lies = (source1 >= b * n_wind) & (source1 < (b + 1) * n_wind)
            pick1 = jnp.where(lies & (target1 == 9 * (source1 - b * n_wind) + shift), 1.0, pick1)
        pick2, pick1 = pick2.astype(BF16), pick1.astype(BF16)
        for part in range(3):
            out2 = out2 + jnp.dot(turned[part][rows], pick2, preferred_element_type=F32)
            out1 = out1 + jnp.dot(split[part][rows], pick1, preferred_element_type=F32)
    c2_ref[...] = out2
    c1_ref[...] = out1
    b1_ref[...] = across[3 * CH + 3 * n_wind : 3 * CH + 3 * n_wind + 1, CH : 2 * CH]
    b2_ref[...] = across[3 * CH + 16 : 3 * CH + 17, :CH]
    for level in range(LEVELS):
        raw = across[3 * CH + 16 : 3 * CH + 25, (level + 1) * CH : (level + 2) * CH]
        mean = jnp.sum(raw, axis=0, keepdims=True) / 9.0
        head_ref[9 * level : 9 * level + 9, :] = CORRECTION * (raw - mean)


def lax_wendroff(courant):
    return (
        0.5 * courant + 0.5 * courant * courant,
        1.0 - courant * courant,
        0.5 * courant * courant - 0.5 * courant,
    )


def tracer_kernel(levels_ref, wind_ref, corr_ref, held_ref, side_ref, below_ref, above_ref, out_ref, coef_ref):
    count, tile, cols = out_ref.shape
    for level in range(LEVELS):
        px = lax_wendroff(COURANT * wind_ref[2 * level])
        py = lax_wendroff(COURANT * wind_ref[2 * level + 1])
        for a in range(3):
            for b in range(3):
                coef = corr_ref[9 * level + 3 * a + b] + px[a] * py[b]
                coef = turn(turn(coef, -STEPS[b], 1), HALO - STEPS[a], 0)
                coef_ref[level, 3 * a + b] = coef[:tile, :cols]

    channels = below_ref.shape[0] - 3
    groups = count // GROUP
    for group in range(groups):
        sides = sides_of(groups + group, side_ref, below_ref, above_ref, channels)

        def step(j, carry):
            t = group * GROUP + j
            level = levels_ref[t]
            field = load_field(count + t, held_ref[t], below_ref, above_ref, sides, j)
            total = jnp.zeros((tile, cols), F32)
            for b in range(3):
                moved = turn(field, -STEPS[b], 1)
                for a in range(3):
                    total = total + coef_ref[level, 3 * a + b] * turn(moved, -STEPS[a], 0)[:tile, :cols]
            out_ref[t] = total.astype(BF16)
            return carry

        lax.fori_loop(0, GROUP, step, 0, unroll=4)


def call(kernel, outs, scratch, smem, operands, flops):
    specs = [pl.BlockSpec(memory_space=pltpu.SMEM if i < smem else pltpu.VMEM) for i in range(len(operands))]
    whole = pl.BlockSpec(memory_space=pltpu.VMEM)
    return pl.pallas_call(
        kernel,
        out_shape=outs,
        in_specs=specs,
        out_specs=[whole] * len(outs) if isinstance(outs, (list, tuple)) else whole,
        scratch_shapes=scratch,
        compiler_params=pltpu.CompilerParams(vmem_limit_bytes=40 * 1024 * 1024),
        cost_estimate=pl.CostEstimate(flops=flops, bytes_accessed=2_000_000, transcendentals=0),
    )(*operands)


def stacked(weights):
    return jnp.concatenate(pieces(weights, 2), axis=-2).astype(BF16)


def pad_to(array, rows, cols):
    widths = [(0, 0)] * (array.ndim - 2) + [(0, rows - array.shape[-2]), (0, cols - array.shape[-1])]
    return jnp.pad(array, widths)


def ring_pairs(size, wrap):
    up = [(i, (i + 1) % size) for i in range(size if wrap else size - 1)]
    return up, [(j, i) for i, j in up]


def sum_rounds(value, axes):
    other = jnp.zeros_like(value)
    for axis in axes:
        size = lax.axis_size(axis)
        if size & (size - 1):
            value, other = lax.psum(value + other, axis), jnp.zeros_like(value)
            continue
        step = 1
        while step < size:
            value = value + other
            other = lax.ppermute(value, axis, [(i, i ^ step) for i in range(size)])
            step *= 2
    return value, other


def body(tracers, cotangent, winds, levels, conv1, bias1, conv2, bias2, head):
    count, tile, cols = tracers.shape
    n_wind = winds.shape[0]
    width = cols + LANES
    rows = tile + 2 * HALO
    gy, gy_size = lax.axis_index("gy"), lax.axis_size("gy")
    field = jnp.concatenate([tracers, cotangent] + [p.astype(BF16) for p in pieces(winds, 3)], axis=0)
    groups = -(-field.shape[0] // GROUP)
    packed = call(
        pack_kernel,
        jax.ShapeDtypeStruct((groups + 1, tile, LANES), BF16),
        [],
        0,
        (tracers, cotangent, winds),
        200_000,
    )
    up, down = ring_pairs(gy_size, False)
    lane = lax.broadcasted_iota(jnp.int32, (1, 1, LANES), 2) % (2 * HALO)
    if gy_size == 2:
        got = lax.ppermute(packed, "gy", up + down)
        side = jnp.where(jnp.where(gy == 0, lane >= HALO, lane < HALO), got, 0)
    else:
        right = lax.ppermute(packed, "gy", down)
        left = lax.ppermute(packed, "gy", up)
        side = jnp.where(lane >= HALO, right, left)
    side = side.astype(BF16)
    wide = jnp.concatenate([side[:3], side[3:]], axis=2)
    up, down = ring_pairs(lax.axis_size("gx"), True)
    above = lax.ppermute(jnp.concatenate([field[:, tile - HALO :], wide[:, tile - HALO :]], axis=0), "gx", up)
    below = lax.ppermute(jnp.concatenate([field[:, :HALO], wide[:, :HALO]], axis=0), "gx", down)
    place = lax.broadcasted_iota(jnp.int32, (1, width), 1)
    has_right, has_left = gy < gy_size - 1, gy > 0
    inside = jnp.where(place < cols, True, jnp.where(place < cols + LANES // 2, has_right, has_left)).astype(F32)

    split1 = conv1.reshape(CH, n_wind, 3, 3)
    split2 = conv2.reshape(CH, CH, 3, 3)
    w1 = stacked(pad_to(split1.transpose(2, 0, 3, 1).reshape(3, CH, 3 * n_wind), CH, 16))
    w2 = stacked(split2.transpose(2, 0, 3, 1).reshape(3, CH, 3 * CH))
    w2b = stacked(split2.transpose(2, 1, 3, 0).reshape(3, CH, 3 * CH))
    w1b = stacked(pad_to(split1.transpose(2, 1, 3, 0).reshape(3, n_wind, 3 * CH), 16, 3 * CH))
    by_level = head.reshape(LEVELS, 9, CH)
    centred = (CORRECTION * (by_level - jnp.mean(by_level, axis=1, keepdims=True))).reshape(9 * LEVELS, CH)
    head_w = stacked(pad_to(centred, CH, CH))
    head_t = stacked(pad_to(centred.T, CH, CH))

    vmem = pltpu.VMEM
    mine = call(
        grad_kernel,
        jax.ShapeDtypeStruct((9 * LEVELS, rows, width), F32),
        [vmem((3, count, rows, width), F32), vmem((count, rows, width), F32)],
        1,
        (levels, tracers, cotangent, side, below, above),
        2_000_000,
    )
    pairs = [(i, i ^ 1) for i in range(lax.axis_size("tracer"))]
    other = lax.ppermute(mine, "tracer", pairs)
    first, second, corr, wind_ext = call(
        forward_kernel,
        [
            jax.ShapeDtypeStruct((CH, (rows - 2) * width), F32),
            jax.ShapeDtypeStruct((CH, (rows - 4) * width), F32),
            jax.ShapeDtypeStruct((9 * LEVELS, rows, width), F32),
            jax.ShapeDtypeStruct((n_wind, rows, width), F32),
        ],
        [vmem((16, rows * width), F32)] + [vmem((3 * CH, (rows - 2) * width), BF16)] * 2,
        0,
        (winds, side, below, above, inside, w1, bias1[:, None], w2, bias2[:, None], head_w),
        2_000_000,
    )
    ring, own = (tile + 4) * width, (tile + 2) * width
    params, delta = call(
        backward_kernel,
        [jax.ShapeDtypeStruct((3 * CH, LANES), F32), jax.ShapeDtypeStruct((CH, own), F32)],
        [vmem((9 * LEVELS, rows, width), F32), vmem((CH, ring), F32)]
        + [vmem((3 * CH, ring), BF16)] * 2
        + [vmem((3 * CH, own), BF16)] * 6
        + [vmem((16, own), F32)],
        0,
        (mine, other, wind_ext, inside, first, second, head_t, w2b),
        2_000_000,
    )
    params = sum_rounds(params, ("gy", "gx"))
    tracer_grad = call(
        tracer_kernel,
        jax.ShapeDtypeStruct((count, tile, cols), BF16),
        [vmem((LEVELS, 9, tile, cols), F32)],
        1,
        (levels, wind_ext, corr, cotangent, side, below, above),
        2_000_000,
    )
    wind_grad = call(
        wind_kernel,
        jax.ShapeDtypeStruct((n_wind, tile, cols), F32),
        [vmem((3 * CH, own), BF16)] * 2 + [vmem((n_wind, tile, cols), F32)],
        0,
        (mine, other, wind_ext, delta, w1b),
        2_000_000,
    )
    conv1_grad, bias1_grad, conv2_grad, bias2_grad, head_grad = call(
        final_kernel,
        [
            jax.ShapeDtypeStruct(conv1.shape, F32),
            jax.ShapeDtypeStruct((1, CH), F32),
            jax.ShapeDtypeStruct(conv2.shape, F32),
            jax.ShapeDtypeStruct((1, CH), F32),
            jax.ShapeDtypeStruct(head.shape, F32),
        ],
        [],
        0,
        params,
        200_000,
    )
    return (tracer_grad, wind_grad, conv1_grad, bias1_grad[0], conv2_grad, bias2_grad[0], head_grad)


def solution(mesh):
    return jax.shard_map(
        body,
        mesh=mesh,
        in_specs=(
            P(("member", "tracer"), "gx", "gy"),
            P(("member", "tracer"), "gx", "gy"),
            P("member", "gx", "gy"),
            P(("member", "tracer")),
            P(),
            P(),
            P(),
            P(),
            P(),
        ),
        out_specs=(
            P(("member", "tracer"), "gx", "gy"),
            P("member", "gx", "gy"),
            P("member", None),
            P("member"),
            P("member", None),
            P("member"),
            P("member", None),
        ),
        check_vma=False,
    )
```

```python
import functools

import jax
import jax.numpy as jnp
from jax import lax
from jax.experimental import pallas as pl
from jax.experimental.pallas import tpu as pltpu
from jax.sharding import PartitionSpec as P

LEVELS = 2
CH = 32
COURANT = 0.5
CORRECTION = 0.2
STEPS = (-1, 0, 1)
HALO = 4
LANES = 128
GROUP = LANES // (2 * HALO)
F32 = jnp.float32
BF16 = jnp.bfloat16
NT = (((1,), (1,)), ((), ()))


def pieces(array, count):
    parts = []
    for _ in range(count):
        part = lax.reduce_precision(array, 8, 7)
        parts.append(part)
        array = array - part
    return parts


def halves(value):
    high = value.astype(BF16)
    return high, (value - high.astype(F32)).astype(BF16)


def dot3(weights, high, low):
    rows = weights.shape[0] // 2
    both = jnp.dot(weights, high, preferred_element_type=F32)
    rest = jnp.dot(weights[:rows], low, preferred_element_type=F32)
    return both[:rows] + both[rows:] + rest


def dot3_nt(a_high, a_low, b_high, b_low):
    out = lax.dot_general(a_high, b_high, NT, preferred_element_type=F32)
    out = out + lax.dot_general(a_high, b_low, NT, preferred_element_type=F32)
    return out + lax.dot_general(a_low, b_high, NT, preferred_element_type=F32)


def turn(value, step, axis):
    shift = (-step) % value.shape[axis]
    return pltpu.roll(value, shift, axis) if shift else value


def side_mask():
    lane = lax.broadcasted_iota(jnp.int32, (1, LANES), 1)
    return (lane < HALO) | (lane >= LANES - HALO)


def rows_of(below, above):
    return jnp.concatenate([below.astype(F32), above.astype(F32)], axis=0)


def sides_of(group, side_ref, below_ref, above_ref, channels):
    half = side_ref.shape[0] // 2
    index = channels + group % half
    where = slice(group // half * LANES, (group // half + 1) * LANES)
    return side_ref[group].astype(F32), rows_of(below_ref[index, :, where], above_ref[index, :, where])


def placed(side, j):
    return jnp.where(side_mask(), pltpu.roll(side, LANES - HALO - 2 * HALO * j, 1), 0.0)


def load_field(index, main, below_ref, above_ref, sides, j):
    top = jnp.concatenate([main.astype(F32), placed(sides[0], j)], axis=1)
    strip = jnp.concatenate([rows_of(below_ref[index], above_ref[index]), placed(sides[1], j)], axis=1)
    return jnp.concatenate([top, strip], axis=0)


def run_copies(sources, targets, sems):
    copies = [pltpu.make_async_copy(a, b, sems.at[i]) for i, (a, b) in enumerate(zip(sources, targets))]
    for copy in copies:
        copy.start()
    for copy in copies:
        copy.wait()


def pack_kernel(tracer_hbm, cot_hbm, wind_hbm, out_ref, tracer_ref, cot_ref, wind_ref, sems):
    cols = tracer_hbm.shape[2]
    hbm = (tracer_hbm, cot_hbm, wind_hbm)
    refs = (tracer_ref, cot_ref, wind_ref)
    run_copies(
        [ref.at[:, :, where] for ref in hbm for where in (slice(0, LANES), slice(cols - LANES, cols))],
        [ref.at[part] for ref in refs for part in range(2)],
        sems,
    )
    lane = lax.broadcasted_iota(jnp.int32, (1, LANES), 1)
    mask = side_mask()

    def lifted(head, tail, j):
        both = jnp.where(lane < HALO, head, tail)
        return pltpu.roll(jnp.where(mask, both, 0.0), HALO + 2 * HALO * j, 1)

    groups = tracer_ref.shape[1] // GROUP
    for group, ref in ((0, tracer_ref), (groups + 1, cot_ref)):
        for start in range(0, ref.shape[1], GROUP):
            total = jnp.zeros(out_ref.shape[1:], F32)
            for j in range(GROUP):
                total = total + lifted(ref[0, start + j].astype(F32), ref[1, start + j].astype(F32), j)
            out_ref[group] = total.astype(BF16)
            group += 1
    total = jnp.zeros(out_ref.shape[1:], F32)
    count = wind_ref.shape[1]
    for i in range(count):
        head, tail = wind_ref[0, i], wind_ref[1, i]
        for part in range(3):
            high_head, high_tail = head.astype(BF16).astype(F32), tail.astype(BF16).astype(F32)
            total = total + lifted(high_head, high_tail, part * count + i)
            head, tail = head - high_head, tail - high_tail
    out_ref[groups] = total.astype(BF16)
    out_ref[2 * groups + 1] = jnp.zeros(out_ref.shape[1:], BF16)


def picker(shape, source_axis, wanted):
    source = lax.broadcasted_iota(jnp.int32, shape, source_axis)
    target = lax.broadcasted_iota(jnp.int32, shape, 1 - source_axis)
    return jnp.where(source == wanted(target), 1.0, 0.0).astype(BF16)


def prep_kernel(
    c1_hbm, b1_hbm, c2_hbm, b2_hbm, head_hbm,
    w1_ref, w2_ref, w2b_ref, w1b_ref, hw_ref, ht_ref, b1_ref, b2_ref,
    c1, b1, c2, b2, head, wide_ref, slim_ref, tall_ref, sems,
):
    run_copies((c1_hbm, b1_hbm, c2_hbm, b2_hbm, head_hbm), (c1, b1, c2, b2, head), sems)
    n_wind = c1.shape[1] // 9

    def wanted2(target):
        return 9 * (target & (CH - 1)) + (target >> 5)

    def wanted1(target):
        a, r = target >> 4, target & 15
        b = (r >= n_wind).astype(jnp.int32) + (r >= 2 * n_wind).astype(jnp.int32)
        return jnp.where(r < 3 * n_wind, 9 * (r - n_wind * b) + 3 * a + b, -1)

    both2 = jnp.concatenate(halves(c2[...]), axis=0)
    size = both2.shape[1]
    w2_ref[...] = jnp.dot(both2, picker((size, size), 0, wanted2), preferred_element_type=F32).astype(BF16)
    turned = lax.dot_general(picker((size, size), 1, wanted2), both2, NT, preferred_element_type=F32)
    both1 = jnp.concatenate(halves(c1[...]), axis=0)
    size = both1.shape[1]
    w1_ref[...] = jnp.dot(both1, picker((size, 48), 0, wanted1), preferred_element_type=F32).astype(BF16)
    turned1 = lax.dot_general(picker((48, size), 1, wanted1), both1, NT, preferred_element_type=F32)
    slim_ref[...] = jnp.zeros(slim_ref.shape, F32)
    for q in range(9):
        where = slice(q * CH, (q + 1) * CH)
        start = q // 3 * 16 + q % 3 * n_wind
        for part in range(2):
            lanes = slice(part * CH, (part + 1) * CH)
            wide_ref[lanes, where] = turned[where, lanes]
            slim_ref[16 * part : 16 * part + n_wind, where] = turned1[start : start + n_wind, lanes]
    w2b_ref[...] = wide_ref[...].astype(BF16)
    w1b_ref[...] = slim_ref[...].astype(BF16)
    tall_ref[...] = jnp.zeros(tall_ref.shape, F32)
    for level in range(LEVELS):
        rows = slice(9 * level, 9 * level + 9)
        part = head[rows, :]
        part = CORRECTION * (part - jnp.sum(part, axis=0, keepdims=True) / 9.0)
        high = part.astype(BF16).astype(F32)
        tall_ref[rows, :] = high
        tall_ref[CH + 9 * level : CH + 9 * level + 9, :] = part - high
    tall = tall_ref[...].astype(BF16)
    hw_ref[...] = tall
    unit = picker((CH, CH), 0, lambda target: target)
    across = lax.dot_general(unit, tall, NT, preferred_element_type=F32)
    ht_ref[:CH, :] = across[:, :CH].astype(BF16)
    ht_ref[CH:, :] = across[:, CH:].astype(BF16)
    for source, target in ((b1, b1_ref), (b2, b2_ref)):
        target[...] = jnp.sum(unit.astype(F32) * source[...], axis=1, keepdims=True)


def grad_kernel(levels_ref, field_ref, side_ref, below_ref, above_ref, out_ref, moved_ref, held_ref):
    count = levels_ref.shape[0]
    slots, rows, width = moved_ref.shape[1:]
    channels = below_ref.shape[0] - 3
    groups = count // GROUP
    lower = jnp.int32(0)
    for group in range(groups):
        near = sides_of(group, side_ref, below_ref, above_ref, channels)
        far = sides_of(groups + 1 + group, side_ref, below_ref, above_ref, channels)

        def fill(j, lower):
            t = group * GROUP + j
            low = levels_ref[t] == 0
            slot = jnp.where(low, lower, slots - 1 - t + lower)
            field = load_field(t, field_ref[t], below_ref, above_ref, near, j)
            cot = load_field(count + t, field_ref[count + t], below_ref, above_ref, far, j)
            for step in range(3):
                moved_ref[step, slot] = turn(field, STEPS[step], 1)
                held_ref[step, slot] = turn(cot, -STEPS[step], 0)
            return jnp.where(low, lower + 1, lower)

        lower = lax.fori_loop(0, GROUP, fill, lower, unroll=4)
    for gap in (0, 1, 2, 5, 6, 7):
        for step in range(3):
            moved_ref[step, lower + gap] = jnp.zeros((rows, width), F32)
            held_ref[step, lower + gap] = jnp.zeros((rows, width), F32)
    for level in range(LEVELS):
        trips = lax.shift_right_logical((lower if level == 0 else count - lower) + 3, 2)
        for start in range(0, width, LANES):
            lanes = slice(start, start + LANES)

            def step(trip, sums):
                for part in range(4):
                    slot = 4 * trip + part
                    slot = slot if level == 0 else slots - 1 - slot
                    near = [moved_ref[b, slot, :, lanes] for b in range(3)]
                    far = [held_ref[a, slot, :, lanes] for a in range(3)]
                    sums = tuple(sums[k] + far[k // 3] * near[k % 3] for k in range(9))
                return sums

            sums = lax.fori_loop(0, trips, step, (jnp.zeros((rows, LANES), F32),) * 9)
            for k in range(9):
                out_ref[9 * level + k, :, lanes] = turn(sums[k], STEPS[k // 3], 0)


def put_moved(high_ref, low_ref, row, value, sign):
    width = value.shape[1]
    for ref, part in zip((high_ref, low_ref), halves(value)):
        for b in range(3):
            ref[b * CH : (b + 1) * CH, row * width : (row + 1) * width] = turn(part, sign * STEPS[b], 1)


def convolved(weights, high_ref, low_ref, starts, width):
    def rows(ref):
        return jnp.concatenate([ref[:, start * width : (start + 2) * width] for start in starts], axis=0)

    return dot3(weights, rows(high_ref), rows(low_ref))


def put_winds(wind_ref, stack_ref, first_row, rows):
    width = wind_ref.shape[2]
    count = wind_ref.shape[0]
    for row in range(rows):
        value = wind_ref[:, first_row + row, :]
        for b in range(3):
            stack_ref[b * count : (b + 1) * count, row * width : (row + 1) * width] = turn(value, STEPS[b], 1)


def forward_kernel(
    own_ref, side_ref, below_ref, above_ref, inside_ref, w1_ref, b1_ref, w2_ref, b2_ref, head_ref,
    first_ref, second_ref, corr_ref, wind_ref,
    stack_ref, wind_high, wind_low, high_ref, low_ref,
):
    count, rows, width = wind_ref.shape
    tile, cols = own_ref.shape[1:]
    channels = below_ref.shape[0] - 3
    side, side_rows = sides_of((channels - 3 * count) // (2 * GROUP), side_ref, below_ref, above_ref, channels)
    for i in range(count):
        wind_ref[i, HALO : HALO + tile, :cols] = own_ref[i]
        wide = [jnp.zeros((tile, LANES), F32), jnp.zeros((tile, LANES), F32)]
        strip = jnp.zeros((2 * HALO, cols), F32)
        for part in range(3):
            j = part * count + i
            wide[0] = wide[0] + placed(side, j)
            wide[1] = wide[1] + placed(side_rows, j)
            index = channels - 3 * count + j
            strip = strip + rows_of(below_ref[index], above_ref[index])
        wind_ref[i, HALO : HALO + tile, cols:] = wide[0]
        for value, where in ((strip, slice(0, cols)), (wide[1], slice(cols, width))):
            wind_ref[i, HALO + tile :, where] = value[:HALO]
            wind_ref[i, :HALO, where] = value[HALO:]
    stack_ref[...] = jnp.zeros(stack_ref.shape, F32)
    put_winds(wind_ref, stack_ref, 0, rows)
    wind_high[...], wind_low[...] = halves(stack_ref[...])
    bias1, bias2 = b1_ref[...], b2_ref[...]
    inside = jnp.concatenate([inside_ref[...]] * 2, axis=1)
    for row in range(0, rows - 2, 2):
        starts = (row, row + 1, row + 2)
        value = jnp.tanh(convolved(w1_ref[...], wind_high, wind_low, starts, width) + bias1) * inside
        first_ref[:, row * width : (row + 2) * width] = value
        for part in range(2):
            put_moved(high_ref, low_ref, row + part, value[:, part * width : (part + 1) * width], 1)
    for row in range(0, rows - 4, 2):
        starts = (row, row + 1, row + 2)
        value = jnp.tanh(convolved(w2_ref[...], high_ref, low_ref, starts, width) + bias2)
        second_ref[:, row * width : (row + 2) * width] = value
        high, low = halves(value)
        corr = dot3(head_ref[...], high, low)
        for part in range(2):
            corr_ref[:, 2 + row + part, :] = corr[: corr_ref.shape[0], part * width : (part + 1) * width]


def backward_kernel(
    mine_ref, other_ref, wind_ref, inside_ref, first_ref, second_ref, headt_ref, w2b_ref,
    par_ref, d1_ref,
    sum_ref, g_ref, d2_high, d2_low, own2_high, own2_low, act_high, act_low, own1_high, own1_low, wind_stack,
):
    cells = g_ref.shape[1]
    width = wind_ref.shape[2]
    cols = width - LANES
    ring = cells // width
    tile = ring - 4
    sum_ref[...] = mine_ref[...] + other_ref[...]
    wrap = sum_ref.shape[1]
    nine = sum_ref.shape[0]
    g_ref[...] = jnp.zeros(g_ref.shape, F32)
    for row in range(ring):
        g_ref[:nine, row * width : (row + 1) * width] = sum_ref[:, (row - 2) % wrap, :]
    own = lax.broadcasted_iota(jnp.int32, (1, width), 1) < cols
    inside = inside_ref[...]
    for ref in (own2_high, own2_low, own1_high, own1_low):
        ref[...] = jnp.zeros(ref.shape, BF16)
    wind_stack[...] = jnp.zeros(wind_stack.shape, F32)
    put_winds(wind_ref, wind_stack, 3, tile + 2)
    wind_stack[12:13, :] = jnp.ones((1, wind_stack.shape[1]), F32)
    bias2 = jnp.zeros((CH, width), F32)

    def put_own(high_ref, low_ref, x, value):
        high, low = halves(jnp.where(own, value, 0.0))
        for a in range(3):
            high_ref[a * CH : (a + 1) * CH, (x + a) * width : (x + a + 1) * width] = high
            low_ref[a * CH : (a + 1) * CH, (x + a) * width : (x + a + 1) * width] = low

    for row in range(0, ring, 2):
        where = slice(row * width, (row + 2) * width)
        high, low = halves(g_ref[:, where])
        hidden = dot3(headt_ref[...], high, low)
        second = second_ref[:, where]
        delta = hidden * (1.0 - second * second)
        for part in range(2):
            value = delta[:, part * width : (part + 1) * width]
            put_moved(d2_high, d2_low, row + part, value, -1)
            x = row + part - 2
            if 0 <= x < tile:
                put_own(own2_high, own2_low, x, value)
                bias2 = bias2 + jnp.where(own, value, 0.0)
    for row in range(tile + 2):
        put_moved(act_high, act_low, row, first_ref[:, (row + 2) * width : (row + 3) * width], 1)
    par_ref[...] = jnp.zeros(par_ref.shape, F32)
    par_ref[:, : 3 * CH] = dot3_nt(act_high[...], act_low[...], own2_high[...], own2_low[...])
    par_ref[:CH, 3 * CH + 16 : 3 * CH + 17] = jnp.sum(bias2, axis=1, keepdims=True)
    inside2 = jnp.concatenate([inside] * 2, axis=1)
    for row in range(0, tile + 2, 2):
        total = convolved(w2b_ref[...], d2_high, d2_low, (row + 2, row + 1, row), width)
        first = first_ref[:, (row + 2) * width : (row + 4) * width]
        delta = total * (1.0 - first * first) * inside2
        d1_ref[:, row * width : (row + 2) * width] = delta
        for part in range(2):
            value = delta[:, part * width : (part + 1) * width]
            x = row + part - 1
            if 0 <= x < tile:
                put_own(own1_high, own1_low, x, value)
    high, low = halves(wind_stack[...])
    par_ref[:, 3 * CH : 3 * CH + 16] = dot3_nt(own1_high[...], own1_low[...], high, low)
    mid = slice(2 * width, (2 + tile) * width)
    own_rows = jnp.concatenate([own] * tile, axis=1)
    g_high, g_low = halves(jnp.where(own_rows, g_ref[:, mid], 0.0))
    s_high, s_low = halves(second_ref[:, mid])
    raw = dot3_nt(s_high, s_low, g_high, g_low)
    for level in range(LEVELS):
        rows = slice((level + 1) * CH, (level + 2) * CH)
        par_ref[rows, 3 * CH + 16 : 3 * CH + 25] = raw[:, 9 * level : 9 * level + 9]


def wind_kernel(mine_ref, other_ref, wind_ref, d1_ref, w1b_ref, wgrad_ref, d1_high, d1_low, net_ref):
    tile, cols = wgrad_ref.shape[1:]
    width = wind_ref.shape[2]
    for row in range(tile + 2):
        put_moved(d1_high, d1_low, row, d1_ref[:, row * width : (row + 1) * width], -1)
    for row in range(0, tile, 2):
        total = convolved(w1b_ref[...], d1_high, d1_low, (row + 2, row + 1, row), width)
        for part in range(2):
            net_ref[:, row + part, :] = total[:4, part * width : part * width + cols]
    for level in range(LEVELS):
        cx = COURANT * wind_ref[2 * level, HALO : HALO + tile, :cols]
        cy = COURANT * wind_ref[2 * level + 1, HALO : HALO + tile, :cols]
        px, py = lax_wendroff(cx), lax_wendroff(cy)
        dx, dy = (0.5 + cx, -2.0 * cx, cx - 0.5), (0.5 + cy, -2.0 * cy, cy - 0.5)
        gx_sum = jnp.zeros((tile, cols), F32)
        gy_sum = jnp.zeros((tile, cols), F32)
        for a in range(3):
            for b in range(3):
                k = 9 * level + 3 * a + b
                grad = mine_ref[k, :tile, :cols] + other_ref[k, :tile, :cols]
                gx_sum = gx_sum + grad * (dx[a] * py[b])
                gy_sum = gy_sum + grad * (px[a] * dy[b])
        wgrad_ref[2 * level] = COURANT * gx_sum + net_ref[2 * level]
        wgrad_ref[2 * level + 1] = COURANT * gy_sum + net_ref[2 * level + 1]


def final_kernel(mine_ref, other_ref, c1_ref, b1_ref, c2_ref, b2_ref, head_ref):
    total = mine_ref[...] + other_ref[...]
    across = jnp.concatenate([total, jnp.zeros((LANES - total.shape[0], LANES), F32)], axis=0).T
    size2, size1 = c2_ref.shape[1], c1_ref.shape[1]
    n_wind = size1 // 9
    split, rest = [], total
    turned, rest_t = [], across[: 3 * CH, : 3 * CH]
    for _ in range(3):
        high = rest.astype(BF16)
        split.append(high)
        rest = rest - high.astype(F32)
        high = rest_t.astype(BF16)
        turned.append(high)
        rest_t = rest_t - high.astype(F32)
    source = lax.broadcasted_iota(jnp.int32, (3 * CH, size2), 0)
    target = lax.broadcasted_iota(jnp.int32, (3 * CH, size2), 1)
    source1 = lax.broadcasted_iota(jnp.int32, (LANES, size1), 0) - 3 * CH
    target1 = lax.broadcasted_iota(jnp.int32, (LANES, size1), 1)
    out2 = jnp.zeros((CH, size2), F32)
    out1 = jnp.zeros((CH, size1), F32)
    for a in range(3):
        rows = slice(a * CH, (a + 1) * CH)
        pick2 = jnp.zeros((3 * CH, size2), F32)
        pick1 = jnp.zeros((LANES, size1), F32)
        for b in range(3):
            shift = 3 * a + b
            lies = (source >= b * CH) & (source < (b + 1) * CH)
            pick2 = jnp.where(lies & (target == 9 * (source - b * CH) + shift), 1.0, pick2)
            lies = (source1 >= b * n_wind) & (source1 < (b + 1) * n_wind)
            pick1 = jnp.where(lies & (target1 == 9 * (source1 - b * n_wind) + shift), 1.0, pick1)
        pick2, pick1 = pick2.astype(BF16), pick1.astype(BF16)
        for part in range(3):
            out2 = out2 + jnp.dot(turned[part][rows], pick2, preferred_element_type=F32)
            out1 = out1 + jnp.dot(split[part][rows], pick1, preferred_element_type=F32)
    c2_ref[...] = out2
    c1_ref[...] = out1
    b1_ref[...] = across[3 * CH + 3 * n_wind : 3 * CH + 3 * n_wind + 1, CH : 2 * CH]
    b2_ref[...] = across[3 * CH + 16 : 3 * CH + 17, :CH]
    for level in range(LEVELS):
        raw = across[3 * CH + 16 : 3 * CH + 25, (level + 1) * CH : (level + 2) * CH]
        mean = jnp.sum(raw, axis=0, keepdims=True) / 9.0
        head_ref[9 * level : 9 * level + 9, :] = CORRECTION * (raw - mean)


def lax_wendroff(courant):
    return (
        0.5 * courant + 0.5 * courant * courant,
        1.0 - courant * courant,
        0.5 * courant * courant - 0.5 * courant,
    )


def tracer_kernel(levels_ref, wind_ref, corr_ref, field_ref, side_ref, below_ref, above_ref, out_ref, coef_ref):
    count, tile, cols = out_ref.shape
    for level in range(LEVELS):
        px = lax_wendroff(COURANT * wind_ref[2 * level])
        py = lax_wendroff(COURANT * wind_ref[2 * level + 1])
        for a in range(3):
            for b in range(3):
                coef = corr_ref[9 * level + 3 * a + b] + px[a] * py[b]
                coef = turn(turn(coef, -STEPS[b], 1), HALO - STEPS[a], 0)
                coef_ref[level, 3 * a + b] = coef[:tile, :cols]

    channels = below_ref.shape[0] - 3
    groups = count // GROUP
    for group in range(groups):
        sides = sides_of(groups + 1 + group, side_ref, below_ref, above_ref, channels)

        def step(j, carry):
            t = group * GROUP + j
            level = levels_ref[t]
            field = load_field(count + t, field_ref[count + t], below_ref, above_ref, sides, j)
            total = jnp.zeros((tile, cols), F32)
            for b in range(3):
                moved = turn(field, -STEPS[b], 1)
                for a in range(3):
                    total = total + coef_ref[level, 3 * a + b] * turn(moved, -STEPS[a], 0)[:tile, :cols]
            out_ref[t] = total.astype(BF16)
            return carry

        lax.fori_loop(0, GROUP, step, 0, unroll=4)


def call(kernel, outs, scratch, operands, spaces=None, flops=2_000_000, vmem=40):
    specs = [pl.BlockSpec(memory_space=(spaces or {}).get(i, pltpu.VMEM)) for i in range(len(operands))]
    whole = pl.BlockSpec(memory_space=pltpu.VMEM)
    return pl.pallas_call(
        kernel,
        out_shape=outs,
        in_specs=specs,
        out_specs=[whole] * len(outs) if isinstance(outs, (list, tuple)) else whole,
        scratch_shapes=scratch,
        compiler_params=pltpu.CompilerParams(vmem_limit_bytes=vmem * 1024 * 1024),
        cost_estimate=pl.CostEstimate(flops=flops, bytes_accessed=2_000_000, transcendentals=0),
    )(*operands)


def ring_pairs(size, wrap):
    up = [(i, (i + 1) % size) for i in range(size if wrap else size - 1)]
    return up, [(j, i) for i, j in up]


def sum_rounds(value, axes, beside):
    other, done = jnp.zeros_like(value), []
    for axis in axes:
        size = lax.axis_size(axis)
        if size & (size - 1):
            value, other = lax.psum(value + other, axis), jnp.zeros_like(value)
            continue
        step = 1
        while step < size:
            value = value + other
            if step > 1 or axis != axes[0]:
                if len(done) < len(beside):
                    value, made = lax.optimization_barrier((value, beside[len(done)]))
                    done.append(made)
            other = lax.ppermute(value, axis, [(i, i ^ step) for i in range(size)])
            step *= 2
    return value, other, tuple(done) + tuple(beside[len(done) :])


def body(tracers, cotangent, winds, levels, conv1, bias1, conv2, bias2, head):
    count, tile, cols = tracers.shape
    n_wind = winds.shape[0]
    width = cols + LANES
    rows = tile + 2 * HALO
    vmem, spec = pltpu.VMEM, jax.ShapeDtypeStruct
    gy, gy_size = lax.axis_index("gy"), lax.axis_size("gy")
    packed = call(
        pack_kernel,
        spec((2 * (count // GROUP) + 2, tile, LANES), BF16),
        [vmem((2, count, tile, LANES), BF16)] * 2
        + [vmem((2, n_wind, tile, LANES), F32), pltpu.SemaphoreType.DMA((6,))],
        (tracers, cotangent, winds),
        {i: pltpu.HBM for i in range(3)},
        200_000,
        63,
    )
    w1, w2, w2b, w1b, head_w, head_t, bias1_col, bias2_col = call(
        prep_kernel,
        [
            spec((2 * CH, 48), BF16),
            spec((2 * CH, 9 * CH), BF16),
            spec((2 * CH, 9 * CH), BF16),
            spec((32, 9 * CH), BF16),
            spec((2 * CH, CH), BF16),
            spec((2 * CH, CH), BF16),
            spec((CH, 1), F32),
            spec((CH, 1), F32),
        ],
        [
            vmem(conv1.shape, F32),
            vmem((1, CH), F32),
            vmem(conv2.shape, F32),
            vmem((1, CH), F32),
            vmem(head.shape, F32),
            vmem((2 * CH, 9 * CH), F32),
            vmem((32, 9 * CH), F32),
            vmem((2 * CH, CH), F32),
            pltpu.SemaphoreType.DMA((5,)),
        ],
        (conv1, bias1[None], conv2, bias2[None], head),
        {i: pltpu.HBM for i in range(5)},
    )
    field = jnp.concatenate([tracers, cotangent] + [p.astype(BF16) for p in pieces(winds, 3)], axis=0)
    up, down = ring_pairs(gy_size, False)
    lane = lax.broadcasted_iota(jnp.int32, (1, 1, LANES), 2) % (2 * HALO)
    if gy_size == 2:
        got = lax.ppermute(packed, "gy", up + down)
        side = jnp.where(jnp.where(gy == 0, lane >= HALO, lane < HALO), got, 0)
    else:
        right = lax.ppermute(packed, "gy", down)
        left = lax.ppermute(packed, "gy", up)
        side = jnp.where(lane >= HALO, right, left)
    side = side.astype(BF16)
    half = side.shape[0] // 2
    wide = jnp.concatenate([side[:half], side[half:]], axis=2)
    up, down = ring_pairs(lax.axis_size("gx"), True)
    above = lax.ppermute(jnp.concatenate([field[:, tile - HALO :], wide[:, tile - HALO :]], axis=0), "gx", up)
    below = lax.ppermute(jnp.concatenate([field[:, :HALO], wide[:, :HALO]], axis=0), "gx", down)
    place = lax.broadcasted_iota(jnp.int32, (1, width), 1)
    has_right, has_left = gy < gy_size - 1, gy > 0
    inside = jnp.where(place < cols, True, jnp.where(place < cols + LANES // 2, has_right, has_left)).astype(F32)

    above, below, w1, w2 = lax.optimization_barrier((above, below, w1, w2))
    mine = call(
        grad_kernel,
        spec((9 * LEVELS, rows, width), F32),
        [vmem((3, count + 8, rows, width), F32)] * 2,
        (levels, field, side, below, above),
        {0: pltpu.SMEM},
    )
    other = lax.ppermute(mine, "tracer", [(i, i ^ 1) for i in range(lax.axis_size("tracer"))])
    first, second, corr, wind_ext = call(
        forward_kernel,
        [
            spec((CH, (rows - 2) * width), F32),
            spec((CH, (rows - 4) * width), F32),
            spec((9 * LEVELS, rows, width), F32),
            spec((n_wind, rows, width), F32),
        ],
        [vmem((16, rows * width), F32)]
        + [vmem((16, rows * width), BF16)] * 2
        + [vmem((3 * CH, (rows - 2) * width), BF16)] * 2,
        (winds, side, below, above, inside, w1, bias1_col, w2, bias2_col, head_w),
    )
    ring, own = (tile + 4) * width, (tile + 2) * width
    params, delta = call(
        backward_kernel,
        [spec((3 * CH, LANES), F32), spec((CH, own), F32)],
        [vmem((9 * LEVELS, rows, width), F32), vmem((CH, ring), F32)]
        + [vmem((3 * CH, ring), BF16)] * 2
        + [vmem((3 * CH, own), BF16)] * 6
        + [vmem((16, own), F32)],
        (mine, other, wind_ext, inside, first, second, head_t, w2b),
    )
    tracer_grad = call(
        tracer_kernel,
        spec((count, tile, cols), BF16),
        [vmem((LEVELS, 9, tile, cols), F32)],
        (levels, wind_ext, corr, field, side, below, above),
        {0: pltpu.SMEM},
    )
    wind_grad = call(
        wind_kernel,
        spec((n_wind, tile, cols), F32),
        [vmem((3 * CH, own), BF16)] * 2 + [vmem((n_wind, tile, cols), F32)],
        (mine, other, wind_ext, delta, w1b),
    )
    mine, other, (tracer_grad, wind_grad) = sum_rounds(params, ("gy", "gx"), (tracer_grad, wind_grad))
    conv1_grad, bias1_grad, conv2_grad, bias2_grad, head_grad = call(
        final_kernel,
        [spec(conv1.shape, F32), spec((1, CH), F32), spec(conv2.shape, F32), spec((1, CH), F32), spec(head.shape, F32)],
        [],
        (mine, other),
        flops=200_000,
    )
    return (tracer_grad, wind_grad, conv1_grad, bias1_grad[0], conv2_grad, bias2_grad[0], head_grad)


def solution(mesh):
    return jax.shard_map(
        body,
        mesh=mesh,
        in_specs=(
            P(("member", "tracer"), "gx", "gy"),
            P(("member", "tracer"), "gx", "gy"),
            P("member", "gx", "gy"),
            P(("member", "tracer")),
            P(),
            P(),
            P(),
            P(),
            P(),
        ),
        out_specs=(
            P(("member", "tracer"), "gx", "gy"),
            P("member", "gx", "gy"),
            P("member", None),
            P("member"),
            P("member", None),
            P("member"),
            P("member", None),
        ),
        check_vma=False,
    )
```

```python
import functools

import jax
import jax.numpy as jnp
from jax import lax
from jax.experimental import pallas as pl
from jax.experimental.pallas import tpu as pltpu
from jax.sharding import PartitionSpec as P

LEVELS = 2
CH = 32
COURANT = 0.5
CORRECTION = 0.2
STEPS = (-1, 0, 1)
HALO = 4
LANES = 128
GROUP = LANES // (2 * HALO)
F32 = jnp.float32
BF16 = jnp.bfloat16
NT = (((1,), (1,)), ((), ()))


def halves(value):
    high = value.astype(BF16)
    return high, (value - high.astype(F32)).astype(BF16)


def dot3(weights, high, low):
    rows = weights.shape[0] // 2
    both = jnp.dot(weights, high, preferred_element_type=F32)
    rest = jnp.dot(weights[:rows], low, preferred_element_type=F32)
    return both[:rows] + both[rows:] + rest


def dot3_nt(a_high, a_low, b_high, b_low):
    out = lax.dot_general(a_high, b_high, NT, preferred_element_type=F32)
    out = out + lax.dot_general(a_high, b_low, NT, preferred_element_type=F32)
    return out + lax.dot_general(a_low, b_high, NT, preferred_element_type=F32)


def turn(value, step, axis):
    shift = (-step) % value.shape[axis]
    return pltpu.roll(value, shift, axis) if shift else value


def side_mask():
    lane = lax.broadcasted_iota(jnp.int32, (1, LANES), 1)
    return (lane < HALO) | (lane >= LANES - HALO)


def rows_of(below, above):
    return jnp.concatenate([below.astype(F32), above.astype(F32)], axis=0)


def sides_of(group, side_ref, below_ref, above_ref, channels):
    half = side_ref.shape[0] // 2
    index = channels + group % half
    where = slice(group // half * LANES, (group // half + 1) * LANES)
    return side_ref[group].astype(F32), rows_of(below_ref[index, :, where], above_ref[index, :, where])


def placed(side, j):
    return jnp.where(side_mask(), pltpu.roll(side, LANES - HALO - 2 * HALO * j, 1), 0.0)


def joined(main, side, strip, strip_side, j):
    top = jnp.concatenate([main.astype(F32), placed(side, j)], axis=1)
    return jnp.concatenate([top, jnp.concatenate([strip, placed(strip_side, j)], axis=1)], axis=0)


def cot_strip(strip, spare, part):
    slot = lax.broadcasted_iota(jnp.int32, strip.shape, 0)
    value = jnp.where(slot == 0, turn(strip, 3, 0), jnp.where(slot == 6, turn(strip, -2, 0), 0.0))
    value = jnp.where(slot == 1, spare[part : part + 1], value)
    return jnp.where(slot == 7, spare[HALO + part : HALO + part + 1], value)


def run_copies(sources, targets, sems):
    copies = [pltpu.make_async_copy(a, b, sems.at[i]) for i, (a, b) in enumerate(zip(sources, targets))]
    for copy in copies:
        copy.start()
    for copy in copies:
        copy.wait()


def pack_kernel(odd_ref, tracer_hbm, cot_hbm, wind_hbm, out_ref, one_ref, two_ref, tracer_ref, cot_ref, wind_ref, sems):
    run_copies((tracer_hbm, cot_hbm, wind_hbm), (tracer_ref, cot_ref, wind_ref), sems)
    count, tile, cols = tracer_ref.shape
    n_wind = wind_ref.shape[0]
    lane = lax.broadcasted_iota(jnp.int32, (1, LANES), 1)
    mask = side_mask()
    odd = jnp.full((HALO, cols), odd_ref[0], jnp.int32) == 1

    def lifted(value, j):
        both = jnp.where(lane < HALO, value[:, :LANES], value[:, cols - LANES :])
        return pltpu.roll(jnp.where(mask, both, 0.0), HALO + 2 * HALO * j, 1)

    def put(entry, first, last):
        one_ref[entry] = jnp.where(odd, first, last).astype(BF16)
        two_ref[entry] = jnp.where(odd, last, first).astype(BF16)

    groups = count // GROUP
    for group in range(groups):
        totals = [jnp.zeros(out_ref.shape[1:], F32)] * 2
        for start in range(0, GROUP, 4):
            first, last = [], []
            for part in range(4):
                j = start + part
                t = group * GROUP + j
                tracer, cot = tracer_ref[t].astype(F32), cot_ref[t].astype(F32)
                totals = [totals[0] + lifted(tracer, j), totals[1] + lifted(cot, j)]
                put(
                    t,
                    jnp.concatenate([tracer[:3], cot[:1]], axis=0),
                    jnp.concatenate([cot[tile - 2 : tile - 1], tracer[tile - 3 :]], axis=0),
                )
                first.append(cot[1:2])
                last.append(cot[tile - 1 :])
            put(count + t // 4, jnp.concatenate(first, axis=0), jnp.concatenate(last, axis=0))
        out_ref[group] = totals[0].astype(BF16)
        out_ref[groups + 1 + group] = totals[1].astype(BF16)
    base = count + count // 4
    total = jnp.zeros(out_ref.shape[1:], F32)
    for i in range(n_wind):
        value = wind_ref[i]
        for part in range(3):
            high = value.astype(BF16).astype(F32)
            total = total + lifted(high, part * n_wind + i)
            put(base + part * n_wind + i, high[:HALO], high[tile - HALO :])
            value = value - high
    out_ref[groups] = total.astype(BF16)
    out_ref[2 * groups + 1] = jnp.zeros(out_ref.shape[1:], BF16)


def picker(shape, source_axis, wanted):
    source = lax.broadcasted_iota(jnp.int32, shape, source_axis)
    target = lax.broadcasted_iota(jnp.int32, shape, 1 - source_axis)
    return jnp.where(source == wanted(target), 1.0, 0.0).astype(BF16)


def prep_kernel(
    c1_hbm, b1_hbm, c2_hbm, b2_hbm, head_hbm,
    w1_ref, w2_ref, w2b_ref, w1b_ref, hw_ref, ht_ref, b1_ref, b2_ref,
    c1, b1, c2, b2, head, wide_ref, slim_ref, tall_ref, sems,
):
    run_copies((c1_hbm, b1_hbm, c2_hbm, b2_hbm, head_hbm), (c1, b1, c2, b2, head), sems)
    n_wind = c1.shape[1] // 9

    def wanted2(target):
        return 9 * (target & (CH - 1)) + (target >> 5)

    def wanted1(target):
        a, r = target >> 4, target & 15
        b = (r >= n_wind).astype(jnp.int32) + (r >= 2 * n_wind).astype(jnp.int32)
        return jnp.where(r < 3 * n_wind, 9 * (r - n_wind * b) + 3 * a + b, -1)

    both2 = jnp.concatenate(halves(c2[...]), axis=0)
    size = both2.shape[1]
    w2_ref[...] = jnp.dot(both2, picker((size, size), 0, wanted2), preferred_element_type=F32).astype(BF16)
    turned = lax.dot_general(picker((size, size), 1, wanted2), both2, NT, preferred_element_type=F32)
    both1 = jnp.concatenate(halves(c1[...]), axis=0)
    size = both1.shape[1]
    w1_ref[...] = jnp.dot(both1, picker((size, 48), 0, wanted1), preferred_element_type=F32).astype(BF16)
    turned1 = lax.dot_general(picker((48, size), 1, wanted1), both1, NT, preferred_element_type=F32)
    slim_ref[...] = jnp.zeros(slim_ref.shape, F32)
    for q in range(9):
        where = slice(q * CH, (q + 1) * CH)
        start = q // 3 * 16 + q % 3 * n_wind
        for part in range(2):
            lanes = slice(part * CH, (part + 1) * CH)
            wide_ref[lanes, where] = turned[where, lanes]
            slim_ref[16 * part : 16 * part + n_wind, where] = turned1[start : start + n_wind, lanes]
    w2b_ref[...] = wide_ref[...].astype(BF16)
    w1b_ref[...] = slim_ref[...].astype(BF16)
    tall_ref[...] = jnp.zeros(tall_ref.shape, F32)
    for level in range(LEVELS):
        rows = slice(9 * level, 9 * level + 9)
        part = head[rows, :]
        part = CORRECTION * (part - jnp.sum(part, axis=0, keepdims=True) / 9.0)
        high = part.astype(BF16).astype(F32)
        tall_ref[rows, :] = high
        tall_ref[CH + 9 * level : CH + 9 * level + 9, :] = part - high
    tall = tall_ref[...].astype(BF16)
    hw_ref[...] = tall
    unit = picker((CH, CH), 0, lambda target: target)
    across = lax.dot_general(unit, tall, NT, preferred_element_type=F32)
    ht_ref[:CH, :] = across[:, :CH].astype(BF16)
    ht_ref[CH:, :] = across[:, CH:].astype(BF16)
    for source, target in ((b1, b1_ref), (b2, b2_ref)):
        target[...] = jnp.sum(unit.astype(F32) * source[...], axis=1, keepdims=True)


def grad_kernel(levels_ref, tracer_ref, cot_ref, side_ref, below_ref, above_ref, out_ref, moved_ref, held_ref):
    count = levels_ref.shape[0]
    slots, rows, width = moved_ref.shape[1:]
    channels = below_ref.shape[0] - 3
    groups = count // GROUP
    lower = jnp.int32(0)
    for group in range(groups):
        near = sides_of(group, side_ref, below_ref, above_ref, channels)
        far = sides_of(groups + 1 + group, side_ref, below_ref, above_ref, channels)

        def fill(entry, lower):
            spare = count + group * (GROUP // 4) + entry
            spare = rows_of(below_ref[spare], above_ref[spare])
            for part in range(4):
                j = 4 * entry + part
                t = group * GROUP + j
                low = levels_ref[t] == 0
                slot = jnp.where(low, lower, slots - 1 - t + lower)
                strip = rows_of(below_ref[t], above_ref[t])
                field = joined(tracer_ref[t], near[0], strip, near[1], j)
                cot = joined(cot_ref[t], far[0], cot_strip(strip, spare, part), far[1], j)
                for step in range(3):
                    moved_ref[step, slot] = turn(field, STEPS[step], 1)
                    held_ref[step, slot] = turn(cot, -STEPS[step], 0)
                lower = jnp.where(low, lower + 1, lower)
            return lower

        lower = lax.fori_loop(0, GROUP // 4, fill, lower)
    for gap in (0, 1, 2, 5, 6, 7):
        for step in range(3):
            moved_ref[step, lower + gap] = jnp.zeros((rows, width), F32)
            held_ref[step, lower + gap] = jnp.zeros((rows, width), F32)
    for level in range(LEVELS):
        trips = lax.shift_right_logical((lower if level == 0 else count - lower) + 3, 2)
        for start in range(0, width, LANES):
            lanes = slice(start, start + LANES)

            def step(trip, sums):
                for part in range(4):
                    slot = 4 * trip + part
                    slot = slot if level == 0 else slots - 1 - slot
                    near = [moved_ref[b, slot, :, lanes] for b in range(3)]
                    far = [held_ref[a, slot, :, lanes] for a in range(3)]
                    sums = tuple(sums[k] + far[k // 3] * near[k % 3] for k in range(9))
                return sums

            sums = lax.fori_loop(0, trips, step, (jnp.zeros((rows, LANES), F32),) * 9)
            for k in range(9):
                out_ref[9 * level + k, :, lanes] = turn(sums[k], STEPS[k // 3], 0)


def put_moved(high_ref, low_ref, row, value, sign):
    width = value.shape[1]
    for ref, part in zip((high_ref, low_ref), halves(value)):
        for b in range(3):
            ref[b * CH : (b + 1) * CH, row * width : (row + 1) * width] = turn(part, sign * STEPS[b], 1)


def convolved(weights, high_ref, low_ref, starts, width):
    def rows(ref):
        return jnp.concatenate([ref[:, start * width : (start + 2) * width] for start in starts], axis=0)

    return dot3(weights, rows(high_ref), rows(low_ref))


def put_winds(wind_ref, stack_ref, first_row, rows):
    width = wind_ref.shape[2]
    count = wind_ref.shape[0]
    for row in range(rows):
        value = wind_ref[:, first_row + row, :]
        for b in range(3):
            stack_ref[b * count : (b + 1) * count, row * width : (row + 1) * width] = turn(value, STEPS[b], 1)


def forward_kernel(
    own_ref, side_ref, below_ref, above_ref, inside_ref, w1_ref, b1_ref, w2_ref, b2_ref, head_ref,
    first_ref, second_ref, corr_ref, wind_ref,
    stack_ref, wind_high, wind_low, high_ref, low_ref,
):
    count, rows, width = wind_ref.shape
    tile, cols = own_ref.shape[1:]
    channels = below_ref.shape[0] - 3
    side, side_rows = sides_of(side_ref.shape[0] // 2 - 1, side_ref, below_ref, above_ref, channels)
    for i in range(count):
        wind_ref[i, HALO : HALO + tile, :cols] = own_ref[i]
        wide = [jnp.zeros((tile, LANES), F32), jnp.zeros((tile, LANES), F32)]
        strip = jnp.zeros((2 * HALO, cols), F32)
        for part in range(3):
            j = part * count + i
            wide[0] = wide[0] + placed(side, j)
            wide[1] = wide[1] + placed(side_rows, j)
            index = channels - 3 * count + j
            strip = strip + rows_of(below_ref[index], above_ref[index])
        wind_ref[i, HALO : HALO + tile, cols:] = wide[0]
        for value, where in ((strip, slice(0, cols)), (wide[1], slice(cols, width))):
            wind_ref[i, HALO + tile :, where] = value[:HALO]
            wind_ref[i, :HALO, where] = value[HALO:]
    stack_ref[...] = jnp.zeros(stack_ref.shape, F32)
    put_winds(wind_ref, stack_ref, 0, rows)
    wind_high[...], wind_low[...] = halves(stack_ref[...])
    bias1, bias2 = b1_ref[...], b2_ref[...]
    inside = jnp.concatenate([inside_ref[...]] * 2, axis=1)
    for row in range(0, rows - 2, 2):
        starts = (row, row + 1, row + 2)
        value = jnp.tanh(convolved(w1_ref[...], wind_high, wind_low, starts, width) + bias1) * inside
        first_ref[:, row * width : (row + 2) * width] = value
        for part in range(2):
            put_moved(high_ref, low_ref, row + part, value[:, part * width : (part + 1) * width], 1)
    for row in range(0, rows - 4, 2):
        starts = (row, row + 1, row + 2)
        value = jnp.tanh(convolved(w2_ref[...], high_ref, low_ref, starts, width) + bias2)
        second_ref[:, row * width : (row + 2) * width] = value
        high, low = halves(value)
        corr = dot3(head_ref[...], high, low)
        for part in range(2):
            corr_ref[:, 2 + row + part, :] = corr[: corr_ref.shape[0], part * width : (part + 1) * width]


def backward_kernel(
    mine_ref, other_ref, wind_ref, inside_ref, first_ref, second_ref, headt_ref, w2b_ref,
    par_ref, d1_ref,
    sum_ref, g_ref, d2_high, d2_low, own2_high, own2_low, act_high, act_low, own1_high, own1_low, wind_stack,
):
    cells = g_ref.shape[1]
    width = wind_ref.shape[2]
    cols = width - LANES
    ring = cells // width
    tile = ring - 4
    sum_ref[...] = mine_ref[...] + other_ref[...]
    wrap = sum_ref.shape[1]
    nine = sum_ref.shape[0]
    g_ref[...] = jnp.zeros(g_ref.shape, F32)
    for row in range(ring):
        g_ref[:nine, row * width : (row + 1) * width] = sum_ref[:, (row - 2) % wrap, :]
    own = lax.broadcasted_iota(jnp.int32, (1, width), 1) < cols
    inside = inside_ref[...]
    for ref in (own2_high, own2_low, own1_high, own1_low):
        ref[...] = jnp.zeros(ref.shape, BF16)
    wind_stack[...] = jnp.zeros(wind_stack.shape, F32)
    put_winds(wind_ref, wind_stack, 3, tile + 2)
    wind_stack[12:13, :] = jnp.ones((1, wind_stack.shape[1]), F32)
    bias2 = jnp.zeros((CH, width), F32)

    def put_own(high_ref, low_ref, x, value):
        high, low = halves(jnp.where(own, value, 0.0))
        for a in range(3):
            high_ref[a * CH : (a + 1) * CH, (x + a) * width : (x + a + 1) * width] = high
            low_ref[a * CH : (a + 1) * CH, (x + a) * width : (x + a + 1) * width] = low

    for row in range(0, ring, 2):
        where = slice(row * width, (row + 2) * width)
        high, low = halves(g_ref[:, where])
        hidden = dot3(headt_ref[...], high, low)
        second = second_ref[:, where]
        delta = hidden * (1.0 - second * second)
        for part in range(2):
            value = delta[:, part * width : (part + 1) * width]
            put_moved(d2_high, d2_low, row + part, value, -1)
            x = row + part - 2
            if 0 <= x < tile:
                put_own(own2_high, own2_low, x, value)
                bias2 = bias2 + jnp.where(own, value, 0.0)
    for row in range(tile + 2):
        put_moved(act_high, act_low, row, first_ref[:, (row + 2) * width : (row + 3) * width], 1)
    par_ref[...] = jnp.zeros(par_ref.shape, F32)
    par_ref[:, : 3 * CH] = dot3_nt(act_high[...], act_low[...], own2_high[...], own2_low[...])
    par_ref[:CH, 3 * CH + 16 : 3 * CH + 17] = jnp.sum(bias2, axis=1, keepdims=True)
    inside2 = jnp.concatenate([inside] * 2, axis=1)
    for row in range(0, tile + 2, 2):
        total = convolved(w2b_ref[...], d2_high, d2_low, (row + 2, row + 1, row), width)
        first = first_ref[:, (row + 2) * width : (row + 4) * width]
        delta = total * (1.0 - first * first) * inside2
        d1_ref[:, row * width : (row + 2) * width] = delta
        for part in range(2):
            value = delta[:, part * width : (part + 1) * width]
            x = row + part - 1
            if 0 <= x < tile:
                put_own(own1_high, own1_low, x, value)
    high, low = halves(wind_stack[...])
    par_ref[:, 3 * CH : 3 * CH + 16] = dot3_nt(own1_high[...], own1_low[...], high, low)
    mid = slice(2 * width, (2 + tile) * width)
    own_rows = jnp.concatenate([own] * tile, axis=1)
    g_high, g_low = halves(jnp.where(own_rows, g_ref[:, mid], 0.0))
    s_high, s_low = halves(second_ref[:, mid])
    raw = dot3_nt(s_high, s_low, g_high, g_low)
    for level in range(LEVELS):
        rows = slice((level + 1) * CH, (level + 2) * CH)
        par_ref[rows, 3 * CH + 16 : 3 * CH + 25] = raw[:, 9 * level : 9 * level + 9]


def wind_kernel(mine_ref, other_ref, wind_ref, d1_ref, w1b_ref, wgrad_ref, d1_high, d1_low, net_ref):
    tile, cols = wgrad_ref.shape[1:]
    width = wind_ref.shape[2]
    for row in range(tile + 2):
        put_moved(d1_high, d1_low, row, d1_ref[:, row * width : (row + 1) * width], -1)
    for row in range(0, tile, 2):
        total = convolved(w1b_ref[...], d1_high, d1_low, (row + 2, row + 1, row), width)
        for part in range(2):
            net_ref[:, row + part, :] = total[:4, part * width : part * width + cols]
    for level in range(LEVELS):
        cx = COURANT * wind_ref[2 * level, HALO : HALO + tile, :cols]
        cy = COURANT * wind_ref[2 * level + 1, HALO : HALO + tile, :cols]
        px, py = lax_wendroff(cx), lax_wendroff(cy)
        dx, dy = (0.5 + cx, -2.0 * cx, cx - 0.5), (0.5 + cy, -2.0 * cy, cy - 0.5)
        gx_sum = jnp.zeros((tile, cols), F32)
        gy_sum = jnp.zeros((tile, cols), F32)
        for a in range(3):
            for b in range(3):
                k = 9 * level + 3 * a + b
                grad = mine_ref[k, :tile, :cols] + other_ref[k, :tile, :cols]
                gx_sum = gx_sum + grad * (dx[a] * py[b])
                gy_sum = gy_sum + grad * (px[a] * dy[b])
        wgrad_ref[2 * level] = COURANT * gx_sum + net_ref[2 * level]
        wgrad_ref[2 * level + 1] = COURANT * gy_sum + net_ref[2 * level + 1]


def final_kernel(mine_ref, other_ref, c1_ref, b1_ref, c2_ref, b2_ref, head_ref):
    total = mine_ref[...] + other_ref[...]
    across = jnp.concatenate([total, jnp.zeros((LANES - total.shape[0], LANES), F32)], axis=0).T
    size2, size1 = c2_ref.shape[1], c1_ref.shape[1]
    n_wind = size1 // 9
    split, rest = [], total
    turned, rest_t = [], across[: 3 * CH, : 3 * CH]
    for _ in range(3):
        high = rest.astype(BF16)
        split.append(high)
        rest = rest - high.astype(F32)
        high = rest_t.astype(BF16)
        turned.append(high)
        rest_t = rest_t - high.astype(F32)
    source = lax.broadcasted_iota(jnp.int32, (3 * CH, size2), 0)
    target = lax.broadcasted_iota(jnp.int32, (3 * CH, size2), 1)
    source1 = lax.broadcasted_iota(jnp.int32, (LANES, size1), 0) - 3 * CH
    target1 = lax.broadcasted_iota(jnp.int32, (LANES, size1), 1)
    out2 = jnp.zeros((CH, size2), F32)
    out1 = jnp.zeros((CH, size1), F32)
    for a in range(3):
        rows = slice(a * CH, (a + 1) * CH)
        pick2 = jnp.zeros((3 * CH, size2), F32)
        pick1 = jnp.zeros((LANES, size1), F32)
        for b in range(3):
            shift = 3 * a + b
            lies = (source >= b * CH) & (source < (b + 1) * CH)
            pick2 = jnp.where(lies & (target == 9 * (source - b * CH) + shift), 1.0, pick2)
            lies = (source1 >= b * n_wind) & (source1 < (b + 1) * n_wind)
            pick1 = jnp.where(lies & (target1 == 9 * (source1 - b * n_wind) + shift), 1.0, pick1)
        pick2, pick1 = pick2.astype(BF16), pick1.astype(BF16)
        for part in range(3):
            out2 = out2 + jnp.dot(turned[part][rows], pick2, preferred_element_type=F32)
            out1 = out1 + jnp.dot(split[part][rows], pick1, preferred_element_type=F32)
    c2_ref[...] = out2
    c1_ref[...] = out1
    b1_ref[...] = across[3 * CH + 3 * n_wind : 3 * CH + 3 * n_wind + 1, CH : 2 * CH]
    b2_ref[...] = across[3 * CH + 16 : 3 * CH + 17, :CH]
    for level in range(LEVELS):
        raw = across[3 * CH + 16 : 3 * CH + 25, (level + 1) * CH : (level + 2) * CH]
        mean = jnp.sum(raw, axis=0, keepdims=True) / 9.0
        head_ref[9 * level : 9 * level + 9, :] = CORRECTION * (raw - mean)


def lax_wendroff(courant):
    return (
        0.5 * courant + 0.5 * courant * courant,
        1.0 - courant * courant,
        0.5 * courant * courant - 0.5 * courant,
    )


def tracer_kernel(levels_ref, wind_ref, corr_ref, cot_ref, side_ref, below_ref, above_ref, out_ref, coef_ref):
    count, tile, cols = out_ref.shape
    for level in range(LEVELS):
        px = lax_wendroff(COURANT * wind_ref[2 * level])
        py = lax_wendroff(COURANT * wind_ref[2 * level + 1])
        for a in range(3):
            for b in range(3):
                coef = corr_ref[9 * level + 3 * a + b] + px[a] * py[b]
                coef = turn(turn(coef, -STEPS[b], 1), HALO - STEPS[a], 0)
                coef_ref[level, 3 * a + b] = coef[:tile, :cols]

    channels = below_ref.shape[0] - 3
    groups = count // GROUP
    for group in range(groups):
        sides = sides_of(groups + 1 + group, side_ref, below_ref, above_ref, channels)

        def step(entry, carry):
            spare = count + group * (GROUP // 4) + entry
            spare = rows_of(below_ref[spare], above_ref[spare])
            for part in range(4):
                j = 4 * entry + part
                t = group * GROUP + j
                level = levels_ref[t]
                strip = cot_strip(rows_of(below_ref[t], above_ref[t]), spare, part)
                field = joined(cot_ref[t], sides[0], strip, sides[1], j)
                total = jnp.zeros((tile, cols), F32)
                for b in range(3):
                    moved = turn(field, -STEPS[b], 1)
                    for a in range(3):
                        total = total + coef_ref[level, 3 * a + b] * turn(moved, -STEPS[a], 0)[:tile, :cols]
                out_ref[t] = total.astype(BF16)
            return carry

        lax.fori_loop(0, GROUP // 4, step, 0)


def call(kernel, outs, scratch, operands, spaces=None, flops=2_000_000, vmem=40):
    specs = [pl.BlockSpec(memory_space=(spaces or {}).get(i, pltpu.VMEM)) for i in range(len(operands))]
    whole = pl.BlockSpec(memory_space=pltpu.VMEM)
    return pl.pallas_call(
        kernel,
        out_shape=outs,
        in_specs=specs,
        out_specs=[whole] * len(outs) if isinstance(outs, (list, tuple)) else whole,
        scratch_shapes=scratch,
        compiler_params=pltpu.CompilerParams(vmem_limit_bytes=vmem * 1024 * 1024),
        cost_estimate=pl.CostEstimate(flops=flops, bytes_accessed=2_000_000, transcendentals=0),
    )(*operands)


def ring_pairs(size, wrap):
    up = [(i, (i + 1) % size) for i in range(size if wrap else size - 1)]
    return up, [(j, i) for i, j in up]


def sum_rounds(value, axes, beside):
    other, done = jnp.zeros_like(value), []
    for axis in axes:
        size = lax.axis_size(axis)
        if size & (size - 1):
            value, other = lax.psum(value + other, axis), jnp.zeros_like(value)
            continue
        step = 1
        while step < size:
            value = value + other
            if step > 1 or axis != axes[0]:
                if len(done) < len(beside):
                    value, made = lax.optimization_barrier((value, beside[len(done)]))
                    done.append(made)
            other = lax.ppermute(value, axis, [(i, i ^ step) for i in range(size)])
            step *= 2
    return value, other, tuple(done) + tuple(beside[len(done) :])


def body(tracers, cotangent, winds, levels, conv1, bias1, conv2, bias2, head):
    count, tile, cols = tracers.shape
    n_wind = winds.shape[0]
    width = cols + LANES
    rows = tile + 2 * HALO
    vmem, spec = pltpu.VMEM, jax.ShapeDtypeStruct
    gy, gy_size = lax.axis_index("gy"), lax.axis_size("gy")
    gx, gx_size = lax.axis_index("gx"), lax.axis_size("gx")
    paired = gx_size % 2 == 0
    odd = (gx % 2 if paired else 0 * gx).astype(jnp.int32)
    strip = spec((count + count // 4 + 3 * n_wind, HALO, cols), BF16)
    packed, one, two = call(
        pack_kernel,
        [spec((2 * (count // GROUP) + 2, tile, LANES), BF16), strip, strip],
        [vmem((count, tile, cols), BF16)] * 2
        + [vmem((n_wind, tile, cols), F32), pltpu.SemaphoreType.DMA((3,))],
        (odd[None], tracers, cotangent, winds),
        {0: pltpu.SMEM} | {i: pltpu.HBM for i in range(1, 4)},
        vmem=60,
    )
    spare = ((0, packed.shape[0] // 2), (0, 0), (0, 0))
    one, two = lax.optimization_barrier((jnp.pad(one, spare), jnp.pad(two, spare)))
    up, down = ring_pairs(gy_size, False)
    lane = lax.broadcasted_iota(jnp.int32, (1, 1, LANES), 2) % (2 * HALO)
    if gy_size == 2:
        got = lax.ppermute(packed, "gy", up + down)
        side = jnp.where(jnp.where(gy == 0, lane >= HALO, lane < HALO), got, 0)
    else:
        right = lax.ppermute(packed, "gy", down)
        left = lax.ppermute(packed, "gy", up)
        side = jnp.where(lane >= HALO, right, left)
    side = side.astype(BF16)
    w1, w2, w2b, w1b, head_w, head_t, bias1_col, bias2_col = call(
        prep_kernel,
        [
            spec((2 * CH, 48), BF16),
            spec((2 * CH, 9 * CH), BF16),
            spec((2 * CH, 9 * CH), BF16),
            spec((32, 9 * CH), BF16),
            spec((2 * CH, CH), BF16),
            spec((2 * CH, CH), BF16),
            spec((CH, 1), F32),
            spec((CH, 1), F32),
        ],
        [
            vmem(conv1.shape, F32),
            vmem((1, CH), F32),
            vmem(conv2.shape, F32),
            vmem((1, CH), F32),
            vmem(head.shape, F32),
            vmem((2 * CH, 9 * CH), F32),
            vmem((32, 9 * CH), F32),
            vmem((2 * CH, CH), F32),
            pltpu.SemaphoreType.DMA((5,)),
        ],
        lax.optimization_barrier((conv1, bias1[None], conv2, bias2[None], head, side))[:5],
        {i: pltpu.HBM for i in range(5)},
    )
    half = side.shape[0] // 2
    wide = jnp.concatenate([side[:half], side[half:]], axis=2)
    first_rows, last_rows = wide[:, :HALO], wide[:, tile - HALO :]
    is_odd = odd == 1
    one = lax.dynamic_update_slice(one, jnp.where(is_odd, first_rows, last_rows), (one.shape[0] - half, 0, 0))
    two = lax.dynamic_update_slice(two, jnp.where(is_odd, last_rows, first_rows), (two.shape[0] - half, 0, 0))
    if paired:
        ahead = [(i, i ^ 1) for i in range(gx_size)]
        behind = [(i, (i + 1) % gx_size if i % 2 else (i - 1) % gx_size) for i in range(gx_size)]
        one, two = lax.ppermute(one, "gx", ahead), lax.ppermute(two, "gx", behind)
        below, above = jnp.where(is_odd, two, one), jnp.where(is_odd, one, two)
    else:
        up, down = ring_pairs(gx_size, True)
        above, below = lax.ppermute(one, "gx", up), lax.ppermute(two, "gx", down)
    place = lax.broadcasted_iota(jnp.int32, (1, width), 1)
    has_right, has_left = gy < gy_size - 1, gy > 0
    inside = jnp.where(place < cols, True, jnp.where(place < cols + LANES // 2, has_right, has_left)).astype(F32)

    levels = jnp.clip(levels, 0, LEVELS - 1)
    above, below, w1, w2, levels = lax.optimization_barrier((above, below, w1, w2, levels))
    mine = call(
        grad_kernel,
        spec((9 * LEVELS, rows, width), F32),
        [vmem((3, count + 8, rows, width), F32)] * 2,
        (levels, tracers, cotangent, side, below, above),
        {0: pltpu.SMEM},
    )
    other = lax.ppermute(mine, "tracer", [(i, i ^ 1) for i in range(lax.axis_size("tracer"))])
    first, second, corr, wind_ext = call(
        forward_kernel,
        [
            spec((CH, (rows - 2) * width), F32),
            spec((CH, (rows - 4) * width), F32),
            spec((9 * LEVELS, rows, width), F32),
            spec((n_wind, rows, width), F32),
        ],
        [vmem((16, rows * width), F32)]
        + [vmem((16, rows * width), BF16)] * 2
        + [vmem((3 * CH, (rows - 2) * width), BF16)] * 2,
        (winds, side, below, above, inside, w1, bias1_col, w2, bias2_col, head_w),
    )
    ring, own = (tile + 4) * width, (tile + 2) * width
    params, delta = call(
        backward_kernel,
        [spec((3 * CH, LANES), F32), spec((CH, own), F32)],
        [vmem((9 * LEVELS, rows, width), F32), vmem((CH, ring), F32)]
        + [vmem((3 * CH, ring), BF16)] * 2
        + [vmem((3 * CH, own), BF16)] * 6
        + [vmem((16, own), F32)],
        (mine, other, wind_ext, inside, first, second, head_t, w2b),
    )
    tracer_grad = call(
        tracer_kernel,
        spec((count, tile, cols), BF16),
        [vmem((LEVELS, 9, tile, cols), F32)],
        (levels, wind_ext, corr, cotangent, side, below, above),
        {0: pltpu.SMEM},
    )
    wind_grad = call(
        wind_kernel,
        spec((n_wind, tile, cols), F32),
        [vmem((3 * CH, own), BF16)] * 2 + [vmem((n_wind, tile, cols), F32)],
        (mine, other, wind_ext, delta, w1b),
    )
    mine, other, (tracer_grad, wind_grad) = sum_rounds(params, ("gy", "gx"), (tracer_grad, wind_grad))
    conv1_grad, bias1_grad, conv2_grad, bias2_grad, head_grad = call(
        final_kernel,
        [spec(conv1.shape, F32), spec((1, CH), F32), spec(conv2.shape, F32), spec((1, CH), F32), spec(head.shape, F32)],
        [],
        (mine, other),
        flops=200_000,
    )
    return (tracer_grad, wind_grad, conv1_grad, bias1_grad[0], conv2_grad, bias2_grad[0], head_grad)


def solution(mesh):
    return jax.shard_map(
        body,
        mesh=mesh,
        in_specs=(
            P(("member", "tracer"), "gx", "gy"),
            P(("member", "tracer"), "gx", "gy"),
            P("member", "gx", "gy"),
            P(("member", "tracer")),
            P(),
            P(),
            P(),
            P(),
            P(),
        ),
        out_specs=(
            P(("member", "tracer"), "gx", "gy"),
            P("member", "gx", "gy"),
            P("member", None),
            P("member"),
            P("member", None),
            P("member"),
            P("member", None),
        ),
        check_vma=False,
    )
```

```python
import functools

import jax
import jax.numpy as jnp
from jax import lax
from jax.experimental import pallas as pl
from jax.experimental.pallas import tpu as pltpu
from jax.sharding import PartitionSpec as P

LEVELS = 2
CH = 32
COURANT = 0.5
CORRECTION = 0.2
STEPS = (-1, 0, 1)
HALO = 4
LANES = 128
GROUP = LANES // (2 * HALO)
F32 = jnp.float32
BF16 = jnp.bfloat16
NT = (((1,), (1,)), ((), ()))


def halves(value):
    high = value.astype(BF16)
    return high, (value - high.astype(F32)).astype(BF16)


def dot3(weights, high, low):
    rows = weights.shape[0] // 2
    both = jnp.dot(weights, jnp.concatenate([high, low], axis=0), preferred_element_type=F32)
    return both[:rows] + both[rows:]


def dot3_nt(left, right):
    rows, cols = left.shape[0] // 2, right.shape[0] // 2
    out = lax.dot_general(left, right, NT, preferred_element_type=F32)
    return out[:rows, :cols] + out[:rows, cols:] + out[rows:, :cols]


def turn(value, step, axis):
    shift = (-step) % value.shape[axis]
    return pltpu.roll(value, shift, axis) if shift else value


def side_mask():
    lane = lax.broadcasted_iota(jnp.int32, (1, LANES), 1)
    return (lane < HALO) | (lane >= LANES - HALO)


def rows_of(below, above):
    return jnp.concatenate([below.astype(F32), above.astype(F32)], axis=0)


def sides_of(group, side_ref, below_ref, above_ref, channels):
    half = side_ref.shape[0] // 2
    index = channels + group % half
    where = slice(group // half * LANES, (group // half + 1) * LANES)
    return side_ref[group].astype(F32), rows_of(below_ref[index, :, where], above_ref[index, :, where])


def placed(side, j):
    return jnp.where(side_mask(), pltpu.roll(side, LANES - HALO - 2 * HALO * j, 1), 0.0)


def joined(main, side, strip, strip_side, j):
    top = jnp.concatenate([main.astype(F32), placed(side, j)], axis=1)
    return jnp.concatenate([top, jnp.concatenate([strip, placed(strip_side, j)], axis=1)], axis=0)


def cot_strip(strip, spare, part):
    slot = lax.broadcasted_iota(jnp.int32, strip.shape, 0)
    value = jnp.where(slot == 0, turn(strip, 3, 0), jnp.where(slot == 6, turn(strip, -2, 0), 0.0))
    value = jnp.where(slot == 1, spare[part : part + 1], value)
    return jnp.where(slot == 7, spare[HALO + part : HALO + part + 1], value)


def run_copies(sources, targets, sems):
    copies = [pltpu.make_async_copy(a, b, sems.at[i]) for i, (a, b) in enumerate(zip(sources, targets))]
    for copy in copies:
        copy.start()
    for copy in copies:
        copy.wait()


def pack_kernel(odd_ref, tracer_hbm, cot_hbm, wind_hbm, out_ref, one_ref, two_ref, tracer_ref, cot_ref, wind_ref, sems):
    run_copies((tracer_hbm, cot_hbm, wind_hbm), (tracer_ref, cot_ref, wind_ref), sems)
    count, tile, cols = tracer_ref.shape
    n_wind = wind_ref.shape[0]
    lane = lax.broadcasted_iota(jnp.int32, (1, LANES), 1)
    mask = side_mask()
    odd = jnp.full((HALO, cols), odd_ref[0], jnp.int32) == 1

    def lifted(value, j):
        both = jnp.where(lane < HALO, value[:, :LANES], value[:, cols - LANES :])
        return pltpu.roll(jnp.where(mask, both, 0.0), HALO + 2 * HALO * j, 1)

    def put(entry, first, last):
        one_ref[entry] = jnp.where(odd, first, last).astype(BF16)
        two_ref[entry] = jnp.where(odd, last, first).astype(BF16)

    groups = count // GROUP
    for group in range(groups):
        totals = [jnp.zeros(out_ref.shape[1:], F32)] * 2
        for start in range(0, GROUP, 4):
            first, last = [], []
            for part in range(4):
                j = start + part
                t = group * GROUP + j
                tracer, cot = tracer_ref[t].astype(F32), cot_ref[t].astype(F32)
                totals = [totals[0] + lifted(tracer, j), totals[1] + lifted(cot, j)]
                put(
                    t,
                    jnp.concatenate([tracer[:3], cot[:1]], axis=0),
                    jnp.concatenate([cot[tile - 2 : tile - 1], tracer[tile - 3 :]], axis=0),
                )
                first.append(cot[1:2])
                last.append(cot[tile - 1 :])
            put(count + t // 4, jnp.concatenate(first, axis=0), jnp.concatenate(last, axis=0))
        out_ref[group] = totals[0].astype(BF16)
        out_ref[groups + 1 + group] = totals[1].astype(BF16)
    base = count + count // 4
    total = jnp.zeros(out_ref.shape[1:], F32)
    for i in range(n_wind):
        value = wind_ref[i]
        for part in range(3):
            high = value.astype(BF16).astype(F32)
            total = total + lifted(high, part * n_wind + i)
            put(base + part * n_wind + i, high[:HALO], high[tile - HALO :])
            value = value - high
    out_ref[groups] = total.astype(BF16)
    out_ref[2 * groups + 1] = jnp.zeros(out_ref.shape[1:], BF16)


def picker(shape, source_axis, wanted):
    source = lax.broadcasted_iota(jnp.int32, shape, source_axis)
    target = lax.broadcasted_iota(jnp.int32, shape, 1 - source_axis)
    return jnp.where(source == wanted(target), 1.0, 0.0).astype(BF16)


def prep_kernel(
    c1_hbm, b1_hbm, c2_hbm, b2_hbm, head_hbm,
    w1_ref, w2_ref, w2b_ref, w1b_ref, hw_ref, ht_ref, b1_ref, b2_ref,
    c1, b1, c2, b2, head, wide_ref, slim_ref, tall_ref, pair_ref, sems,
):
    run_copies((c1_hbm, b1_hbm, c2_hbm, b2_hbm, head_hbm), (c1, b1, c2, b2, head), sems)
    n_wind = c1.shape[1] // 9

    def wanted2(target):
        return 9 * (target & (CH - 1)) + (target >> 5)

    def wanted1(target):
        a, r = target >> 4, target & 15
        b = (r >= n_wind).astype(jnp.int32) + (r >= 2 * n_wind).astype(jnp.int32)
        return jnp.where(r < 3 * n_wind, 9 * (r - n_wind * b) + 3 * a + b, -1)

    def doubled(target, value):
        rows, depth = value.shape[0] // 2, value.shape[1]
        pair_ref[: 2 * rows, :depth] = value
        pair_ref[:rows, depth : 2 * depth] = value[:rows]
        pair_ref[rows : 2 * rows, depth : 2 * depth] = jnp.zeros((rows, depth), F32)
        target[...] = pair_ref[: 2 * rows, : 2 * depth].astype(BF16)

    both2 = jnp.concatenate(halves(c2[...]), axis=0)
    size = both2.shape[1]
    doubled(w2_ref, jnp.dot(both2, picker((size, size), 0, wanted2), preferred_element_type=F32))
    turned = lax.dot_general(picker((size, size), 1, wanted2), both2, NT, preferred_element_type=F32)
    both1 = jnp.concatenate(halves(c1[...]), axis=0)
    size = both1.shape[1]
    doubled(w1_ref, jnp.dot(both1, picker((size, 48), 0, wanted1), preferred_element_type=F32))
    turned1 = lax.dot_general(picker((48, size), 1, wanted1), both1, NT, preferred_element_type=F32)
    slim_ref[...] = jnp.zeros(slim_ref.shape, F32)
    for q in range(9):
        where = slice(q * CH, (q + 1) * CH)
        start = q // 3 * 16 + q % 3 * n_wind
        for part in range(2):
            lanes = slice(part * CH, (part + 1) * CH)
            wide_ref[lanes, where] = turned[where, lanes]
            slim_ref[16 * part : 16 * part + n_wind, where] = turned1[start : start + n_wind, lanes]
    doubled(w2b_ref, wide_ref[...])
    doubled(w1b_ref, slim_ref[...])
    tall_ref[...] = jnp.zeros(tall_ref.shape, F32)
    for level in range(LEVELS):
        rows = slice(9 * level, 9 * level + 9)
        part = head[rows, :]
        part = CORRECTION * (part - jnp.sum(part, axis=0, keepdims=True) / 9.0)
        high = part.astype(BF16).astype(F32)
        tall_ref[rows, :] = high
        tall_ref[CH + 9 * level : CH + 9 * level + 9, :] = part - high
    tall = tall_ref[...].astype(BF16)
    doubled(hw_ref, tall_ref[...])
    unit = picker((CH, CH), 0, lambda target: target)
    across = lax.dot_general(unit, tall, NT, preferred_element_type=F32)
    doubled(ht_ref, jnp.concatenate([across[:, :CH], across[:, CH:]], axis=0))
    for source, target in ((b1, b1_ref), (b2, b2_ref)):
        target[...] = jnp.sum(unit.astype(F32) * source[...], axis=1, keepdims=True)


def gap_zeroed(refs, lower):
    for ref in refs:
        for gap in (0, 1, 2, 5, 6, 7):
            for step in range(3):
                ref[step, lower + gap] = jnp.zeros(ref.shape[2:], F32)


def slot_sums(moved_ref, held_ref, lower, count, store):
    slots, rows, width = moved_ref.shape[1:]
    for level in range(LEVELS):
        trips = lax.shift_right_logical((lower if level == 0 else count - lower) + 3, 2)
        for start in range(0, width, LANES):
            lanes = slice(start, start + LANES)

            def step(trip, sums):
                for part in range(4):
                    slot = 4 * trip + part
                    slot = slot if level == 0 else slots - 1 - slot
                    near = [moved_ref[b, slot, :, lanes] for b in range(3)]
                    far = [held_ref[a, slot, :, lanes] for a in range(3)]
                    sums = tuple(sums[k] + far[k // 3] * near[k % 3] for k in range(9))
                return sums

            sums = lax.fori_loop(0, trips, step, (jnp.zeros((rows, LANES), F32),) * 9)
            for k in range(9):
                store(level, k, lanes, sums[k])


def slot_of(level, t, lower, slots):
    low = level == 0
    return jnp.where(low, lower, slots - 1 - t + lower), jnp.where(low, lower + 1, lower)


def inner_kernel(levels_ref, tracer_ref, cot_ref, side_ref, out_ref, edge_ref, moved_ref, held_ref):
    count, tile, cols = tracer_ref.shape
    slots, _, width = moved_ref.shape[1:]
    half = side_ref.shape[0] // 2
    row = lax.broadcasted_iota(jnp.int32, (tile, width), 0)
    lower = jnp.int32(0)
    for group in range(count // GROUP):
        near, far = side_ref[group].astype(F32), side_ref[half + group].astype(F32)

        def fill(entry, lower):
            for part in range(4):
                j = 4 * entry + part
                t = group * GROUP + j
                slot, lower = slot_of(levels_ref[t], t, lower, slots)
                field = jnp.concatenate([tracer_ref[t].astype(F32), placed(near, j)], axis=1)
                cot = jnp.concatenate([cot_ref[t].astype(F32), placed(far, j)], axis=1)
                for b in range(3):
                    moved_ref[b, slot] = turn(field, STEPS[b], 1)
                later, sooner = turn(cot, 1, 0), turn(cot, -1, 0)
                held_ref[0, slot] = jnp.where(row == tile - 1, 0.0, later)
                held_ref[1, slot] = cot
                held_ref[2, slot] = jnp.where(row == 0, 0.0, sooner)
                edge_ref[0, t] = turn(field, HALO, 0)
                edge_ref[1, t] = jnp.where(row == 0, sooner, later)
            return lower

        lower = lax.fori_loop(0, GROUP // 4, fill, lower)
    gap_zeroed((moved_ref, held_ref), lower)

    def store(level, k, lanes, total):
        out_ref[9 * level + k, :, lanes] = turn(total, STEPS[k // 3], 0)

    slot_sums(moved_ref, held_ref, lower, count, store)


def border_kernel(levels_ref, inner_ref, edge_ref, side_ref, below_ref, above_ref, out_ref, moved_ref, held_ref):
    count = levels_ref.shape[0]
    slots, rows, width = moved_ref.shape[1:]
    tile = inner_ref.shape[1]
    channels = below_ref.shape[0] - side_ref.shape[0] // 2
    groups = count // GROUP
    row = lax.broadcasted_iota(jnp.int32, (rows, width), 0)
    lower = jnp.int32(0)
    for group in range(groups):
        near = sides_of(group, side_ref, below_ref, above_ref, channels)[1]
        far = sides_of(groups + 1 + group, side_ref, below_ref, above_ref, channels)[1]

        def fill(entry, lower):
            spare = count + group * (GROUP // 4) + entry
            spare = rows_of(below_ref[spare], above_ref[spare])
            for part in range(4):
                j = 4 * entry + part
                t = group * GROUP + j
                slot, lower = slot_of(levels_ref[t], t, lower, slots)
                strip = rows_of(below_ref[t], above_ref[t])
                field = jnp.concatenate([strip, placed(near, j)], axis=1)
                field = jnp.where((row == 3) | (row == 4), edge_ref[0, t], field)
                cot = jnp.concatenate([cot_strip(strip, spare, part), placed(far, j)], axis=1)
                edge = edge_ref[1, t]
                for b in range(3):
                    moved_ref[b, slot] = turn(field, STEPS[b], 1)
                held_ref[0, slot] = jnp.where(row == 7, edge, jnp.where(row == 3, turn(cot, -3, 0), turn(cot, 1, 0)))
                held_ref[1, slot] = cot
                held_ref[2, slot] = jnp.where(row == 0, edge, jnp.where(row == 4, turn(cot, 3, 0), turn(cot, -1, 0)))
            return lower

        lower = lax.fori_loop(0, GROUP // 4, fill, lower)
    gap_zeroed((moved_ref, held_ref), lower)
    place = row[:, :LANES]

    def store(level, k, lanes, total):
        index, step = 9 * level + k, STEPS[k // 3]
        inner = inner_ref[index, :, lanes]
        if step:
            last = 7 if step == 1 else 0
            shifted = turn(total, step, 0)
            inner = inner + jnp.where(place == last, shifted, 0.0)
            total = jnp.where(place == last, turn(total, 5 if step == 1 else 3, 0), shifted)
        out_ref[index, :tile, lanes] = inner
        out_ref[index, tile:, lanes] = total

    slot_sums(moved_ref, held_ref, lower, count, store)


def put_moved(high_ref, low_ref, row, value, sign):
    width = value.shape[1]
    for ref, part in zip((high_ref, low_ref), halves(value)):
        for b in range(3):
            ref[b * CH : (b + 1) * CH, row * width : (row + 1) * width] = turn(part, sign * STEPS[b], 1)


def convolved(weights, high_ref, low_ref, starts, width):
    def rows(ref):
        return jnp.concatenate([ref[:, start * width : (start + 2) * width] for start in starts], axis=0)

    return dot3(weights, rows(high_ref), rows(low_ref))


def put_winds(wind_ref, stack_ref, first_row, rows):
    width = wind_ref.shape[2]
    count = wind_ref.shape[0]
    for row in range(rows):
        value = wind_ref[:, first_row + row, :]
        for b in range(3):
            stack_ref[b * count : (b + 1) * count, row * width : (row + 1) * width] = turn(value, STEPS[b], 1)


def forward_kernel(
    own_ref, side_ref, below_ref, above_ref, inside_ref, w1_ref, b1_ref, w2_ref, b2_ref, head_ref,
    first_ref, second_ref, corr_ref, wind_ref,
    stack_ref, wind_high, wind_low, high_ref, low_ref,
):
    count, rows, width = wind_ref.shape
    tile, cols = own_ref.shape[1:]
    channels = below_ref.shape[0] - 3
    side, side_rows = sides_of(side_ref.shape[0] // 2 - 1, side_ref, below_ref, above_ref, channels)
    for i in range(count):
        wind_ref[i, HALO : HALO + tile, :cols] = own_ref[i]
        wide = [jnp.zeros((tile, LANES), F32), jnp.zeros((tile, LANES), F32)]
        strip = jnp.zeros((2 * HALO, cols), F32)
        for part in range(3):
            j = part * count + i
            wide[0] = wide[0] + placed(side, j)
            wide[1] = wide[1] + placed(side_rows, j)
            index = channels - 3 * count + j
            strip = strip + rows_of(below_ref[index], above_ref[index])
        wind_ref[i, HALO : HALO + tile, cols:] = wide[0]
        for value, where in ((strip, slice(0, cols)), (wide[1], slice(cols, width))):
            wind_ref[i, HALO + tile :, where] = value[:HALO]
            wind_ref[i, :HALO, where] = value[HALO:]
    stack_ref[...] = jnp.zeros(stack_ref.shape, F32)
    put_winds(wind_ref, stack_ref, 0, rows)
    wind_high[...], wind_low[...] = halves(stack_ref[...])
    bias1, bias2 = b1_ref[...], b2_ref[...]
    inside = jnp.concatenate([inside_ref[...]] * 2, axis=1)
    for row in range(0, rows - 2, 2):
        starts = (row, row + 1, row + 2)
        value = jnp.tanh(convolved(w1_ref[...], wind_high, wind_low, starts, width) + bias1) * inside
        first_ref[:, row * width : (row + 2) * width] = value
        for part in range(2):
            put_moved(high_ref, low_ref, row + part, value[:, part * width : (part + 1) * width], 1)
    for row in range(0, rows - 4, 2):
        starts = (row, row + 1, row + 2)
        value = jnp.tanh(convolved(w2_ref[...], high_ref, low_ref, starts, width) + bias2)
        second_ref[:, row * width : (row + 2) * width] = value
        high, low = halves(value)
        corr = dot3(head_ref[...], high, low)
        for part in range(2):
            corr_ref[:, 2 + row + part, :] = corr[: corr_ref.shape[0], part * width : (part + 1) * width]


def backward_kernel(
    mine_ref, other_ref, wind_ref, inside_ref, first_ref, second_ref, headt_ref, w2b_ref,
    par_ref, d1_ref,
    sum_ref, g_ref, d2_high, d2_low, own2_ref, act_ref, own1_ref, wind_stack,
):
    cells = g_ref.shape[1]
    width = wind_ref.shape[2]
    cols = width - LANES
    ring = cells // width
    tile = ring - 4
    sum_ref[...] = mine_ref[...] + other_ref[...]
    wrap = sum_ref.shape[1]
    nine = sum_ref.shape[0]
    g_ref[...] = jnp.zeros(g_ref.shape, F32)
    for row in range(ring):
        g_ref[:nine, row * width : (row + 1) * width] = sum_ref[:, (row - 2) % wrap, :]
    own = lax.broadcasted_iota(jnp.int32, (1, width), 1) < cols
    inside = inside_ref[...]
    for ref in (own2_ref, own1_ref):
        ref[...] = jnp.zeros(ref.shape, BF16)
    wind_stack[...] = jnp.zeros(wind_stack.shape, F32)
    put_winds(wind_ref, wind_stack, 3, tile + 2)
    wind_stack[12:13, :] = jnp.ones((1, wind_stack.shape[1]), F32)
    bias2 = jnp.zeros((CH, width), F32)

    def put_own(ref, x, value):
        for half, part in enumerate(halves(jnp.where(own, value, 0.0))):
            for a in range(3):
                start = (3 * half + a) * CH
                ref[start : start + CH, (x + a) * width : (x + a + 1) * width] = part

    for row in range(0, ring, 2):
        where = slice(row * width, (row + 2) * width)
        high, low = halves(g_ref[:, where])
        hidden = dot3(headt_ref[...], high, low)
        second = second_ref[:, where]
        delta = hidden * (1.0 - second * second)
        for part in range(2):
            value = delta[:, part * width : (part + 1) * width]
            put_moved(d2_high, d2_low, row + part, value, -1)
            x = row + part - 2
            if 0 <= x < tile:
                put_own(own2_ref, x, value)
                bias2 = bias2 + jnp.where(own, value, 0.0)
    for row in range(tile + 2):
        put_moved(act_ref.at[: 3 * CH], act_ref.at[3 * CH :], row, first_ref[:, (row + 2) * width : (row + 3) * width], 1)
    par_ref[...] = jnp.zeros(par_ref.shape, F32)
    par_ref[:, : 3 * CH] = dot3_nt(act_ref[...], own2_ref[...])
    par_ref[:CH, 3 * CH + 16 : 3 * CH + 17] = jnp.sum(bias2, axis=1, keepdims=True)
    inside2 = jnp.concatenate([inside] * 2, axis=1)
    for row in range(0, tile + 2, 2):
        total = convolved(w2b_ref[...], d2_high, d2_low, (row + 2, row + 1, row), width)
        first = first_ref[:, (row + 2) * width : (row + 4) * width]
        delta = total * (1.0 - first * first) * inside2
        d1_ref[:, row * width : (row + 2) * width] = delta
        for part in range(2):
            value = delta[:, part * width : (part + 1) * width]
            x = row + part - 1
            if 0 <= x < tile:
                put_own(own1_ref, x, value)
    par_ref[:, 3 * CH : 3 * CH + 16] = dot3_nt(own1_ref[...], jnp.concatenate(halves(wind_stack[...]), axis=0))
    mid = slice(2 * width, (2 + tile) * width)
    own_rows = jnp.concatenate([own] * tile, axis=1)
    grads = jnp.concatenate(halves(jnp.where(own_rows, g_ref[:, mid], 0.0)), axis=0)
    raw = dot3_nt(jnp.concatenate(halves(second_ref[:, mid]), axis=0), grads)
    for level in range(LEVELS):
        rows = slice((level + 1) * CH, (level + 2) * CH)
        par_ref[rows, 3 * CH + 16 : 3 * CH + 25] = raw[:, 9 * level : 9 * level + 9]


def wind_kernel(mine_ref, other_ref, wind_ref, d1_ref, w1b_ref, wgrad_ref, d1_high, d1_low, net_ref):
    tile, cols = wgrad_ref.shape[1:]
    width = wind_ref.shape[2]
    for row in range(tile + 2):
        put_moved(d1_high, d1_low, row, d1_ref[:, row * width : (row + 1) * width], -1)
    for row in range(0, tile, 2):
        total = convolved(w1b_ref[...], d1_high, d1_low, (row + 2, row + 1, row), width)
        for part in range(2):
            net_ref[:, row + part, :] = total[:4, part * width : part * width + cols]
    for level in range(LEVELS):
        cx = COURANT * wind_ref[2 * level, HALO : HALO + tile, :cols]
        cy = COURANT * wind_ref[2 * level + 1, HALO : HALO + tile, :cols]
        px, py = lax_wendroff(cx), lax_wendroff(cy)
        dx, dy = (0.5 + cx, -2.0 * cx, cx - 0.5), (0.5 + cy, -2.0 * cy, cy - 0.5)
        gx_sum = jnp.zeros((tile, cols), F32)
        gy_sum = jnp.zeros((tile, cols), F32)
        for a in range(3):
            for b in range(3):
                k = 9 * level + 3 * a + b
                grad = mine_ref[k, :tile, :cols] + other_ref[k, :tile, :cols]
                gx_sum = gx_sum + grad * (dx[a] * py[b])
                gy_sum = gy_sum + grad * (px[a] * dy[b])
        wgrad_ref[2 * level] = COURANT * gx_sum + net_ref[2 * level]
        wgrad_ref[2 * level + 1] = COURANT * gy_sum + net_ref[2 * level + 1]


def final_kernel(mine_ref, other_ref, c1_ref, b1_ref, c2_ref, b2_ref, head_ref):
    total = mine_ref[...] + other_ref[...]
    across = jnp.concatenate([total, jnp.zeros((LANES - total.shape[0], LANES), F32)], axis=0).T
    size2, size1 = c2_ref.shape[1], c1_ref.shape[1]
    n_wind = size1 // 9
    split, rest = [], total
    turned, rest_t = [], across[: 3 * CH, : 3 * CH]
    for _ in range(3):
        high = rest.astype(BF16)
        split.append(high)
        rest = rest - high.astype(F32)
        high = rest_t.astype(BF16)
        turned.append(high)
        rest_t = rest_t - high.astype(F32)
    source = lax.broadcasted_iota(jnp.int32, (3 * CH, size2), 0)
    target = lax.broadcasted_iota(jnp.int32, (3 * CH, size2), 1)
    source1 = lax.broadcasted_iota(jnp.int32, (LANES, size1), 0) - 3 * CH
    target1 = lax.broadcasted_iota(jnp.int32, (LANES, size1), 1)
    out2 = jnp.zeros((CH, size2), F32)
    out1 = jnp.zeros((CH, size1), F32)
    for a in range(3):
        rows = slice(a * CH, (a + 1) * CH)
        pick2 = jnp.zeros((3 * CH, size2), F32)
        pick1 = jnp.zeros((LANES, size1), F32)
        for b in range(3):
            shift = 3 * a + b
            lies = (source >= b * CH) & (source < (b + 1) * CH)
            pick2 = jnp.where(lies & (target == 9 * (source - b * CH) + shift), 1.0, pick2)
            lies = (source1 >= b * n_wind) & (source1 < (b + 1) * n_wind)
            pick1 = jnp.where(lies & (target1 == 9 * (source1 - b * n_wind) + shift), 1.0, pick1)
        pick2, pick1 = pick2.astype(BF16), pick1.astype(BF16)
        for part in range(3):
            out2 = out2 + jnp.dot(turned[part][rows], pick2, preferred_element_type=F32)
            out1 = out1 + jnp.dot(split[part][rows], pick1, preferred_element_type=F32)
    c2_ref[...] = out2
    c1_ref[...] = out1
    b1_ref[...] = across[3 * CH + 3 * n_wind : 3 * CH + 3 * n_wind + 1, CH : 2 * CH]
    b2_ref[...] = across[3 * CH + 16 : 3 * CH + 17, :CH]
    for level in range(LEVELS):
        raw = across[3 * CH + 16 : 3 * CH + 25, (level + 1) * CH : (level + 2) * CH]
        mean = jnp.sum(raw, axis=0, keepdims=True) / 9.0
        head_ref[9 * level : 9 * level + 9, :] = CORRECTION * (raw - mean)


def lax_wendroff(courant):
    return (
        0.5 * courant + 0.5 * courant * courant,
        1.0 - courant * courant,
        0.5 * courant * courant - 0.5 * courant,
    )


def tracer_kernel(levels_ref, wind_ref, corr_ref, cot_ref, side_ref, below_ref, above_ref, out_ref, coef_ref):
    count, tile, cols = out_ref.shape
    for level in range(LEVELS):
        px = lax_wendroff(COURANT * wind_ref[2 * level])
        py = lax_wendroff(COURANT * wind_ref[2 * level + 1])
        for a in range(3):
            for b in range(3):
                coef = corr_ref[9 * level + 3 * a + b] + px[a] * py[b]
                coef = turn(turn(coef, -STEPS[b], 1), HALO - STEPS[a], 0)
                coef_ref[level, 3 * a + b] = coef[:tile, :cols]

    channels = below_ref.shape[0] - 3
    groups = count // GROUP
    for group in range(groups):
        sides = sides_of(groups + 1 + group, side_ref, below_ref, above_ref, channels)

        def step(entry, carry):
            spare = count + group * (GROUP // 4) + entry
            spare = rows_of(below_ref[spare], above_ref[spare])
            for part in range(4):
                j = 4 * entry + part
                t = group * GROUP + j
                level = levels_ref[t]
                strip = cot_strip(rows_of(below_ref[t], above_ref[t]), spare, part)
                field = joined(cot_ref[t], sides[0], strip, sides[1], j)
                total = jnp.zeros((tile, cols), F32)
                for b in range(3):
                    moved = turn(field, -STEPS[b], 1)
                    for a in range(3):
                        total = total + coef_ref[level, 3 * a + b] * turn(moved, -STEPS[a], 0)[:tile, :cols]
                out_ref[t] = total.astype(BF16)
            return carry

        lax.fori_loop(0, GROUP // 4, step, 0)


def call(kernel, outs, scratch, operands, spaces=None, flops=2_000_000, vmem=40):
    specs = [pl.BlockSpec(memory_space=(spaces or {}).get(i, pltpu.VMEM)) for i in range(len(operands))]
    whole = pl.BlockSpec(memory_space=pltpu.VMEM)
    return pl.pallas_call(
        kernel,
        out_shape=outs,
        in_specs=specs,
        out_specs=[whole] * len(outs) if isinstance(outs, (list, tuple)) else whole,
        scratch_shapes=scratch,
        compiler_params=pltpu.CompilerParams(vmem_limit_bytes=vmem * 1024 * 1024),
        cost_estimate=pl.CostEstimate(flops=flops, bytes_accessed=2_000_000, transcendentals=0),
    )(*operands)


def ring_pairs(size, wrap):
    up = [(i, (i + 1) % size) for i in range(size if wrap else size - 1)]
    return up, [(j, i) for i, j in up]


def sum_rounds(value, axes, early, late):
    sizes = [lax.axis_size(axis) for axis in axes]
    other = jnp.zeros_like(value)
    if any(size & (size - 1) for size in sizes):
        return lax.psum(value, axes), other, early, late
    rounds = [(axis, 1 << bit) for axis, size in zip(axes, sizes) for bit in range(size.bit_length() - 1)]
    for index, (axis, step) in enumerate(rounds):
        value = value + other
        if index == 1:
            value, early = lax.optimization_barrier((value, early))
        if index == len(rounds) - 1:
            value, late = lax.optimization_barrier((value, late))
        other = lax.ppermute(value, axis, [(i, i ^ step) for i in range(lax.axis_size(axis))])
    return value, other, early, late


def body(tracers, cotangent, winds, levels, conv1, bias1, conv2, bias2, head):
    count, tile, cols = tracers.shape
    n_wind = winds.shape[0]
    width = cols + LANES
    rows = tile + 2 * HALO
    vmem, spec = pltpu.VMEM, jax.ShapeDtypeStruct
    gy, gy_size = lax.axis_index("gy"), lax.axis_size("gy")
    gx, gx_size = lax.axis_index("gx"), lax.axis_size("gx")
    paired = gx_size % 2 == 0
    odd = (gx % 2 if paired else 0 * gx).astype(jnp.int32)
    strip = spec((count + count // 4 + 3 * n_wind, HALO, cols), BF16)
    packed, one, two = call(
        pack_kernel,
        [spec((2 * (count // GROUP) + 2, tile, LANES), BF16), strip, strip],
        [vmem((count, tile, cols), BF16)] * 2
        + [vmem((n_wind, tile, cols), F32), pltpu.SemaphoreType.DMA((3,))],
        (odd[None], tracers, cotangent, winds),
        {0: pltpu.SMEM} | {i: pltpu.HBM for i in range(1, 4)},
        vmem=60,
    )
    spare = ((0, packed.shape[0] // 2), (0, 0), (0, 0))
    one, two = lax.optimization_barrier((jnp.pad(one, spare), jnp.pad(two, spare)))
    up, down = ring_pairs(gy_size, False)
    lane = lax.broadcasted_iota(jnp.int32, (1, 1, LANES), 2) % (2 * HALO)
    if gy_size == 2:
        got = lax.ppermute(packed, "gy", up + down)
        side = jnp.where(jnp.where(gy == 0, lane >= HALO, lane < HALO), got, 0)
    else:
        right = lax.ppermute(packed, "gy", down)
        left = lax.ppermute(packed, "gy", up)
        side = jnp.where(lane >= HALO, right, left)
    side = side.astype(BF16)
    w1, w2, w2b, w1b, head_w, head_t, bias1_col, bias2_col = call(
        prep_kernel,
        [
            spec((2 * CH, 96), BF16),
            spec((2 * CH, 18 * CH), BF16),
            spec((2 * CH, 18 * CH), BF16),
            spec((32, 18 * CH), BF16),
            spec((2 * CH, 2 * CH), BF16),
            spec((2 * CH, 2 * CH), BF16),
            spec((CH, 1), F32),
            spec((CH, 1), F32),
        ],
        [
            vmem(conv1.shape, F32),
            vmem((1, CH), F32),
            vmem(conv2.shape, F32),
            vmem((1, CH), F32),
            vmem(head.shape, F32),
            vmem((2 * CH, 9 * CH), F32),
            vmem((32, 9 * CH), F32),
            vmem((2 * CH, CH), F32),
            vmem((2 * CH, 18 * CH), F32),
            pltpu.SemaphoreType.DMA((5,)),
        ],
        lax.optimization_barrier((conv1, bias1[None], conv2, bias2[None], head, side))[:5],
        {i: pltpu.HBM for i in range(5)},
    )
    half = side.shape[0] // 2
    wide = jnp.concatenate([side[:half], side[half:]], axis=2)
    first_rows, last_rows = wide[:, :HALO], wide[:, tile - HALO :]
    is_odd = odd == 1
    one = lax.dynamic_update_slice(one, jnp.where(is_odd, first_rows, last_rows), (one.shape[0] - half, 0, 0))
    two = lax.dynamic_update_slice(two, jnp.where(is_odd, last_rows, first_rows), (two.shape[0] - half, 0, 0))
    if paired:
        ahead = [(i, i ^ 1) for i in range(gx_size)]
        behind = [(i, (i + 1) % gx_size if i % 2 else (i - 1) % gx_size) for i in range(gx_size)]
        one, two = lax.ppermute(one, "gx", ahead), lax.ppermute(two, "gx", behind)
        below, above = jnp.where(is_odd, two, one), jnp.where(is_odd, one, two)
    else:
        up, down = ring_pairs(gx_size, True)
        above, below = lax.ppermute(one, "gx", up), lax.ppermute(two, "gx", down)
    place = lax.broadcasted_iota(jnp.int32, (1, width), 1)
    has_right, has_left = gy < gy_size - 1, gy > 0
    inside = jnp.where(place < cols, True, jnp.where(place < cols + LANES // 2, has_right, has_left)).astype(F32)

    levels = jnp.clip(levels, 0, LEVELS - 1)
    inner, edge = call(
        inner_kernel,
        [spec((9 * LEVELS, tile, width), F32), spec((2, count, tile, width), F32)],
        [vmem((3, count + 8, tile, width), F32)] * 2,
        (levels, tracers, cotangent, side),
        {0: pltpu.SMEM},
    )
    above, below, w1, w2, inner = lax.optimization_barrier((above, below, w1, w2, inner))
    mine = call(
        border_kernel,
        spec((9 * LEVELS, rows, width), F32),
        [vmem((3, count + 8, 2 * HALO, width), F32)] * 2,
        (levels, inner, edge, side, below, above),
        {0: pltpu.SMEM},
    )
    other = lax.ppermute(mine, "tracer", [(i, i ^ 1) for i in range(lax.axis_size("tracer"))])
    first, second, corr, wind_ext = call(
        forward_kernel,
        [
            spec((CH, (rows - 2) * width), F32),
            spec((CH, (rows - 4) * width), F32),
            spec((9 * LEVELS, rows, width), F32),
            spec((n_wind, rows, width), F32),
        ],
        [vmem((16, rows * width), F32)]
        + [vmem((16, rows * width), BF16)] * 2
        + [vmem((3 * CH, (rows - 2) * width), BF16)] * 2,
        (winds, side, below, above, inside, w1, bias1_col, w2, bias2_col, head_w),
    )
    ring, own = (tile + 4) * width, (tile + 2) * width
    params, delta = call(
        backward_kernel,
        [spec((3 * CH, LANES), F32), spec((CH, own), F32)],
        [vmem((9 * LEVELS, rows, width), F32), vmem((CH, ring), F32)]
        + [vmem((3 * CH, ring), BF16)] * 2
        + [vmem((6 * CH, own), BF16)] * 3
        + [vmem((16, own), F32)],
        (mine, other, wind_ext, inside, first, second, head_t, w2b),
    )
    wind_grad = call(
        wind_kernel,
        spec((n_wind, tile, cols), F32),
        [vmem((3 * CH, own), BF16)] * 2 + [vmem((n_wind, tile, cols), F32)],
        (mine, other, wind_ext, delta, w1b),
    )
    mine, other, wind_grad, corr = sum_rounds(params, ("gy", "gx"), wind_grad, corr)
    tracer_grad = call(
        tracer_kernel,
        spec((count, tile, cols), BF16),
        [vmem((LEVELS, 9, tile, cols), F32)],
        (levels, wind_ext, corr, cotangent, side, below, above),
        {0: pltpu.SMEM},
    )
    conv1_grad, bias1_grad, conv2_grad, bias2_grad, head_grad = call(
        final_kernel,
        [spec(conv1.shape, F32), spec((1, CH), F32), spec(conv2.shape, F32), spec((1, CH), F32), spec(head.shape, F32)],
        [],
        (mine, other),
        flops=200_000,
    )
    return (tracer_grad, wind_grad, conv1_grad, bias1_grad[0], conv2_grad, bias2_grad[0], head_grad)


def solution(mesh):
    return jax.shard_map(
        body,
        mesh=mesh,
        in_specs=(
            P(("member", "tracer"), "gx", "gy"),
            P(("member", "tracer"), "gx", "gy"),
            P("member", "gx", "gy"),
            P(("member", "tracer")),
            P(),
            P(),
            P(),
            P(),
            P(),
        ),
        out_specs=(
            P(("member", "tracer"), "gx", "gy"),
            P("member", "gx", "gy"),
            P("member", None),
            P("member"),
            P("member", None),
            P("member"),
            P("member", None),
        ),
        check_vma=False,
    )
```

```python
import functools

import jax
import jax.numpy as jnp
from jax import lax
from jax.experimental import pallas as pl
from jax.experimental.pallas import tpu as pltpu
from jax.sharding import PartitionSpec as P

LEVELS = 2
CH = 32
COURANT = 0.5
CORRECTION = 0.2
STEPS = (-1, 0, 1)
HALO = 4
LANES = 128
GROUP = LANES // (2 * HALO)
F32 = jnp.float32
BF16 = jnp.bfloat16
NT = (((1,), (1,)), ((), ()))


def halves(value):
    high = value.astype(BF16)
    return high, (value - high.astype(F32)).astype(BF16)


def dot3(weights, high, low):
    rows = weights.shape[0] // 2
    both = jnp.dot(weights, jnp.concatenate([high, low], axis=0), preferred_element_type=F32)
    return both[:rows] + both[rows:]


def dot3_nt(left, right):
    rows, cols = left.shape[0] // 2, right.shape[0] // 2
    out = lax.dot_general(left, right, NT, preferred_element_type=F32)
    return out[:rows, :cols] + out[:rows, cols:] + out[rows:, :cols]


def turn(value, step, axis):
    shift = (-step) % value.shape[axis]
    return pltpu.roll(value, shift, axis) if shift else value


def side_mask():
    lane = lax.broadcasted_iota(jnp.int32, (1, LANES), 1)
    return (lane < HALO) | (lane >= LANES - HALO)


def rows_of(below, above):
    return jnp.concatenate([below.astype(F32), above.astype(F32)], axis=0)


def sides_of(group, side_ref, below_ref, above_ref, channels):
    half = side_ref.shape[0] // 2
    index = channels + group % half
    where = slice(group // half * LANES, (group // half + 1) * LANES)
    return side_ref[group].astype(F32), rows_of(below_ref[index, :, where], above_ref[index, :, where])


def placed(side, j):
    return jnp.where(side_mask(), pltpu.roll(side, LANES - HALO - 2 * HALO * j, 1), 0.0)


def joined(main, side, strip, strip_side, j):
    top = jnp.concatenate([main.astype(F32), placed(side, j)], axis=1)
    return jnp.concatenate([top, jnp.concatenate([strip, placed(strip_side, j)], axis=1)], axis=0)


def cot_strip(strip, spare, part):
    slot = lax.broadcasted_iota(jnp.int32, strip.shape, 0)
    value = jnp.where(slot == 0, turn(strip, 3, 0), jnp.where(slot == 6, turn(strip, -2, 0), 0.0))
    value = jnp.where(slot == 1, spare[part : part + 1], value)
    return jnp.where(slot == 7, spare[HALO + part : HALO + part + 1], value)


def run_copies(sources, targets, sems):
    copies = [pltpu.make_async_copy(a, b, sems.at[i]) for i, (a, b) in enumerate(zip(sources, targets))]
    for copy in copies:
        copy.start()
    for copy in copies:
        copy.wait()


def pack_kernel(odd_ref, tracer_hbm, cot_hbm, wind_hbm, out_ref, one_ref, two_ref, tracer_ref, cot_ref, wind_ref, sems):
    run_copies((tracer_hbm, cot_hbm, wind_hbm), (tracer_ref, cot_ref, wind_ref), sems)
    count, tile, cols = tracer_ref.shape
    n_wind = wind_ref.shape[0]
    lane = lax.broadcasted_iota(jnp.int32, (1, LANES), 1)
    mask = side_mask()
    odd = jnp.full((HALO, cols), odd_ref[0], jnp.int32) == 1

    def lifted(value, j):
        both = jnp.where(lane < HALO, value[:, :LANES], value[:, cols - LANES :])
        return pltpu.roll(jnp.where(mask, both, 0.0), HALO + 2 * HALO * j, 1)

    def put(entry, first, last):
        one_ref[entry] = jnp.where(odd, first, last).astype(BF16)
        two_ref[entry] = jnp.where(odd, last, first).astype(BF16)

    groups = count // GROUP
    for group in range(groups):
        totals = [jnp.zeros(out_ref.shape[1:], F32)] * 2
        for start in range(0, GROUP, 4):
            first, last = [], []
            for part in range(4):
                j = start + part
                t = group * GROUP + j
                tracer, cot = tracer_ref[t].astype(F32), cot_ref[t].astype(F32)
                totals = [totals[0] + lifted(tracer, j), totals[1] + lifted(cot, j)]
                put(
                    t,
                    jnp.concatenate([tracer[:3], cot[:1]], axis=0),
                    jnp.concatenate([cot[tile - 2 : tile - 1], tracer[tile - 3 :]], axis=0),
                )
                first.append(cot[1:2])
                last.append(cot[tile - 1 :])
            put(count + t // 4, jnp.concatenate(first, axis=0), jnp.concatenate(last, axis=0))
        out_ref[group] = totals[0].astype(BF16)
        out_ref[groups + 1 + group] = totals[1].astype(BF16)
    base = count + count // 4
    total = jnp.zeros(out_ref.shape[1:], F32)
    for i in range(n_wind):
        value = wind_ref[i]
        for part in range(3):
            high = value.astype(BF16).astype(F32)
            total = total + lifted(high, part * n_wind + i)
            put(base + part * n_wind + i, high[:HALO], high[tile - HALO :])
            value = value - high
    out_ref[groups] = total.astype(BF16)
    out_ref[2 * groups + 1] = jnp.zeros(out_ref.shape[1:], BF16)


def picker(shape, source_axis, wanted):
    source = lax.broadcasted_iota(jnp.int32, shape, source_axis)
    target = lax.broadcasted_iota(jnp.int32, shape, 1 - source_axis)
    return jnp.where(source == wanted(target), 1.0, 0.0).astype(BF16)


def prep_kernel(
    c1_hbm, b1_hbm, c2_hbm, b2_hbm, head_hbm,
    w1_ref, w2_ref, w2b_ref, w1b_ref, hw_ref, ht_ref, b1_ref, b2_ref,
    c1, b1, c2, b2, head, wide_ref, slim_ref, tall_ref, pair_ref, sems,
):
    run_copies((c1_hbm, b1_hbm, c2_hbm, b2_hbm, head_hbm), (c1, b1, c2, b2, head), sems)
    n_wind = c1.shape[1] // 9

    def wanted2(target):
        return 9 * (target & (CH - 1)) + (target >> 5)

    def wanted1(target):
        a, r = target >> 4, target & 15
        b = (r >= n_wind).astype(jnp.int32) + (r >= 2 * n_wind).astype(jnp.int32)
        return jnp.where(r < 3 * n_wind, 9 * (r - n_wind * b) + 3 * a + b, -1)

    def doubled(target, value):
        rows, depth = value.shape[0] // 2, value.shape[1]
        pair_ref[: 2 * rows, :depth] = value
        pair_ref[:rows, depth : 2 * depth] = value[:rows]
        pair_ref[rows : 2 * rows, depth : 2 * depth] = jnp.zeros((rows, depth), F32)
        target[...] = pair_ref[: 2 * rows, : 2 * depth].astype(BF16)

    both2 = jnp.concatenate(halves(c2[...]), axis=0)
    size = both2.shape[1]
    doubled(w2_ref, jnp.dot(both2, picker((size, size), 0, wanted2), preferred_element_type=F32))
    turned = lax.dot_general(picker((size, size), 1, wanted2), both2, NT, preferred_element_type=F32)
    both1 = jnp.concatenate(halves(c1[...]), axis=0)
    size = both1.shape[1]
    doubled(w1_ref, jnp.dot(both1, picker((size, 48), 0, wanted1), preferred_element_type=F32))
    turned1 = lax.dot_general(picker((48, size), 1, wanted1), both1, NT, preferred_element_type=F32)
    slim_ref[...] = jnp.zeros(slim_ref.shape, F32)
    for q in range(9):
        where = slice(q * CH, (q + 1) * CH)
        start = q // 3 * 16 + q % 3 * n_wind
        for part in range(2):
            lanes = slice(part * CH, (part + 1) * CH)
            wide_ref[lanes, where] = turned[where, lanes]
            slim_ref[16 * part : 16 * part + n_wind, where] = turned1[start : start + n_wind, lanes]
    doubled(w2b_ref, wide_ref[...])
    doubled(w1b_ref, slim_ref[...])
    tall_ref[...] = jnp.zeros(tall_ref.shape, F32)
    for level in range(LEVELS):
        rows = slice(9 * level, 9 * level + 9)
        part = head[rows, :]
        part = CORRECTION * (part - jnp.sum(part, axis=0, keepdims=True) / 9.0)
        high = part.astype(BF16).astype(F32)
        tall_ref[rows, :] = high
        tall_ref[CH + 9 * level : CH + 9 * level + 9, :] = part - high
    tall = tall_ref[...].astype(BF16)
    doubled(hw_ref, tall_ref[...])
    unit = picker((CH, CH), 0, lambda target: target)
    across = lax.dot_general(unit, tall, NT, preferred_element_type=F32)
    doubled(ht_ref, jnp.concatenate([across[:, :CH], across[:, CH:]], axis=0))
    for source, target in ((b1, b1_ref), (b2, b2_ref)):
        target[...] = jnp.sum(unit.astype(F32) * source[...], axis=1, keepdims=True)


def gap_zeroed(refs, lower):
    for ref in refs:
        for gap in (0, 1, 2, 5, 6, 7):
            for step in range(3):
                ref[step, lower + gap] = jnp.zeros(ref.shape[2:], F32)


def slot_sums(moved_ref, held_ref, lower, count, store):
    slots, rows, width = moved_ref.shape[1:]
    for level in range(LEVELS):
        trips = lax.shift_right_logical((lower if level == 0 else count - lower) + 3, 2)
        for start in range(0, width, LANES):
            lanes = slice(start, start + LANES)

            def step(trip, sums):
                for part in range(4):
                    slot = 4 * trip + part
                    slot = slot if level == 0 else slots - 1 - slot
                    near = [moved_ref[b, slot, :, lanes] for b in range(3)]
                    far = [held_ref[a, slot, :, lanes] for a in range(3)]
                    sums = tuple(sums[k] + far[k // 3] * near[k % 3] for k in range(9))
                return sums

            sums = lax.fori_loop(0, trips, step, (jnp.zeros((rows, LANES), F32),) * 9)
            for k in range(9):
                store(level, k, lanes, sums[k])


def slot_of(level, t, lower, slots):
    low = level == 0
    return jnp.where(low, lower, slots - 1 - t + lower), jnp.where(low, lower + 1, lower)


def inner_kernel(levels_ref, tracer_ref, cot_ref, side_ref, out_ref, edge_ref, moved_ref, held_ref):
    count, tile, cols = tracer_ref.shape
    slots, _, width = moved_ref.shape[1:]
    half = side_ref.shape[0] // 2
    row = lax.broadcasted_iota(jnp.int32, (tile, width), 0)
    lower = jnp.int32(0)
    for group in range(count // GROUP):
        near, far = side_ref[group].astype(F32), side_ref[half + group].astype(F32)

        def fill(entry, lower):
            for part in range(4):
                j = 4 * entry + part
                t = group * GROUP + j
                slot, lower = slot_of(levels_ref[t], t, lower, slots)
                field = jnp.concatenate([tracer_ref[t].astype(F32), placed(near, j)], axis=1)
                cot = jnp.concatenate([cot_ref[t].astype(F32), placed(far, j)], axis=1)
                for b in range(3):
                    moved_ref[b, slot] = turn(field, STEPS[b], 1)
                later, sooner = turn(cot, 1, 0), turn(cot, -1, 0)
                held_ref[0, slot] = jnp.where(row == tile - 1, 0.0, later)
                held_ref[1, slot] = cot
                held_ref[2, slot] = jnp.where(row == 0, 0.0, sooner)
                edge_ref[0, t] = turn(field, HALO, 0)
                edge_ref[1, t] = jnp.where(row == 0, sooner, later)
            return lower

        lower = lax.fori_loop(0, GROUP // 4, fill, lower)
    gap_zeroed((moved_ref, held_ref), lower)

    def store(level, k, lanes, total):
        out_ref[9 * level + k, :, lanes] = turn(total, STEPS[k // 3], 0)

    slot_sums(moved_ref, held_ref, lower, count, store)


def border_kernel(levels_ref, inner_ref, edge_ref, side_ref, below_ref, above_ref, out_ref, moved_ref, held_ref):
    count = levels_ref.shape[0]
    slots, rows, width = moved_ref.shape[1:]
    tile = inner_ref.shape[1]
    channels = below_ref.shape[0] - side_ref.shape[0] // 2
    groups = count // GROUP
    row = lax.broadcasted_iota(jnp.int32, (rows, width), 0)
    lower = jnp.int32(0)
    for group in range(groups):
        near = sides_of(group, side_ref, below_ref, above_ref, channels)[1]
        far = sides_of(groups + 1 + group, side_ref, below_ref, above_ref, channels)[1]

        def fill(entry, lower):
            spare = count + group * (GROUP // 4) + entry
            spare = rows_of(below_ref[spare], above_ref[spare])
            for part in range(4):
                j = 4 * entry + part
                t = group * GROUP + j
                slot, lower = slot_of(levels_ref[t], t, lower, slots)
                strip = rows_of(below_ref[t], above_ref[t])
                field = jnp.concatenate([strip, placed(near, j)], axis=1)
                field = jnp.where((row == 3) | (row == 4), edge_ref[0, t], field)
                cot = jnp.concatenate([cot_strip(strip, spare, part), placed(far, j)], axis=1)
                edge = edge_ref[1, t]
                for b in range(3):
                    moved_ref[b, slot] = turn(field, STEPS[b], 1)
                held_ref[0, slot] = jnp.where(row == 7, edge, jnp.where(row == 3, turn(cot, -3, 0), turn(cot, 1, 0)))
                held_ref[1, slot] = cot
                held_ref[2, slot] = jnp.where(row == 0, edge, jnp.where(row == 4, turn(cot, 3, 0), turn(cot, -1, 0)))
            return lower

        lower = lax.fori_loop(0, GROUP // 4, fill, lower)
    gap_zeroed((moved_ref, held_ref), lower)
    place = row[:, :LANES]

    def store(level, k, lanes, total):
        index, step = 9 * level + k, STEPS[k // 3]
        inner = inner_ref[index, :, lanes]
        if step:
            last = 7 if step == 1 else 0
            shifted = turn(total, step, 0)
            inner = inner + jnp.where(place == last, shifted, 0.0)
            total = jnp.where(place == last, turn(total, 5 if step == 1 else 3, 0), shifted)
        out_ref[index, :tile, lanes] = inner
        out_ref[index, tile:, lanes] = total

    slot_sums(moved_ref, held_ref, lower, count, store)


def put_moved(high_ref, low_ref, row, value, sign):
    width = value.shape[1]
    for ref, part in zip((high_ref, low_ref), halves(value)):
        for b in range(3):
            ref[b * CH : (b + 1) * CH, row * width : (row + 1) * width] = turn(part, sign * STEPS[b], 1)


def convolved(weights, high_ref, low_ref, starts, width):
    def rows(ref):
        return jnp.concatenate([ref[:, start * width : (start + 2) * width] for start in starts], axis=0)

    return dot3(weights, rows(high_ref), rows(low_ref))


def put_winds(wind_ref, stack_ref, pairs, keep):
    count = wind_ref.shape[0]
    for row, place in pairs:
        value = wind_ref[:, row, :]
        for b in range(3):
            moved = turn(value, STEPS[b], 1)[:, :keep]
            stack_ref[b * count : (b + 1) * count, place * keep : (place + 1) * keep] = moved


def network_rows(weights, bias, high_ref, low_ref, row, width):
    starts = (row, row + 1, row + 2)
    return jnp.tanh(convolved(weights, high_ref, low_ref, starts, width) + bias)


def inner_forward_kernel(
    own_ref, side_ref, inside_ref, w1_ref, b1_ref, w2_ref, b2_ref,
    first_ref, high_ref, low_ref, second_ref,
    wind_ref, stack_ref, wind_high, wind_low,
):
    count, tile, width = wind_ref.shape
    cols = own_ref.shape[2]
    side = side_ref[side_ref.shape[0] // 2 - 1].astype(F32)
    for i in range(count):
        wind_ref[i, :, :cols] = own_ref[i]
        wind_ref[i, :, cols:] = sum(placed(side, part * count + i) for part in range(3))
    stack_ref[...] = jnp.zeros(stack_ref.shape, F32)
    put_winds(wind_ref, stack_ref, [(row, row) for row in range(tile)], width)
    wind_high[...], wind_low[...] = halves(stack_ref[...])
    bias1, bias2 = b1_ref[...], b2_ref[...]
    inside = jnp.concatenate([inside_ref[...]] * 2, axis=1)
    for row in range(0, tile - 2, 2):
        value = network_rows(w1_ref[...], bias1, wind_high, wind_low, row, width) * inside
        first_ref[:, row * width : (row + 2) * width] = value
        for part in range(2):
            put_moved(high_ref, low_ref, row + part, value[:, part * width : (part + 1) * width], 1)
    for row in range(0, tile - 4, 2):
        second_ref[:, row * width : (row + 2) * width] = network_rows(w2_ref[...], bias2, high_ref, low_ref, row, width)


def forward_kernel(
    own_ref, side_ref, below_ref, above_ref, inside_ref, w1_ref, b1_ref, w2_ref, b2_ref, head_ref,
    inner_first, inner_high, inner_low, inner_second,
    first_ref, second_ref, corr_ref, wind_ref,
    stack_ref, wind_high, wind_low, high_ref, low_ref,
):
    count, rows, width = wind_ref.shape
    tile, cols = own_ref.shape[1:]
    channels = below_ref.shape[0] - 3
    side, side_rows = sides_of(side_ref.shape[0] // 2 - 1, side_ref, below_ref, above_ref, channels)
    for i in range(count):
        wind_ref[i, HALO : HALO + tile, :cols] = own_ref[i]
        wide = [jnp.zeros((tile, LANES), F32), jnp.zeros((tile, LANES), F32)]
        strip = jnp.zeros((2 * HALO, cols), F32)
        for part in range(3):
            j = part * count + i
            wide[0] = wide[0] + placed(side, j)
            wide[1] = wide[1] + placed(side_rows, j)
            index = channels - 3 * count + j
            strip = strip + rows_of(below_ref[index], above_ref[index])
        wind_ref[i, HALO : HALO + tile, cols:] = wide[0]
        for value, where in ((strip, slice(0, cols)), (wide[1], slice(cols, width))):
            wind_ref[i, HALO + tile :, where] = value[:HALO]
            wind_ref[i, :HALO, where] = value[HALO:]
    stack_ref[...] = jnp.zeros(stack_ref.shape, F32)
    edge = HALO + 2
    put_winds(wind_ref, stack_ref, [(row, row) for row in range(rows) if row < edge or row >= rows - edge], width)
    wind_high[...], wind_low[...] = halves(stack_ref[...])
    bias1, bias2 = b1_ref[...], b2_ref[...]
    inside = jnp.concatenate([inside_ref[...]] * 2, axis=1)
    first_ref[:, HALO * width : (rows - 2 - HALO) * width] = inner_first[...]
    for row in list(range(2)) + list(range(tile - 4, tile - 2)):
        source = slice(row * width, (row + 1) * width)
        target = slice((HALO + row) * width, (HALO + row + 1) * width)
        high_ref[:, target] = inner_high[:, source]
        low_ref[:, target] = inner_low[:, source]
    for row in range(0, rows - 2, 2):
        if HALO <= row < rows - 2 - HALO:
            continue
        value = network_rows(w1_ref[...], bias1, wind_high, wind_low, row, width) * inside
        first_ref[:, row * width : (row + 2) * width] = value
        for part in range(2):
            put_moved(high_ref, low_ref, row + part, value[:, part * width : (part + 1) * width], 1)
    for row in range(0, rows - 4, 2):
        if HALO <= row < rows - 4 - HALO:
            value = inner_second[:, (row - HALO) * width : (row - HALO + 2) * width]
        else:
            value = network_rows(w2_ref[...], bias2, high_ref, low_ref, row, width)
        second_ref[:, row * width : (row + 2) * width] = value
        high, low = halves(value)
        corr = dot3(head_ref[...], high, low)
        for part in range(2):
            corr_ref[:, 2 + row + part, :] = corr[: corr_ref.shape[0], part * width : (part + 1) * width]


def backward_kernel(
    mine_ref, other_ref, wind_ref, inside_ref, first_ref, second_ref, headt_ref, w2b_ref,
    par_ref, d1_ref,
    sum_ref, g_ref, d2_high, d2_low, own2_ref, act_ref, own1_ref, wind_stack,
):
    cells = g_ref.shape[1]
    width = wind_ref.shape[2]
    cols = width - LANES
    ring = cells // width
    tile = ring - 4
    sum_ref[...] = mine_ref[...] + other_ref[...]
    wrap = sum_ref.shape[1]
    nine = sum_ref.shape[0]
    g_ref[...] = jnp.zeros(g_ref.shape, F32)
    for row in range(ring):
        g_ref[:nine, row * width : (row + 1) * width] = sum_ref[:, (row - 2) % wrap, :]
    inside = inside_ref[...]
    for ref in (own2_ref, own1_ref):
        ref[...] = jnp.zeros(ref.shape, BF16)
    wind_stack[...] = jnp.zeros(wind_stack.shape, F32)
    put_winds(wind_ref, wind_stack, [(row + 3, row) for row in range(tile + 2)], cols)
    wind_stack[12:13, :] = jnp.ones((1, wind_stack.shape[1]), F32)
    bias2 = jnp.zeros((CH, cols), F32)

    def put_own(ref, x, value):
        for half, part in enumerate(halves(value[:, :cols])):
            for a in range(3):
                start = (3 * half + a) * CH
                ref[start : start + CH, (x + a) * cols : (x + a + 1) * cols] = part

    for row in range(0, ring, 2):
        where = slice(row * width, (row + 2) * width)
        high, low = halves(g_ref[:, where])
        hidden = dot3(headt_ref[...], high, low)
        second = second_ref[:, where]
        delta = hidden * (1.0 - second * second)
        for part in range(2):
            value = delta[:, part * width : (part + 1) * width]
            put_moved(d2_high, d2_low, row + part, value, -1)
            x = row + part - 2
            if 0 <= x < tile:
                put_own(own2_ref, x, value)
                bias2 = bias2 + value[:, :cols]
    for row in range(tile + 2):
        for half, part in enumerate(halves(first_ref[:, (row + 2) * width : (row + 3) * width])):
            for b in range(3):
                start = (3 * half + b) * CH
                act_ref[start : start + CH, row * cols : (row + 1) * cols] = turn(part, STEPS[b], 1)[:, :cols]
    par_ref[...] = jnp.zeros(par_ref.shape, F32)
    par_ref[:, : 3 * CH] = dot3_nt(act_ref[...], own2_ref[...])
    par_ref[:CH, 3 * CH + 16 : 3 * CH + 17] = jnp.sum(bias2, axis=1, keepdims=True)
    inside2 = jnp.concatenate([inside] * 2, axis=1)
    for row in range(0, tile + 2, 2):
        total = convolved(w2b_ref[...], d2_high, d2_low, (row + 2, row + 1, row), width)
        first = first_ref[:, (row + 2) * width : (row + 4) * width]
        delta = total * (1.0 - first * first) * inside2
        d1_ref[:, row * width : (row + 2) * width] = delta
        for part in range(2):
            value = delta[:, part * width : (part + 1) * width]
            x = row + part - 1
            if 0 <= x < tile:
                put_own(own1_ref, x, value)
    par_ref[:, 3 * CH : 3 * CH + 16] = dot3_nt(own1_ref[...], jnp.concatenate(halves(wind_stack[...]), axis=0))

    def own_cells(ref):
        rows = [ref[:, row * width : row * width + cols] for row in range(2, 2 + tile)]
        return jnp.concatenate(halves(jnp.concatenate(rows, axis=1)), axis=0)

    raw = dot3_nt(own_cells(second_ref), own_cells(g_ref))
    for level in range(LEVELS):
        rows = slice((level + 1) * CH, (level + 2) * CH)
        par_ref[rows, 3 * CH + 16 : 3 * CH + 25] = raw[:, 9 * level : 9 * level + 9]


def wind_kernel(mine_ref, other_ref, wind_ref, d1_ref, w1b_ref, wgrad_ref, d1_high, d1_low, net_ref):
    tile, cols = wgrad_ref.shape[1:]
    width = wind_ref.shape[2]
    for row in range(tile + 2):
        put_moved(d1_high, d1_low, row, d1_ref[:, row * width : (row + 1) * width], -1)
    for row in range(0, tile, 2):
        total = convolved(w1b_ref[...], d1_high, d1_low, (row + 2, row + 1, row), width)
        for part in range(2):
            net_ref[:, row + part, :] = total[:4, part * width : part * width + cols]
    for level in range(LEVELS):
        cx = COURANT * wind_ref[2 * level, HALO : HALO + tile, :cols]
        cy = COURANT * wind_ref[2 * level + 1, HALO : HALO + tile, :cols]
        px, py = lax_wendroff(cx), lax_wendroff(cy)
        dx, dy = (0.5 + cx, -2.0 * cx, cx - 0.5), (0.5 + cy, -2.0 * cy, cy - 0.5)
        gx_sum = jnp.zeros((tile, cols), F32)
        gy_sum = jnp.zeros((tile, cols), F32)
        for a in range(3):
            for b in range(3):
                k = 9 * level + 3 * a + b
                grad = mine_ref[k, :tile, :cols] + other_ref[k, :tile, :cols]
                gx_sum = gx_sum + grad * (dx[a] * py[b])
                gy_sum = gy_sum + grad * (px[a] * dy[b])
        wgrad_ref[2 * level] = COURANT * gx_sum + net_ref[2 * level]
        wgrad_ref[2 * level + 1] = COURANT * gy_sum + net_ref[2 * level + 1]


def final_kernel(mine_ref, other_ref, c1_ref, b1_ref, c2_ref, b2_ref, head_ref):
    total = mine_ref[...] + other_ref[...]
    across = jnp.concatenate([total, jnp.zeros((LANES - total.shape[0], LANES), F32)], axis=0).T
    size2, size1 = c2_ref.shape[1], c1_ref.shape[1]
    n_wind = size1 // 9
    split, rest = [], total
    turned, rest_t = [], across[: 3 * CH, : 3 * CH]
    for _ in range(3):
        high = rest.astype(BF16)
        split.append(high)
        rest = rest - high.astype(F32)
        high = rest_t.astype(BF16)
        turned.append(high)
        rest_t = rest_t - high.astype(F32)
    source = lax.broadcasted_iota(jnp.int32, (3 * CH, size2), 0)
    target = lax.broadcasted_iota(jnp.int32, (3 * CH, size2), 1)
    source1 = lax.broadcasted_iota(jnp.int32, (LANES, size1), 0) - 3 * CH
    target1 = lax.broadcasted_iota(jnp.int32, (LANES, size1), 1)
    out2 = jnp.zeros((CH, size2), F32)
    out1 = jnp.zeros((CH, size1), F32)
    for a in range(3):
        rows = slice(a * CH, (a + 1) * CH)
        pick2 = jnp.zeros((3 * CH, size2), F32)
        pick1 = jnp.zeros((LANES, size1), F32)
        for b in range(3):
            shift = 3 * a + b
            lies = (source >= b * CH) & (source < (b + 1) * CH)
            pick2 = jnp.where(lies & (target == 9 * (source - b * CH) + shift), 1.0, pick2)
            lies = (source1 >= b * n_wind) & (source1 < (b + 1) * n_wind)
            pick1 = jnp.where(lies & (target1 == 9 * (source1 - b * n_wind) + shift), 1.0, pick1)
        pick2, pick1 = pick2.astype(BF16), pick1.astype(BF16)
        for part in range(3):
            out2 = out2 + jnp.dot(turned[part][rows], pick2, preferred_element_type=F32)
            out1 = out1 + jnp.dot(split[part][rows], pick1, preferred_element_type=F32)
    c2_ref[...] = out2
    c1_ref[...] = out1
    b1_ref[...] = across[3 * CH + 3 * n_wind : 3 * CH + 3 * n_wind + 1, CH : 2 * CH]
    b2_ref[...] = across[3 * CH + 16 : 3 * CH + 17, :CH]
    for level in range(LEVELS):
        raw = across[3 * CH + 16 : 3 * CH + 25, (level + 1) * CH : (level + 2) * CH]
        mean = jnp.sum(raw, axis=0, keepdims=True) / 9.0
        head_ref[9 * level : 9 * level + 9, :] = CORRECTION * (raw - mean)


def lax_wendroff(courant):
    return (
        0.5 * courant + 0.5 * courant * courant,
        1.0 - courant * courant,
        0.5 * courant * courant - 0.5 * courant,
    )


def tracer_kernel(levels_ref, wind_ref, corr_ref, cot_ref, side_ref, below_ref, above_ref, out_ref, coef_ref):
    count, tile, cols = out_ref.shape
    for level in range(LEVELS):
        px = lax_wendroff(COURANT * wind_ref[2 * level])
        py = lax_wendroff(COURANT * wind_ref[2 * level + 1])
        for a in range(3):
            for b in range(3):
                coef = corr_ref[9 * level + 3 * a + b] + px[a] * py[b]
                coef = turn(turn(coef, -STEPS[b], 1), HALO - STEPS[a], 0)
                coef_ref[level, 3 * a + b] = coef[:tile, :cols]

    channels = below_ref.shape[0] - 3
    groups = count // GROUP
    for group in range(groups):
        sides = sides_of(groups + 1 + group, side_ref, below_ref, above_ref, channels)

        def step(entry, carry):
            spare = count + group * (GROUP // 4) + entry
            spare = rows_of(below_ref[spare], above_ref[spare])
            for part in range(4):
                j = 4 * entry + part
                t = group * GROUP + j
                level = levels_ref[t]
                strip = cot_strip(rows_of(below_ref[t], above_ref[t]), spare, part)
                field = joined(cot_ref[t], sides[0], strip, sides[1], j)
                total = jnp.zeros((tile, cols), F32)
                for b in range(3):
                    moved = turn(field, -STEPS[b], 1)
                    for a in range(3):
                        total = total + coef_ref[level, 3 * a + b] * turn(moved, -STEPS[a], 0)[:tile, :cols]
                out_ref[t] = total.astype(BF16)
            return carry

        lax.fori_loop(0, GROUP // 4, step, 0)


def call(kernel, outs, scratch, operands, spaces=None, flops=2_000_000, vmem=40):
    specs = [pl.BlockSpec(memory_space=(spaces or {}).get(i, pltpu.VMEM)) for i in range(len(operands))]
    whole = pl.BlockSpec(memory_space=pltpu.VMEM)
    return pl.pallas_call(
        kernel,
        out_shape=outs,
        in_specs=specs,
        out_specs=[whole] * len(outs) if isinstance(outs, (list, tuple)) else whole,
        scratch_shapes=scratch,
        compiler_params=pltpu.CompilerParams(vmem_limit_bytes=vmem * 1024 * 1024),
        cost_estimate=pl.CostEstimate(flops=flops, bytes_accessed=2_000_000, transcendentals=0),
    )(*operands)


def ring_pairs(size, wrap):
    up = [(i, (i + 1) % size) for i in range(size if wrap else size - 1)]
    return up, [(j, i) for i, j in up]


def sum_rounds(value, axes, early, late):
    sizes = [lax.axis_size(axis) for axis in axes]
    other = jnp.zeros_like(value)
    if any(size & (size - 1) for size in sizes):
        return lax.psum(value, axes), other, early, late
    rounds = [(axis, 1 << bit) for axis, size in zip(axes, sizes) for bit in range(size.bit_length() - 1)]
    for index, (axis, step) in enumerate(rounds):
        value = value + other
        if index == 1:
            value, early = lax.optimization_barrier((value, early))
        if index == len(rounds) - 1:
            value, late = lax.optimization_barrier((value, late))
        other = lax.ppermute(value, axis, [(i, i ^ step) for i in range(lax.axis_size(axis))])
    return value, other, early, late


def body(tracers, cotangent, winds, levels, conv1, bias1, conv2, bias2, head):
    count, tile, cols = tracers.shape
    n_wind = winds.shape[0]
    width = cols + LANES
    rows = tile + 2 * HALO
    vmem, spec = pltpu.VMEM, jax.ShapeDtypeStruct
    gy, gy_size = lax.axis_index("gy"), lax.axis_size("gy")
    gx, gx_size = lax.axis_index("gx"), lax.axis_size("gx")
    paired = gx_size % 2 == 0
    odd = (gx % 2 if paired else 0 * gx).astype(jnp.int32)
    strip = spec((count + count // 4 + 3 * n_wind, HALO, cols), BF16)
    packed, one, two = call(
        pack_kernel,
        [spec((2 * (count // GROUP) + 2, tile, LANES), BF16), strip, strip],
        [vmem((count, tile, cols), BF16)] * 2
        + [vmem((n_wind, tile, cols), F32), pltpu.SemaphoreType.DMA((3,))],
        (odd[None], tracers, cotangent, winds),
        {0: pltpu.SMEM} | {i: pltpu.HBM for i in range(1, 4)},
        vmem=60,
    )
    spare = ((0, packed.shape[0] // 2), (0, 0), (0, 0))
    one, two = lax.optimization_barrier((jnp.pad(one, spare), jnp.pad(two, spare)))
    up, down = ring_pairs(gy_size, False)
    lane = lax.broadcasted_iota(jnp.int32, (1, 1, LANES), 2) % (2 * HALO)
    if gy_size == 2:
        got = lax.ppermute(packed, "gy", up + down)
        side = jnp.where(jnp.where(gy == 0, lane >= HALO, lane < HALO), got, 0)
    else:
        right = lax.ppermute(packed, "gy", down)
        left = lax.ppermute(packed, "gy", up)
        side = jnp.where(lane >= HALO, right, left)
    side = side.astype(BF16)
    w1, w2, w2b, w1b, head_w, head_t, bias1_col, bias2_col = call(
        prep_kernel,
        [
            spec((2 * CH, 96), BF16),
            spec((2 * CH, 18 * CH), BF16),
            spec((2 * CH, 18 * CH), BF16),
            spec((32, 18 * CH), BF16),
            spec((2 * CH, 2 * CH), BF16),
            spec((2 * CH, 2 * CH), BF16),
            spec((CH, 1), F32),
            spec((CH, 1), F32),
        ],
        [
            vmem(conv1.shape, F32),
            vmem((1, CH), F32),
            vmem(conv2.shape, F32),
            vmem((1, CH), F32),
            vmem(head.shape, F32),
            vmem((2 * CH, 9 * CH), F32),
            vmem((32, 9 * CH), F32),
            vmem((2 * CH, CH), F32),
            vmem((2 * CH, 18 * CH), F32),
            pltpu.SemaphoreType.DMA((5,)),
        ],
        lax.optimization_barrier((conv1, bias1[None], conv2, bias2[None], head, side))[:5],
        {i: pltpu.HBM for i in range(5)},
    )
    half = side.shape[0] // 2
    wide = jnp.concatenate([side[:half], side[half:]], axis=2)
    first_rows, last_rows = wide[:, :HALO], wide[:, tile - HALO :]
    is_odd = odd == 1
    one = lax.dynamic_update_slice(one, jnp.where(is_odd, first_rows, last_rows), (one.shape[0] - half, 0, 0))
    two = lax.dynamic_update_slice(two, jnp.where(is_odd, last_rows, first_rows), (two.shape[0] - half, 0, 0))
    if paired:
        ahead = [(i, i ^ 1) for i in range(gx_size)]
        behind = [(i, (i + 1) % gx_size if i % 2 else (i - 1) % gx_size) for i in range(gx_size)]
        one, two = lax.ppermute(one, "gx", ahead), lax.ppermute(two, "gx", behind)
        below, above = jnp.where(is_odd, two, one), jnp.where(is_odd, one, two)
    else:
        up, down = ring_pairs(gx_size, True)
        above, below = lax.ppermute(one, "gx", up), lax.ppermute(two, "gx", down)
    place = lax.broadcasted_iota(jnp.int32, (1, width), 1)
    has_right, has_left = gy < gy_size - 1, gy > 0
    inside = jnp.where(place < cols, True, jnp.where(place < cols + LANES // 2, has_right, has_left)).astype(F32)

    levels = jnp.clip(levels, 0, LEVELS - 1)
    inner, edge = call(
        inner_kernel,
        [spec((9 * LEVELS, tile, width), F32), spec((2, count, tile, width), F32)],
        [vmem((3, count + 8, tile, width), F32)] * 2,
        (levels, tracers, cotangent, side),
        {0: pltpu.SMEM},
    )
    inner_net = call(
        inner_forward_kernel,
        [
            spec((CH, (tile - 2) * width), F32),
            spec((3 * CH, (tile - 2) * width), BF16),
            spec((3 * CH, (tile - 2) * width), BF16),
            spec((CH, (tile - 4) * width), F32),
        ],
        [vmem((n_wind, tile, width), F32), vmem((16, tile * width), F32)] + [vmem((16, tile * width), BF16)] * 2,
        (winds, side, inside, w1, bias1_col, w2, bias2_col),
    )
    above, below, inner_net, inner = lax.optimization_barrier((above, below, inner_net, inner))
    mine = call(
        border_kernel,
        spec((9 * LEVELS, rows, width), F32),
        [vmem((3, count + 8, 2 * HALO, width), F32)] * 2,
        (levels, inner, edge, side, below, above),
        {0: pltpu.SMEM},
    )
    other = lax.ppermute(mine, "tracer", [(i, i ^ 1) for i in range(lax.axis_size("tracer"))])
    first, second, corr, wind_ext = call(
        forward_kernel,
        [
            spec((CH, (rows - 2) * width), F32),
            spec((CH, (rows - 4) * width), F32),
            spec((9 * LEVELS, rows, width), F32),
            spec((n_wind, rows, width), F32),
        ],
        [vmem((16, rows * width), F32)]
        + [vmem((16, rows * width), BF16)] * 2
        + [vmem((3 * CH, (rows - 2) * width), BF16)] * 2,
        (winds, side, below, above, inside, w1, bias1_col, w2, bias2_col, head_w) + tuple(inner_net),
    )
    ring, own = (tile + 4) * width, (tile + 2) * width
    params, delta = call(
        backward_kernel,
        [spec((3 * CH, LANES), F32), spec((CH, own), F32)],
        [vmem((9 * LEVELS, rows, width), F32), vmem((CH, ring), F32)]
        + [vmem((3 * CH, ring), BF16)] * 2
        + [vmem((6 * CH, (tile + 2) * cols), BF16)] * 3
        + [vmem((16, (tile + 2) * cols), F32)],
        (mine, other, wind_ext, inside, first, second, head_t, w2b),
    )
    wind_grad = call(
        wind_kernel,
        spec((n_wind, tile, cols), F32),
        [vmem((3 * CH, own), BF16)] * 2 + [vmem((n_wind, tile, cols), F32)],
        (mine, other, wind_ext, delta, w1b),
    )
    mine, other, wind_grad, corr = sum_rounds(params, ("gy", "gx"), wind_grad, corr)
    tracer_grad = call(
        tracer_kernel,
        spec((count, tile, cols), BF16),
        [vmem((LEVELS, 9, tile, cols), F32)],
        (levels, wind_ext, corr, cotangent, side, below, above),
        {0: pltpu.SMEM},
    )
    conv1_grad, bias1_grad, conv2_grad, bias2_grad, head_grad = call(
        final_kernel,
        [spec(conv1.shape, F32), spec((1, CH), F32), spec(conv2.shape, F32), spec((1, CH), F32), spec(head.shape, F32)],
        [],
        (mine, other),
        flops=200_000,
    )
    return (tracer_grad, wind_grad, conv1_grad, bias1_grad[0], conv2_grad, bias2_grad[0], head_grad)


def solution(mesh):
    return jax.shard_map(
        body,
        mesh=mesh,
        in_specs=(
            P(("member", "tracer"), "gx", "gy"),
            P(("member", "tracer"), "gx", "gy"),
            P("member", "gx", "gy"),
            P(("member", "tracer")),
            P(),
            P(),
            P(),
            P(),
            P(),
        ),
        out_specs=(
            P(("member", "tracer"), "gx", "gy"),
            P("member", "gx", "gy"),
            P("member", None),
            P("member"),
            P("member", None),
            P("member"),
            P("member", None),
        ),
        check_vma=False,
    )
```

```python
import functools

import jax
import jax.numpy as jnp
from jax import lax
from jax.experimental import pallas as pl
from jax.experimental.pallas import tpu as pltpu
from jax.sharding import PartitionSpec as P

LEVELS = 2
CH = 32
COURANT = 0.5
CORRECTION = 0.2
STEPS = (-1, 0, 1)
HALO = 4
LANES = 128
GROUP = LANES // (2 * HALO)
F32 = jnp.float32
BF16 = jnp.bfloat16
NT = (((1,), (1,)), ((), ()))


def halves(value):
    high = value.astype(BF16)
    return high, (value - high.astype(F32)).astype(BF16)


def dot3(weights, high, low):
    rows = weights.shape[0] // 2
    both = jnp.dot(weights, jnp.concatenate([high, low], axis=0), preferred_element_type=F32)
    return both[:rows] + both[rows:]


def dot3_nt(left, right):
    rows, cols = left.shape[0] // 2, right.shape[0] // 2
    out = lax.dot_general(left, right, NT, preferred_element_type=F32)
    return out[:rows, :cols] + out[:rows, cols:] + out[rows:, :cols]


def turn(value, step, axis):
    shift = (-step) % value.shape[axis]
    return pltpu.roll(value, shift, axis) if shift else value


def side_mask():
    lane = lax.broadcasted_iota(jnp.int32, (1, LANES), 1)
    return (lane < HALO) | (lane >= LANES - HALO)


def rows_of(below, above):
    return jnp.concatenate([below.astype(F32), above.astype(F32)], axis=0)


def sides_of(group, side_ref, below_ref, above_ref, channels):
    half = side_ref.shape[0] // 2
    index = channels + group % half
    where = slice(group // half * LANES, (group // half + 1) * LANES)
    return side_ref[group].astype(F32), rows_of(below_ref[index, :, where], above_ref[index, :, where])


def placed(side, j):
    return jnp.where(side_mask(), pltpu.roll(side, LANES - HALO - 2 * HALO * j, 1), 0.0)


def joined(main, side, strip, strip_side, j):
    top = jnp.concatenate([main.astype(F32), placed(side, j)], axis=1)
    return jnp.concatenate([top, jnp.concatenate([strip, placed(strip_side, j)], axis=1)], axis=0)


def cot_strip(strip, spare, part):
    slot = lax.broadcasted_iota(jnp.int32, strip.shape, 0)
    value = jnp.where(slot == 0, turn(strip, 3, 0), jnp.where(slot == 7, turn(strip, -3, 0), 0.0))
    value = jnp.where(slot == 1, spare[part : part + 1], value)
    return jnp.where(slot == 6, spare[HALO + part : HALO + part + 1], value)


def in_slots(row, *pairs):
    value = jnp.zeros(row.shape, F32)
    for slot, part in pairs:
        value = jnp.where(row == slot, part, value)
    return value


def run_copies(sources, targets, sems):
    copies = [pltpu.make_async_copy(a, b, sems.at[i]) for i, (a, b) in enumerate(zip(sources, targets))]
    for copy in copies:
        copy.start()
    for copy in copies:
        copy.wait()


def pack_kernel(odd_ref, tracer_hbm, cot_hbm, wind_hbm, out_ref, one_ref, two_ref, tracer_ref, cot_ref, wind_ref, sems):
    run_copies((tracer_hbm, cot_hbm, wind_hbm), (tracer_ref, cot_ref, wind_ref), sems)
    count, tile, cols = tracer_ref.shape
    n_wind = wind_ref.shape[0]
    lane = lax.broadcasted_iota(jnp.int32, (1, LANES), 1)
    mask = side_mask()
    odd = jnp.full((HALO, cols), odd_ref[0], jnp.int32) == 1

    def lifted(value, j):
        both = jnp.where(lane < HALO, value[:, :LANES], value[:, cols - LANES :])
        return pltpu.roll(jnp.where(mask, both, 0.0), HALO + 2 * HALO * j, 1)

    def put(entry, first, last):
        one_ref[entry] = jnp.where(odd, first, last).astype(BF16)
        two_ref[entry] = jnp.where(odd, last, first).astype(BF16)

    groups = count // GROUP
    for group in range(groups):
        totals = [jnp.zeros(out_ref.shape[1:], F32)] * 2
        for start in range(0, GROUP, 4):
            first, last = [], []
            for part in range(4):
                j = start + part
                t = group * GROUP + j
                tracer, cot = tracer_ref[t].astype(F32), cot_ref[t].astype(F32)
                totals = [totals[0] + lifted(tracer, j), totals[1] + lifted(cot, j)]
                put(
                    t,
                    jnp.concatenate([tracer[:3], cot[:1]], axis=0),
                    jnp.concatenate([cot[tile - 1 :], tracer[tile - 3 :]], axis=0),
                )
                first.append(cot[1:2])
                last.append(cot[tile - 2 : tile - 1])
            put(count + t // 4, jnp.concatenate(first, axis=0), jnp.concatenate(last, axis=0))
        out_ref[group] = totals[0].astype(BF16)
        out_ref[groups + 1 + group] = totals[1].astype(BF16)
    base = count + count // 4
    total = jnp.zeros(out_ref.shape[1:], F32)
    for i in range(n_wind):
        value = wind_ref[i]
        for part in range(3):
            high = value.astype(BF16).astype(F32)
            total = total + lifted(high, part * n_wind + i)
            put(base + part * n_wind + i, high[:HALO], high[tile - HALO :])
            value = value - high
    out_ref[groups] = total.astype(BF16)
    out_ref[2 * groups + 1] = jnp.zeros(out_ref.shape[1:], BF16)


def picker(shape, source_axis, wanted):
    source = lax.broadcasted_iota(jnp.int32, shape, source_axis)
    target = lax.broadcasted_iota(jnp.int32, shape, 1 - source_axis)
    return jnp.where(source == wanted(target), 1.0, 0.0).astype(BF16)


def prep_kernel(
    c1_hbm, b1_hbm, c2_hbm, b2_hbm, head_hbm,
    w1_ref, w2_ref, w2b_ref, w1b_ref, hw_ref, ht_ref, b1_ref, b2_ref,
    c1, b1, c2, b2, head, wide_ref, slim_ref, tall_ref, pair_ref, sems,
):
    run_copies((c1_hbm, b1_hbm, c2_hbm, b2_hbm, head_hbm), (c1, b1, c2, b2, head), sems)
    n_wind = c1.shape[1] // 9

    def wanted2(target):
        return 9 * (target & (CH - 1)) + (target >> 5)

    def wanted1(target):
        a, r = target >> 4, target & 15
        b = (r >= n_wind).astype(jnp.int32) + (r >= 2 * n_wind).astype(jnp.int32)
        return jnp.where(r < 3 * n_wind, 9 * (r - n_wind * b) + 3 * a + b, -1)

    def doubled(target, value):
        rows, depth = value.shape[0] // 2, value.shape[1]
        pair_ref[: 2 * rows, :depth] = value
        pair_ref[:rows, depth : 2 * depth] = value[:rows]
        pair_ref[rows : 2 * rows, depth : 2 * depth] = jnp.zeros((rows, depth), F32)
        target[...] = pair_ref[: 2 * rows, : 2 * depth].astype(BF16)

    both2 = jnp.concatenate(halves(c2[...]), axis=0)
    size = both2.shape[1]
    doubled(w2_ref, jnp.dot(both2, picker((size, size), 0, wanted2), preferred_element_type=F32))
    turned = lax.dot_general(picker((size, size), 1, wanted2), both2, NT, preferred_element_type=F32)
    both1 = jnp.concatenate(halves(c1[...]), axis=0)
    size = both1.shape[1]
    doubled(w1_ref, jnp.dot(both1, picker((size, 48), 0, wanted1), preferred_element_type=F32))
    turned1 = lax.dot_general(picker((48, size), 1, wanted1), both1, NT, preferred_element_type=F32)
    slim_ref[...] = jnp.zeros(slim_ref.shape, F32)
    for q in range(9):
        where = slice(q * CH, (q + 1) * CH)
        start = q // 3 * 16 + q % 3 * n_wind
        for part in range(2):
            lanes = slice(part * CH, (part + 1) * CH)
            wide_ref[lanes, where] = turned[where, lanes]
            slim_ref[16 * part : 16 * part + n_wind, where] = turned1[start : start + n_wind, lanes]
    doubled(w2b_ref, wide_ref[...])
    doubled(w1b_ref, slim_ref[...])
    tall_ref[...] = jnp.zeros(tall_ref.shape, F32)
    for level in range(LEVELS):
        rows = slice(9 * level, 9 * level + 9)
        part = head[rows, :]
        part = CORRECTION * (part - jnp.sum(part, axis=0, keepdims=True) / 9.0)
        high = part.astype(BF16).astype(F32)
        tall_ref[rows, :] = high
        tall_ref[CH + 9 * level : CH + 9 * level + 9, :] = part - high
    tall = tall_ref[...].astype(BF16)
    doubled(hw_ref, tall_ref[...])
    unit = picker((CH, CH), 0, lambda target: target)
    across = lax.dot_general(unit, tall, NT, preferred_element_type=F32)
    doubled(ht_ref, jnp.concatenate([across[:, :CH], across[:, CH:]], axis=0))
    for source, target in ((b1, b1_ref), (b2, b2_ref)):
        target[...] = jnp.sum(unit.astype(F32) * source[...], axis=1, keepdims=True)


def gap_zeroed(refs, lower):
    for ref in refs:
        for gap in (0, 1, 2, 5, 6, 7):
            for step in range(3):
                ref[step, lower + gap] = jnp.zeros(ref.shape[2:], F32)


def slot_sums(moved_ref, held_ref, lower, count, store):
    slots, rows, width = moved_ref.shape[1:]
    for level in range(LEVELS):
        trips = lax.shift_right_logical((lower if level == 0 else count - lower) + 3, 2)
        for start in range(0, width, LANES):
            lanes = slice(start, start + LANES)

            def step(trip, sums):
                for part in range(4):
                    slot = 4 * trip + part
                    slot = slot if level == 0 else slots - 1 - slot
                    near = [moved_ref[b, slot, :, lanes] for b in range(3)]
                    far = [held_ref[a, slot, :, lanes] for a in range(3)]
                    sums = tuple(sums[k] + far[k // 3] * near[k % 3] for k in range(9))
                return sums

            sums = lax.fori_loop(0, trips, step, (jnp.zeros((rows, LANES), F32),) * 9)
            for k in range(9):
                store(level, k, lanes, sums[k])


def slot_of(level, t, lower, slots):
    low = level == 0
    return jnp.where(low, lower, slots - 1 - t + lower), jnp.where(low, lower + 1, lower)


def inner_kernel(levels_ref, tracer_ref, cot_ref, side_ref, out_ref, edge_ref, moved_ref, held_ref):
    count, tile, cols = tracer_ref.shape
    slots, _, width = moved_ref.shape[1:]
    half = side_ref.shape[0] // 2
    row = lax.broadcasted_iota(jnp.int32, (tile, width), 0)
    lower = jnp.int32(0)
    for group in range(count // GROUP):
        near, far = side_ref[group].astype(F32), side_ref[half + group].astype(F32)

        def fill(entry, lower):
            for part in range(4):
                j = 4 * entry + part
                t = group * GROUP + j
                slot, lower = slot_of(levels_ref[t], t, lower, slots)
                field = jnp.concatenate([tracer_ref[t].astype(F32), placed(near, j)], axis=1)
                cot = jnp.concatenate([cot_ref[t].astype(F32), placed(far, j)], axis=1)
                for b in range(3):
                    moved_ref[b, slot] = turn(field, STEPS[b], 1)
                later, sooner = turn(cot, 1, 0), turn(cot, -1, 0)
                held_ref[0, slot] = jnp.where(row == tile - 1, 0.0, later)
                held_ref[1, slot] = cot
                held_ref[2, slot] = jnp.where(row == 0, 0.0, sooner)
                edge_ref[0, t] = turn(field, HALO, 0)
                edge_ref[1, t] = jnp.where(row == 0, sooner, later)
            return lower

        lower = lax.fori_loop(0, GROUP // 4, fill, lower)
    gap_zeroed((moved_ref, held_ref), lower)

    def store(level, k, lanes, total):
        out_ref[9 * level + k, :, lanes] = turn(total, STEPS[k // 3], 0)

    slot_sums(moved_ref, held_ref, lower, count, store)


def border_kernel(levels_ref, edge_ref, side_ref, below_ref, above_ref, out_ref, moved_ref, held_ref):
    count = levels_ref.shape[0]
    slots, rows, width = moved_ref.shape[1:]
    channels = below_ref.shape[0] - side_ref.shape[0] // 2
    groups = count // GROUP
    row = lax.broadcasted_iota(jnp.int32, (rows, width), 0)
    lower = jnp.int32(0)
    for group in range(groups):
        near = sides_of(group, side_ref, below_ref, above_ref, channels)[1]
        far = sides_of(groups + 1 + group, side_ref, below_ref, above_ref, channels)[1]

        def fill(entry, lower):
            spare = count + group * (GROUP // 4) + entry
            spare = rows_of(below_ref[spare], above_ref[spare])
            for part in range(4):
                j = 4 * entry + part
                t = group * GROUP + j
                slot, lower = slot_of(levels_ref[t], t, lower, slots)
                strip = rows_of(below_ref[t], above_ref[t])
                field = jnp.concatenate([strip, placed(near, j)], axis=1)
                field = jnp.where((row == 3) | (row == 4), edge_ref[0, t], field)
                edge = edge_ref[1, t]
                for b in range(3):
                    moved_ref[b, slot] = turn(field, STEPS[b], 1)
                next0, next1 = strip[3:4], spare[part : part + 1]
                back1, back2 = strip[4:5], spare[HALO + part : HALO + part + 1]
                where = row[:, : strip.shape[1]]
                later = in_slots(where, (0, next1), (3, next0), (5, back2), (6, back1))
                cot = in_slots(where, (0, next0), (1, next1), (6, back2), (7, back1))
                sooner = in_slots(where, (1, next0), (2, next1), (4, back1), (7, back2))
                tail, place = placed(far, j), row[:, :LANES]
                tail_later = jnp.where(place == 3, turn(tail, -3, 0), turn(tail, 1, 0))
                tail_sooner = jnp.where(place == 4, turn(tail, 3, 0), turn(tail, -1, 0))
                later = jnp.concatenate([later, tail_later], axis=1)
                sooner = jnp.concatenate([sooner, tail_sooner], axis=1)
                held_ref[0, slot] = jnp.where(row == 7, edge, later)
                held_ref[1, slot] = jnp.concatenate([cot, tail], axis=1)
                held_ref[2, slot] = jnp.where(row == 0, edge, sooner)
            return lower

        lower = lax.fori_loop(0, GROUP // 4, fill, lower)
    gap_zeroed((moved_ref, held_ref), lower)

    def store(level, k, lanes, total):
        out_ref[9 * level + k, :, lanes] = total

    slot_sums(moved_ref, held_ref, lower, count, store)


def merged(inner, border, k):
    step = STEPS[k // 3]
    if not step:
        return inner, border
    place = lax.broadcasted_iota(jnp.int32, border.shape, 0)
    last = place == (7 if step == 1 else 0)
    shifted = turn(border, step, 0)
    strip = jnp.where(last, turn(border, 5 if step == 1 else 3, 0), shifted)
    return inner + jnp.where(last, shifted, 0.0), strip


def put_moved(high_ref, low_ref, row, value, sign):
    width = value.shape[1]
    for ref, part in zip((high_ref, low_ref), halves(value)):
        for b in range(3):
            ref[b * CH : (b + 1) * CH, row * width : (row + 1) * width] = turn(part, sign * STEPS[b], 1)


def convolved(weights, high_ref, low_ref, starts, width):
    def rows(ref):
        return jnp.concatenate([ref[:, start * width : (start + 2) * width] for start in starts], axis=0)

    return dot3(weights, rows(high_ref), rows(low_ref))


def put_winds(wind_ref, stack_ref, pairs, keep):
    count = wind_ref.shape[0]
    for row, place in pairs:
        value = wind_ref[:, row, :]
        for b in range(3):
            moved = turn(value, STEPS[b], 1)[:, :keep]
            stack_ref[b * count : (b + 1) * count, place * keep : (place + 1) * keep] = moved


def network_rows(weights, bias, high_ref, low_ref, row, width):
    starts = (row, row + 1, row + 2)
    return jnp.tanh(convolved(weights, high_ref, low_ref, starts, width) + bias)


def inner_forward_kernel(
    own_ref, side_ref, inside_ref, w1_ref, b1_ref, w2_ref, b2_ref,
    first_ref, high_ref, low_ref, second_ref,
    wind_ref, stack_ref, wind_high, wind_low,
):
    count, tile, width = wind_ref.shape
    cols = own_ref.shape[2]
    side = side_ref[side_ref.shape[0] // 2 - 1].astype(F32)
    for i in range(count):
        wind_ref[i, :, :cols] = own_ref[i]
        wind_ref[i, :, cols:] = sum(placed(side, part * count + i) for part in range(3))
    stack_ref[...] = jnp.zeros(stack_ref.shape, F32)
    put_winds(wind_ref, stack_ref, [(row, row) for row in range(tile)], width)
    wind_high[...], wind_low[...] = halves(stack_ref[...])
    bias1, bias2 = b1_ref[...], b2_ref[...]
    inside = jnp.concatenate([inside_ref[...]] * 2, axis=1)
    for row in range(0, tile - 2, 2):
        value = network_rows(w1_ref[...], bias1, wind_high, wind_low, row, width) * inside
        first_ref[:, row * width : (row + 2) * width] = value
        for part in range(2):
            put_moved(high_ref, low_ref, row + part, value[:, part * width : (part + 1) * width], 1)
    for row in range(0, tile - 4, 2):
        second_ref[:, row * width : (row + 2) * width] = network_rows(w2_ref[...], bias2, high_ref, low_ref, row, width)


def forward_kernel(
    own_ref, side_ref, below_ref, above_ref, inside_ref, w1_ref, b1_ref, w2_ref, b2_ref,
    inner_first, inner_high, inner_low, inner_second,
    first_ref, second_ref, wind_ref,
    stack_ref, wind_high, wind_low, high_ref, low_ref,
):
    count, rows, width = wind_ref.shape
    tile, cols = own_ref.shape[1:]
    channels = below_ref.shape[0] - 3
    side, side_rows = sides_of(side_ref.shape[0] // 2 - 1, side_ref, below_ref, above_ref, channels)
    for i in range(count):
        wind_ref[i, HALO : HALO + tile, :cols] = own_ref[i]
        wide = [jnp.zeros((tile, LANES), F32), jnp.zeros((tile, LANES), F32)]
        strip = jnp.zeros((2 * HALO, cols), F32)
        for part in range(3):
            j = part * count + i
            wide[0] = wide[0] + placed(side, j)
            wide[1] = wide[1] + placed(side_rows, j)
            index = channels - 3 * count + j
            strip = strip + rows_of(below_ref[index], above_ref[index])
        wind_ref[i, HALO : HALO + tile, cols:] = wide[0]
        for value, where in ((strip, slice(0, cols)), (wide[1], slice(cols, width))):
            wind_ref[i, HALO + tile :, where] = value[:HALO]
            wind_ref[i, :HALO, where] = value[HALO:]
    stack_ref[...] = jnp.zeros(stack_ref.shape, F32)
    edge = HALO + 2
    put_winds(wind_ref, stack_ref, [(row, row) for row in range(rows) if row < edge or row >= rows - edge], width)
    wind_high[...], wind_low[...] = halves(stack_ref[...])
    bias1, bias2 = b1_ref[...], b2_ref[...]
    inside = jnp.concatenate([inside_ref[...]] * 2, axis=1)
    first_ref[:, HALO * width : (rows - 2 - HALO) * width] = inner_first[...]
    for row in list(range(2)) + list(range(tile - 4, tile - 2)):
        source = slice(row * width, (row + 1) * width)
        target = slice((HALO + row) * width, (HALO + row + 1) * width)
        high_ref[:, target] = inner_high[:, source]
        low_ref[:, target] = inner_low[:, source]
    for row in range(0, rows - 2, 2):
        if HALO <= row < rows - 2 - HALO:
            continue
        value = network_rows(w1_ref[...], bias1, wind_high, wind_low, row, width) * inside
        first_ref[:, row * width : (row + 2) * width] = value
        for part in range(2):
            put_moved(high_ref, low_ref, row + part, value[:, part * width : (part + 1) * width], 1)
    for row in range(0, rows - 4, 2):
        if HALO <= row < rows - 4 - HALO:
            value = inner_second[:, (row - HALO) * width : (row - HALO + 2) * width]
        else:
            value = network_rows(w2_ref[...], bias2, high_ref, low_ref, row, width)
        second_ref[:, row * width : (row + 2) * width] = value


def backward_kernel(
    inner_ref, inner_other, border_ref, border_other, wind_ref, inside_ref, first_ref, second_ref, headt_ref, w2b_ref,
    par_ref, d1_ref,
    sum_ref, g_ref, d2_high, d2_low, own2_ref, act_ref, own1_ref, wind_stack,
):
    cells = g_ref.shape[1]
    width = wind_ref.shape[2]
    cols = width - LANES
    ring = cells // width
    tile = ring - 4
    wrap = sum_ref.shape[1]
    nine = sum_ref.shape[0]
    for index in range(nine):
        inner, border = inner_ref[index] + inner_other[index], border_ref[index] + border_other[index]
        sum_ref[index, :tile], sum_ref[index, tile:] = merged(inner, border, index % 9)
    g_ref[...] = jnp.zeros(g_ref.shape, F32)
    for row in range(ring):
        g_ref[:nine, row * width : (row + 1) * width] = sum_ref[:, (row - 2) % wrap, :]
    inside = inside_ref[...]
    for ref in (own2_ref, own1_ref):
        ref[...] = jnp.zeros(ref.shape, BF16)
    wind_stack[...] = jnp.zeros(wind_stack.shape, F32)
    put_winds(wind_ref, wind_stack, [(row + 3, row) for row in range(tile + 2)], cols)
    wind_stack[12:13, :] = jnp.ones((1, wind_stack.shape[1]), F32)
    bias2 = jnp.zeros((CH, cols), F32)

    def put_own(ref, x, value):
        for half, part in enumerate(halves(value[:, :cols])):
            for a in range(3):
                start = (3 * half + a) * CH
                ref[start : start + CH, (x + a) * cols : (x + a + 1) * cols] = part

    for row in range(0, ring, 2):
        where = slice(row * width, (row + 2) * width)
        high, low = halves(g_ref[:, where])
        hidden = dot3(headt_ref[...], high, low)
        second = second_ref[:, where]
        delta = hidden * (1.0 - second * second)
        for part in range(2):
            value = delta[:, part * width : (part + 1) * width]
            put_moved(d2_high, d2_low, row + part, value, -1)
            x = row + part - 2
            if 0 <= x < tile:
                put_own(own2_ref, x, value)
                bias2 = bias2 + value[:, :cols]
    for row in range(tile + 2):
        for half, part in enumerate(halves(first_ref[:, (row + 2) * width : (row + 3) * width])):
            for b in range(3):
                start = (3 * half + b) * CH
                act_ref[start : start + CH, row * cols : (row + 1) * cols] = turn(part, STEPS[b], 1)[:, :cols]
    par_ref[...] = jnp.zeros(par_ref.shape, F32)
    par_ref[:, : 3 * CH] = dot3_nt(act_ref[...], own2_ref[...])
    par_ref[:CH, 3 * CH + 16 : 3 * CH + 17] = jnp.sum(bias2, axis=1, keepdims=True)
    inside2 = jnp.concatenate([inside] * 2, axis=1)
    for row in range(0, tile + 2, 2):
        total = convolved(w2b_ref[...], d2_high, d2_low, (row + 2, row + 1, row), width)
        first = first_ref[:, (row + 2) * width : (row + 4) * width]
        delta = total * (1.0 - first * first) * inside2
        d1_ref[:, row * width : (row + 2) * width] = delta
        for part in range(2):
            value = delta[:, part * width : (part + 1) * width]
            x = row + part - 1
            if 0 <= x < tile:
                put_own(own1_ref, x, value)
    par_ref[:, 3 * CH : 3 * CH + 16] = dot3_nt(own1_ref[...], jnp.concatenate(halves(wind_stack[...]), axis=0))

    def own_cells(ref):
        rows = [ref[:, row * width : row * width + cols] for row in range(2, 2 + tile)]
        return jnp.concatenate(halves(jnp.concatenate(rows, axis=1)), axis=0)

    raw = dot3_nt(own_cells(second_ref), own_cells(g_ref))
    for level in range(LEVELS):
        rows = slice((level + 1) * CH, (level + 2) * CH)
        par_ref[rows, 3 * CH + 16 : 3 * CH + 25] = raw[:, 9 * level : 9 * level + 9]


def wind_kernel(inner_ref, inner_other, border_ref, border_other, wind_ref, d1_ref, w1b_ref, wgrad_ref, d1_high, d1_low, net_ref):
    tile, cols = wgrad_ref.shape[1:]
    width = wind_ref.shape[2]
    for row in range(tile + 2):
        put_moved(d1_high, d1_low, row, d1_ref[:, row * width : (row + 1) * width], -1)
    for row in range(0, tile, 2):
        total = convolved(w1b_ref[...], d1_high, d1_low, (row + 2, row + 1, row), width)
        for part in range(2):
            net_ref[:, row + part, :] = total[:4, part * width : part * width + cols]
    for level in range(LEVELS):
        cx = COURANT * wind_ref[2 * level, HALO : HALO + tile, :cols]
        cy = COURANT * wind_ref[2 * level + 1, HALO : HALO + tile, :cols]
        px, py = lax_wendroff(cx), lax_wendroff(cy)
        dx, dy = (0.5 + cx, -2.0 * cx, cx - 0.5), (0.5 + cy, -2.0 * cy, cy - 0.5)
        gx_sum = jnp.zeros((tile, cols), F32)
        gy_sum = jnp.zeros((tile, cols), F32)
        for a in range(3):
            for b in range(3):
                k = 9 * level + 3 * a + b
                inner = inner_ref[k, :, :cols] + inner_other[k, :, :cols]
                border = border_ref[k, :, :cols] + border_other[k, :, :cols]
                grad = merged(inner, border, k % 9)[0]
                gx_sum = gx_sum + grad * (dx[a] * py[b])
                gy_sum = gy_sum + grad * (px[a] * dy[b])
        wgrad_ref[2 * level] = COURANT * gx_sum + net_ref[2 * level]
        wgrad_ref[2 * level + 1] = COURANT * gy_sum + net_ref[2 * level + 1]


def final_kernel(mine_ref, other_ref, c1_ref, b1_ref, c2_ref, b2_ref, head_ref):
    total = mine_ref[...] + other_ref[...]
    across = jnp.concatenate([total, jnp.zeros((LANES - total.shape[0], LANES), F32)], axis=0).T
    size2, size1 = c2_ref.shape[1], c1_ref.shape[1]
    n_wind = size1 // 9
    split, rest = [], total
    turned, rest_t = [], across[: 3 * CH, : 3 * CH]
    for _ in range(3):
        high = rest.astype(BF16)
        split.append(high)
        rest = rest - high.astype(F32)
        high = rest_t.astype(BF16)
        turned.append(high)
        rest_t = rest_t - high.astype(F32)
    source = lax.broadcasted_iota(jnp.int32, (3 * CH, size2), 0)
    target = lax.broadcasted_iota(jnp.int32, (3 * CH, size2), 1)
    source1 = lax.broadcasted_iota(jnp.int32, (LANES, size1), 0) - 3 * CH
    target1 = lax.broadcasted_iota(jnp.int32, (LANES, size1), 1)
    out2 = jnp.zeros((CH, size2), F32)
    out1 = jnp.zeros((CH, size1), F32)
    for a in range(3):
        rows = slice(a * CH, (a + 1) * CH)
        pick2 = jnp.zeros((3 * CH, size2), F32)
        pick1 = jnp.zeros((LANES, size1), F32)
        for b in range(3):
            shift = 3 * a + b
            lies = (source >= b * CH) & (source < (b + 1) * CH)
            pick2 = jnp.where(lies & (target == 9 * (source - b * CH) + shift), 1.0, pick2)
            lies = (source1 >= b * n_wind) & (source1 < (b + 1) * n_wind)
            pick1 = jnp.where(lies & (target1 == 9 * (source1 - b * n_wind) + shift), 1.0, pick1)
        pick2, pick1 = pick2.astype(BF16), pick1.astype(BF16)
        for part in range(3):
            out2 = out2 + jnp.dot(turned[part][rows], pick2, preferred_element_type=F32)
            out1 = out1 + jnp.dot(split[part][rows], pick1, preferred_element_type=F32)
    c2_ref[...] = out2
    c1_ref[...] = out1
    b1_ref[...] = across[3 * CH + 3 * n_wind : 3 * CH + 3 * n_wind + 1, CH : 2 * CH]
    b2_ref[...] = across[3 * CH + 16 : 3 * CH + 17, :CH]
    for level in range(LEVELS):
        raw = across[3 * CH + 16 : 3 * CH + 25, (level + 1) * CH : (level + 2) * CH]
        mean = jnp.sum(raw, axis=0, keepdims=True) / 9.0
        head_ref[9 * level : 9 * level + 9, :] = CORRECTION * (raw - mean)


def lax_wendroff(courant):
    return (
        0.5 * courant + 0.5 * courant * courant,
        1.0 - courant * courant,
        0.5 * courant * courant - 0.5 * courant,
    )


def tracer_kernel(levels_ref, wind_ref, second_ref, head_ref, cot_ref, side_ref, below_ref, above_ref, out_ref, coef_ref, corr_ref):
    count, tile, cols = out_ref.shape
    width = wind_ref.shape[2]
    for row in range(0, tile + 4, 2):
        high, low = halves(second_ref[:, row * width : (row + 2) * width])
        corr = dot3(head_ref[...], high, low)
        for part in range(2):
            corr_ref[:, 2 + row + part, :] = corr[: corr_ref.shape[0], part * width : (part + 1) * width]
    for level in range(LEVELS):
        px = lax_wendroff(COURANT * wind_ref[2 * level])
        py = lax_wendroff(COURANT * wind_ref[2 * level + 1])
        for a in range(3):
            for b in range(3):
                coef = corr_ref[9 * level + 3 * a + b] + px[a] * py[b]
                coef = turn(turn(coef, -STEPS[b], 1), HALO - STEPS[a], 0)
                coef_ref[level, 3 * a + b] = coef[:tile, :cols]

    channels = below_ref.shape[0] - 3
    groups = count // GROUP
    for group in range(groups):
        sides = sides_of(groups + 1 + group, side_ref, below_ref, above_ref, channels)

        def step(entry, carry):
            spare = count + group * (GROUP // 4) + entry
            spare = rows_of(below_ref[spare], above_ref[spare])
            for part in range(4):
                j = 4 * entry + part
                t = group * GROUP + j
                level = levels_ref[t]
                strip = cot_strip(rows_of(below_ref[t], above_ref[t]), spare, part)
                field = joined(cot_ref[t], sides[0], strip, sides[1], j)
                total = jnp.zeros((tile, cols), F32)
                for b in range(3):
                    moved = turn(field, -STEPS[b], 1)
                    for a in range(3):
                        total = total + coef_ref[level, 3 * a + b] * turn(moved, -STEPS[a], 0)[:tile, :cols]
                out_ref[t] = total.astype(BF16)
            return carry

        lax.fori_loop(0, GROUP // 4, step, 0)


def call(kernel, outs, scratch, operands, spaces=None, flops=2_000_000, vmem=40):
    specs = [pl.BlockSpec(memory_space=(spaces or {}).get(i, pltpu.VMEM)) for i in range(len(operands))]
    whole = pl.BlockSpec(memory_space=pltpu.VMEM)
    return pl.pallas_call(
        kernel,
        out_shape=outs,
        in_specs=specs,
        out_specs=[whole] * len(outs) if isinstance(outs, (list, tuple)) else whole,
        scratch_shapes=scratch,
        compiler_params=pltpu.CompilerParams(vmem_limit_bytes=vmem * 1024 * 1024),
        cost_estimate=pl.CostEstimate(flops=flops, bytes_accessed=2_000_000, transcendentals=0),
    )(*operands)


def ring_pairs(size, wrap):
    up = [(i, (i + 1) % size) for i in range(size if wrap else size - 1)]
    return up, [(j, i) for i, j in up]


def sum_rounds(value, axes, early, late):
    sizes = [lax.axis_size(axis) for axis in axes]
    other = jnp.zeros_like(value)
    if any(size & (size - 1) for size in sizes):
        return lax.psum(value, axes), other, early, late
    rounds = [(axis, 1 << bit) for axis, size in zip(axes, sizes) for bit in range(size.bit_length() - 1)]
    for index, (axis, step) in enumerate(rounds):
        value = value + other
        if index == 1:
            value, early = lax.optimization_barrier((value, early))
        if index == len(rounds) - 1:
            value, late = lax.optimization_barrier((value, late))
        other = lax.ppermute(value, axis, [(i, i ^ step) for i in range(lax.axis_size(axis))])
    return value, other, early, late


def body(tracers, cotangent, winds, levels, conv1, bias1, conv2, bias2, head):
    count, tile, cols = tracers.shape
    n_wind = winds.shape[0]
    width = cols + LANES
    rows = tile + 2 * HALO
    vmem, spec = pltpu.VMEM, jax.ShapeDtypeStruct
    gy, gy_size = lax.axis_index("gy"), lax.axis_size("gy")
    gx, gx_size = lax.axis_index("gx"), lax.axis_size("gx")
    paired = gx_size % 2 == 0
    odd = (gx % 2 if paired else 0 * gx).astype(jnp.int32)
    strip = spec((count + count // 4 + 3 * n_wind, HALO, cols), BF16)
    packed, one, two = call(
        pack_kernel,
        [spec((2 * (count // GROUP) + 2, tile, LANES), BF16), strip, strip],
        [vmem((count, tile, cols), BF16)] * 2
        + [vmem((n_wind, tile, cols), F32), pltpu.SemaphoreType.DMA((3,))],
        (odd[None], tracers, cotangent, winds),
        {0: pltpu.SMEM} | {i: pltpu.HBM for i in range(1, 4)},
        vmem=60,
    )
    spare = ((0, packed.shape[0] // 2), (0, 0), (0, 0))
    one, two = lax.optimization_barrier((jnp.pad(one, spare), jnp.pad(two, spare)))
    up, down = ring_pairs(gy_size, False)
    lane = lax.broadcasted_iota(jnp.int32, (1, 1, LANES), 2) % (2 * HALO)
    if gy_size == 2:
        got = lax.ppermute(packed, "gy", up + down)
        side = jnp.where(jnp.where(gy == 0, lane >= HALO, lane < HALO), got, 0)
    else:
        right = lax.ppermute(packed, "gy", down)
        left = lax.ppermute(packed, "gy", up)
        side = jnp.where(lane >= HALO, right, left)
    side = side.astype(BF16)
    w1, w2, w2b, w1b, head_w, head_t, bias1_col, bias2_col = call(
        prep_kernel,
        [
            spec((2 * CH, 96), BF16),
            spec((2 * CH, 18 * CH), BF16),
            spec((2 * CH, 18 * CH), BF16),
            spec((32, 18 * CH), BF16),
            spec((2 * CH, 2 * CH), BF16),
            spec((2 * CH, 2 * CH), BF16),
            spec((CH, 1), F32),
            spec((CH, 1), F32),
        ],
        [
            vmem(conv1.shape, F32),
            vmem((1, CH), F32),
            vmem(conv2.shape, F32),
            vmem((1, CH), F32),
            vmem(head.shape, F32),
            vmem((2 * CH, 9 * CH), F32),
            vmem((32, 9 * CH), F32),
            vmem((2 * CH, CH), F32),
            vmem((2 * CH, 18 * CH), F32),
            pltpu.SemaphoreType.DMA((5,)),
        ],
        lax.optimization_barrier((conv1, bias1[None], conv2, bias2[None], head, side))[:5],
        {i: pltpu.HBM for i in range(5)},
    )
    half = side.shape[0] // 2
    wide = jnp.concatenate([side[:half], side[half:]], axis=2)
    first_rows, last_rows = wide[:, :HALO], wide[:, tile - HALO :]
    is_odd = odd == 1
    one = lax.dynamic_update_slice(one, jnp.where(is_odd, first_rows, last_rows), (one.shape[0] - half, 0, 0))
    two = lax.dynamic_update_slice(two, jnp.where(is_odd, last_rows, first_rows), (two.shape[0] - half, 0, 0))
    if paired:
        ahead = [(i, i ^ 1) for i in range(gx_size)]
        behind = [(i, (i + 1) % gx_size if i % 2 else (i - 1) % gx_size) for i in range(gx_size)]
        one, two = lax.ppermute(one, "gx", ahead), lax.ppermute(two, "gx", behind)
        below, above = jnp.where(is_odd, two, one), jnp.where(is_odd, one, two)
    else:
        up, down = ring_pairs(gx_size, True)
        above, below = lax.ppermute(one, "gx", up), lax.ppermute(two, "gx", down)
    place = lax.broadcasted_iota(jnp.int32, (1, width), 1)
    has_right, has_left = gy < gy_size - 1, gy > 0
    inside = jnp.where(place < cols, True, jnp.where(place < cols + LANES // 2, has_right, has_left)).astype(F32)

    levels = jnp.clip(levels, 0, LEVELS - 1)
    inner, edge = call(
        inner_kernel,
        [spec((9 * LEVELS, tile, width), F32), spec((2, count, tile, width), F32)],
        [vmem((3, count + 8, tile, width), F32)] * 2,
        (levels, tracers, cotangent, side),
        {0: pltpu.SMEM},
    )
    inner_net = call(
        inner_forward_kernel,
        [
            spec((CH, (tile - 2) * width), F32),
            spec((3 * CH, (tile - 2) * width), BF16),
            spec((3 * CH, (tile - 2) * width), BF16),
            spec((CH, (tile - 4) * width), F32),
        ],
        [vmem((n_wind, tile, width), F32), vmem((16, tile * width), F32)] + [vmem((16, tile * width), BF16)] * 2,
        (winds, side, inside, w1, bias1_col, w2, bias2_col),
    )
    cores = [(i, i ^ 1) for i in range(lax.axis_size("tracer"))]
    inner_other = lax.ppermute(inner, "tracer", cores)
    above, below, inner_net, inner, inner_other = lax.optimization_barrier((above, below, inner_net, inner, inner_other))
    border = call(
        border_kernel,
        spec((9 * LEVELS, 2 * HALO, width), F32),
        [vmem((3, count + 8, 2 * HALO, width), F32)] * 2,
        (levels, edge, side, below, above),
        {0: pltpu.SMEM},
    )
    totals = (inner, inner_other, border, lax.ppermute(border, "tracer", cores))
    first, second, wind_ext = call(
        forward_kernel,
        [
            spec((CH, (rows - 2) * width), F32),
            spec((CH, (rows - 4) * width), F32),
            spec((n_wind, rows, width), F32),
        ],
        [vmem((16, rows * width), F32)]
        + [vmem((16, rows * width), BF16)] * 2
        + [vmem((3 * CH, (rows - 2) * width), BF16)] * 2,
        (winds, side, below, above, inside, w1, bias1_col, w2, bias2_col) + tuple(inner_net),
    )
    ring, own = (tile + 4) * width, (tile + 2) * width
    params, delta = call(
        backward_kernel,
        [spec((3 * CH, LANES), F32), spec((CH, own), F32)],
        [vmem((9 * LEVELS, rows, width), F32), vmem((CH, ring), F32)]
        + [vmem((3 * CH, ring), BF16)] * 2
        + [vmem((6 * CH, (tile + 2) * cols), BF16)] * 3
        + [vmem((16, (tile + 2) * cols), F32)],
        totals + (wind_ext, inside, first, second, head_t, w2b),
    )
    wind_grad = call(
        wind_kernel,
        spec((n_wind, tile, cols), F32),
        [vmem((3 * CH, own), BF16)] * 2 + [vmem((n_wind, tile, cols), F32)],
        totals + (wind_ext, delta, w1b),
    )
    mine, other, wind_grad, second = sum_rounds(params, ("gy", "gx"), wind_grad, second)
    tracer_grad = call(
        tracer_kernel,
        spec((count, tile, cols), BF16),
        [vmem((LEVELS, 9, tile, cols), F32), vmem((9 * LEVELS, rows, width), F32)],
        (levels, wind_ext, second, head_w, cotangent, side, below, above),
        {0: pltpu.SMEM},
    )
    conv1_grad, bias1_grad, conv2_grad, bias2_grad, head_grad = call(
        final_kernel,
        [spec(conv1.shape, F32), spec((1, CH), F32), spec(conv2.shape, F32), spec((1, CH), F32), spec(head.shape, F32)],
        [],
        (mine, other),
        flops=200_000,
    )
    return (tracer_grad, wind_grad, conv1_grad, bias1_grad[0], conv2_grad, bias2_grad[0], head_grad)


def solution(mesh):
    return jax.shard_map(
        body,
        mesh=mesh,
        in_specs=(
            P(("member", "tracer"), "gx", "gy"),
            P(("member", "tracer"), "gx", "gy"),
            P("member", "gx", "gy"),
            P(("member", "tracer")),
            P(),
            P(),
            P(),
            P(),
            P(),
        ),
        out_specs=(
            P(("member", "tracer"), "gx", "gy"),
            P("member", "gx", "gy"),
            P("member", None),
            P("member"),
            P("member", None),
            P("member"),
            P("member", None),
        ),
        check_vma=False,
    )
```

```python
import functools

import jax
import jax.numpy as jnp
from jax import lax
from jax.experimental import pallas as pl
from jax.experimental.pallas import tpu as pltpu
from jax.sharding import PartitionSpec as P

LEVELS = 2
CH = 32
COURANT = 0.5
CORRECTION = 0.2
STEPS = (-1, 0, 1)
HALO = 4
LANES = 128
GROUP = LANES // (2 * HALO)
F32 = jnp.float32
BF16 = jnp.bfloat16
NT = (((1,), (1,)), ((), ()))


def halves(value):
    high = value.astype(BF16)
    return high, (value - high.astype(F32)).astype(BF16)


def dot3(weights, high, low):
    rows = weights.shape[0] // 2
    both = jnp.dot(weights, jnp.concatenate([high, low], axis=0), preferred_element_type=F32)
    return both[:rows] + both[rows:]


def dot3_nt(left, right):
    rows, cols = left.shape[0] // 2, right.shape[0] // 2
    out = lax.dot_general(left, right, NT, preferred_element_type=F32)
    return out[:rows, :cols] + out[:rows, cols:] + out[rows:, :cols]


def turn(value, step, axis):
    shift = (-step) % value.shape[axis]
    return pltpu.roll(value, shift, axis) if shift else value


def side_mask():
    lane = lax.broadcasted_iota(jnp.int32, (1, LANES), 1)
    return (lane < HALO) | (lane >= LANES - HALO)


def rows_of(below, above):
    return jnp.concatenate([below.astype(F32), above.astype(F32)], axis=0)


def sides_of(group, side_ref, below_ref, above_ref, channels):
    half = side_ref.shape[0] // 2
    index = channels + group % half
    where = slice(group // half * LANES, (group // half + 1) * LANES)
    return side_ref[group].astype(F32), rows_of(below_ref[index, :, where], above_ref[index, :, where])


def placed(side, j):
    return jnp.where(side_mask(), pltpu.roll(side, LANES - HALO - 2 * HALO * j, 1), 0.0)


def joined(main, side, strip, strip_side, j):
    top = jnp.concatenate([main.astype(F32), placed(side, j)], axis=1)
    return jnp.concatenate([top, jnp.concatenate([strip, placed(strip_side, j)], axis=1)], axis=0)


def cot_strip(strip, spare, part):
    slot = lax.broadcasted_iota(jnp.int32, strip.shape, 0)
    value = jnp.where(slot == 0, turn(strip, 3, 0), jnp.where(slot == 7, turn(strip, -3, 0), 0.0))
    value = jnp.where(slot == 1, spare[part : part + 1], value)
    return jnp.where(slot == 6, spare[HALO + part : HALO + part + 1], value)


def in_slots(row, *pairs):
    value = jnp.zeros(row.shape, F32)
    for slot, part in pairs:
        value = jnp.where(row == slot, part, value)
    return value


def run_copies(sources, targets, sems):
    copies = [pltpu.make_async_copy(a, b, sems.at[i]) for i, (a, b) in enumerate(zip(sources, targets))]
    for copy in copies:
        copy.start()
    for copy in copies:
        copy.wait()


def pack_kernel(odd_ref, tracer_hbm, cot_hbm, wind_hbm, out_ref, one_ref, two_ref, tracer_ref, cot_ref, wind_ref, sems):
    run_copies((tracer_hbm, cot_hbm, wind_hbm), (tracer_ref, cot_ref, wind_ref), sems)
    count, tile, cols = tracer_ref.shape
    n_wind = wind_ref.shape[0]
    lane = lax.broadcasted_iota(jnp.int32, (1, LANES), 1)
    mask = side_mask()
    odd = jnp.full((HALO, cols), odd_ref[0], jnp.int32) == 1

    def lifted(value, j):
        both = jnp.where(lane < HALO, value[:, :LANES], value[:, cols - LANES :])
        return pltpu.roll(jnp.where(mask, both, 0.0), HALO + 2 * HALO * j, 1)

    def put(entry, first, last):
        one_ref[entry] = jnp.where(odd, first, last).astype(BF16)
        two_ref[entry] = jnp.where(odd, last, first).astype(BF16)

    groups = count // GROUP
    for group in range(groups):
        totals = [jnp.zeros(out_ref.shape[1:], F32)] * 2
        for start in range(0, GROUP, 4):
            first, last = [], []
            for part in range(4):
                j = start + part
                t = group * GROUP + j
                tracer, cot = tracer_ref[t].astype(F32), cot_ref[t].astype(F32)
                totals = [totals[0] + lifted(tracer, j), totals[1] + lifted(cot, j)]
                put(
                    t,
                    jnp.concatenate([tracer[:3], cot[:1]], axis=0),
                    jnp.concatenate([cot[tile - 1 :], tracer[tile - 3 :]], axis=0),
                )
                first.append(cot[1:2])
                last.append(cot[tile - 2 : tile - 1])
            put(count + t // 4, jnp.concatenate(first, axis=0), jnp.concatenate(last, axis=0))
        out_ref[group] = totals[0].astype(BF16)
        out_ref[groups + 1 + group] = totals[1].astype(BF16)
    base = count + count // 4
    total = jnp.zeros(out_ref.shape[1:], F32)
    for i in range(n_wind):
        value = wind_ref[i]
        for part in range(3):
            high = value.astype(BF16).astype(F32)
            total = total + lifted(high, part * n_wind + i)
            put(base + part * n_wind + i, high[:HALO], high[tile - HALO :])
            value = value - high
    out_ref[groups] = total.astype(BF16)
    out_ref[2 * groups + 1] = jnp.zeros(out_ref.shape[1:], BF16)


def picker(shape, source_axis, wanted):
    source = lax.broadcasted_iota(jnp.int32, shape, source_axis)
    target = lax.broadcasted_iota(jnp.int32, shape, 1 - source_axis)
    return jnp.where(source == wanted(target), 1.0, 0.0).astype(BF16)


def prep_kernel(
    c1_hbm, b1_hbm, c2_hbm, b2_hbm, head_hbm,
    w1_ref, w2_ref, w2b_ref, w1b_ref, hw_ref, ht_ref, b1_ref, b2_ref,
    c1, b1, c2, b2, head, wide_ref, slim_ref, tall_ref, pair_ref, sems,
):
    run_copies((c1_hbm, b1_hbm, c2_hbm, b2_hbm, head_hbm), (c1, b1, c2, b2, head), sems)
    n_wind = c1.shape[1] // 9

    def wanted2(target):
        return 9 * (target & (CH - 1)) + (target >> 5)

    def wanted1(target):
        a, r = target >> 4, target & 15
        b = (r >= n_wind).astype(jnp.int32) + (r >= 2 * n_wind).astype(jnp.int32)
        return jnp.where(r < 3 * n_wind, 9 * (r - n_wind * b) + 3 * a + b, -1)

    def doubled(target, value):
        rows, depth = value.shape[0] // 2, value.shape[1]
        pair_ref[: 2 * rows, :depth] = value
        pair_ref[:rows, depth : 2 * depth] = value[:rows]
        pair_ref[rows : 2 * rows, depth : 2 * depth] = jnp.zeros((rows, depth), F32)
        target[...] = pair_ref[: 2 * rows, : 2 * depth].astype(BF16)

    both2 = jnp.concatenate(halves(c2[...]), axis=0)
    size = both2.shape[1]
    doubled(w2_ref, jnp.dot(both2, picker((size, size), 0, wanted2), preferred_element_type=F32))
    turned = lax.dot_general(picker((size, size), 1, wanted2), both2, NT, preferred_element_type=F32)
    both1 = jnp.concatenate(halves(c1[...]), axis=0)
    size = both1.shape[1]
    doubled(w1_ref, jnp.dot(both1, picker((size, 48), 0, wanted1), preferred_element_type=F32))
    turned1 = lax.dot_general(picker((48, size), 1, wanted1), both1, NT, preferred_element_type=F32)
    slim_ref[...] = jnp.zeros(slim_ref.shape, F32)
    for q in range(9):
        where = slice(q * CH, (q + 1) * CH)
        start = q // 3 * 16 + q % 3 * n_wind
        for part in range(2):
            lanes = slice(part * CH, (part + 1) * CH)
            wide_ref[lanes, where] = turned[where, lanes]
            slim_ref[16 * part : 16 * part + n_wind, where] = turned1[start : start + n_wind, lanes]
    doubled(w2b_ref, wide_ref[...])
    doubled(w1b_ref, slim_ref[...])
    tall_ref[...] = jnp.zeros(tall_ref.shape, F32)
    for level in range(LEVELS):
        rows = slice(9 * level, 9 * level + 9)
        part = head[rows, :]
        part = CORRECTION * (part - jnp.sum(part, axis=0, keepdims=True) / 9.0)
        high = part.astype(BF16).astype(F32)
        tall_ref[rows, :] = high
        tall_ref[CH + 9 * level : CH + 9 * level + 9, :] = part - high
    tall = tall_ref[...].astype(BF16)
    doubled(hw_ref, tall_ref[...])
    unit = picker((CH, CH), 0, lambda target: target)
    across = lax.dot_general(unit, tall, NT, preferred_element_type=F32)
    doubled(ht_ref, jnp.concatenate([across[:, :CH], across[:, CH:]], axis=0))
    for source, target in ((b1, b1_ref), (b2, b2_ref)):
        target[...] = jnp.sum(unit.astype(F32) * source[...], axis=1, keepdims=True)


def gap_zeroed(refs, lower):
    for ref in refs:
        for gap in (0, 1, 2, 5, 6, 7):
            for step in range(3):
                ref[step, lower + gap] = jnp.zeros(ref.shape[2:], F32)


def slot_sums(moved_ref, held_ref, lower, count, store):
    slots, rows, width = moved_ref.shape[1:]
    for level in range(LEVELS):
        trips = lax.shift_right_logical((lower if level == 0 else count - lower) + 3, 2)
        for start in range(0, width, LANES):
            lanes = slice(start, start + LANES)

            def step(trip, sums):
                for part in range(4):
                    slot = 4 * trip + part
                    slot = slot if level == 0 else slots - 1 - slot
                    near = [moved_ref[b, slot, :, lanes] for b in range(3)]
                    far = [held_ref[a, slot, :, lanes] for a in range(3)]
                    sums = tuple(sums[k] + far[k // 3] * near[k % 3] for k in range(9))
                return sums

            sums = lax.fori_loop(0, trips, step, (jnp.zeros((rows, LANES), F32),) * 9)
            for k in range(9):
                store(level, k, lanes, sums[k])


def slot_of(level, t, lower, slots):
    low = level == 0
    return jnp.where(low, lower, slots - 1 - t + lower), jnp.where(low, lower + 1, lower)


def inner_kernel(levels_ref, tracer_ref, cot_ref, side_ref, out_ref, edge_ref, moved_ref, held_ref):
    count, tile, cols = tracer_ref.shape
    slots, _, width = moved_ref.shape[1:]
    half = side_ref.shape[0] // 2
    row = lax.broadcasted_iota(jnp.int32, (tile, width), 0)
    lower = jnp.int32(0)
    for group in range(count // GROUP):
        near, far = side_ref[group].astype(F32), side_ref[half + group].astype(F32)

        def fill(entry, lower):
            for part in range(4):
                j = 4 * entry + part
                t = group * GROUP + j
                slot, lower = slot_of(levels_ref[t], t, lower, slots)
                field = jnp.concatenate([tracer_ref[t].astype(F32), placed(near, j)], axis=1)
                cot = jnp.concatenate([cot_ref[t].astype(F32), placed(far, j)], axis=1)
                for b in range(3):
                    moved_ref[b, slot] = turn(field, STEPS[b], 1)
                later, sooner = turn(cot, 1, 0), turn(cot, -1, 0)
                held_ref[0, slot] = jnp.where(row == tile - 1, 0.0, later)
                held_ref[1, slot] = cot
                held_ref[2, slot] = jnp.where(row == 0, 0.0, sooner)
                edge_ref[0, t] = turn(field, HALO, 0)
                edge_ref[1, t] = jnp.where(row == 0, sooner, later)
            return lower

        lower = lax.fori_loop(0, GROUP // 4, fill, lower)
    gap_zeroed((moved_ref, held_ref), lower)

    def store(level, k, lanes, total):
        out_ref[9 * level + k, :, lanes] = turn(total, STEPS[k // 3], 0)

    slot_sums(moved_ref, held_ref, lower, count, store)


def border_kernel(levels_ref, edge_ref, side_ref, below_ref, above_ref, out_ref, moved_ref, held_ref):
    count = levels_ref.shape[0]
    slots, rows, width = moved_ref.shape[1:]
    channels = below_ref.shape[0] - side_ref.shape[0] // 2
    groups = count // GROUP
    row = lax.broadcasted_iota(jnp.int32, (rows, width), 0)
    lower = jnp.int32(0)
    for group in range(groups):
        near = sides_of(group, side_ref, below_ref, above_ref, channels)[1]
        far = sides_of(groups + 1 + group, side_ref, below_ref, above_ref, channels)[1]

        def fill(entry, lower):
            spare = count + group * (GROUP // 4) + entry
            spare = rows_of(below_ref[spare], above_ref[spare])
            for part in range(4):
                j = 4 * entry + part
                t = group * GROUP + j
                slot, lower = slot_of(levels_ref[t], t, lower, slots)
                strip = rows_of(below_ref[t], above_ref[t])
                field = jnp.concatenate([strip, placed(near, j)], axis=1)
                field = jnp.where((row == 3) | (row == 4), edge_ref[0, t], field)
                edge = edge_ref[1, t]
                for b in range(3):
                    moved_ref[b, slot] = turn(field, STEPS[b], 1)
                next0, next1 = strip[3:4], spare[part : part + 1]
                back1, back2 = strip[4:5], spare[HALO + part : HALO + part + 1]
                where = row[:, : strip.shape[1]]
                later = in_slots(where, (0, next1), (3, next0), (5, back2), (6, back1))
                cot = in_slots(where, (0, next0), (1, next1), (6, back2), (7, back1))
                sooner = in_slots(where, (1, next0), (2, next1), (4, back1), (7, back2))
                tail, place = placed(far, j), row[:, :LANES]
                tail_later = jnp.where(place == 3, turn(tail, -3, 0), turn(tail, 1, 0))
                tail_sooner = jnp.where(place == 4, turn(tail, 3, 0), turn(tail, -1, 0))
                later = jnp.concatenate([later, tail_later], axis=1)
                sooner = jnp.concatenate([sooner, tail_sooner], axis=1)
                held_ref[0, slot] = jnp.where(row == 7, edge, later)
                held_ref[1, slot] = jnp.concatenate([cot, tail], axis=1)
                held_ref[2, slot] = jnp.where(row == 0, edge, sooner)
            return lower

        lower = lax.fori_loop(0, GROUP // 4, fill, lower)
    gap_zeroed((moved_ref, held_ref), lower)

    def store(level, k, lanes, total):
        out_ref[9 * level + k, :, lanes] = total

    slot_sums(moved_ref, held_ref, lower, count, store)


def merged(inner, border, k):
    step = STEPS[k // 3]
    if not step:
        return inner, border
    place = lax.broadcasted_iota(jnp.int32, border.shape, 0)
    last = place == (7 if step == 1 else 0)
    shifted = turn(border, step, 0)
    strip = jnp.where(last, turn(border, 5 if step == 1 else 3, 0), shifted)
    return inner + jnp.where(last, shifted, 0.0), strip


def put_moved(high_ref, low_ref, row, value, sign):
    width = value.shape[1]
    for ref, part in zip((high_ref, low_ref), halves(value)):
        for b in range(3):
            ref[b * CH : (b + 1) * CH, row * width : (row + 1) * width] = turn(part, sign * STEPS[b], 1)


def convolved(weights, high_ref, low_ref, starts, width):
    def rows(ref):
        return jnp.concatenate([ref[:, start * width : (start + 2) * width] for start in starts], axis=0)

    return dot3(weights, rows(high_ref), rows(low_ref))


def put_winds(wind_ref, stack_ref, pairs, keep):
    count = wind_ref.shape[0]
    for row, place in pairs:
        value = wind_ref[:, row, :]
        for b in range(3):
            moved = turn(value, STEPS[b], 1)[:, :keep]
            stack_ref[b * count : (b + 1) * count, place * keep : (place + 1) * keep] = moved


def network_rows(weights, bias, high_ref, low_ref, row, width):
    starts = (row, row + 1, row + 2)
    return jnp.tanh(convolved(weights, high_ref, low_ref, starts, width) + bias)


def inner_forward_kernel(
    own_ref, side_ref, inside_ref, w1_ref, b1_ref, w2_ref, b2_ref,
    first_ref, high_ref, low_ref, second_ref,
    wind_ref, stack_ref, wind_high, wind_low,
):
    count, tile, width = wind_ref.shape
    cols = own_ref.shape[2]
    side = side_ref[side_ref.shape[0] // 2 - 1].astype(F32)
    for i in range(count):
        wind_ref[i, :, :cols] = own_ref[i]
        wind_ref[i, :, cols:] = sum(placed(side, part * count + i) for part in range(3))
    stack_ref[...] = jnp.zeros(stack_ref.shape, F32)
    put_winds(wind_ref, stack_ref, [(row, row) for row in range(tile)], width)
    wind_high[...], wind_low[...] = halves(stack_ref[...])
    bias1, bias2 = b1_ref[...], b2_ref[...]
    inside = jnp.concatenate([inside_ref[...]] * 2, axis=1)
    for row in range(0, tile - 2, 2):
        value = network_rows(w1_ref[...], bias1, wind_high, wind_low, row, width) * inside
        first_ref[:, row * width : (row + 2) * width] = value
        for part in range(2):
            put_moved(high_ref, low_ref, row + part, value[:, part * width : (part + 1) * width], 1)
    for row in range(0, tile - 4, 2):
        second_ref[:, row * width : (row + 2) * width] = network_rows(w2_ref[...], bias2, high_ref, low_ref, row, width)


def forward_kernel(
    own_ref, side_ref, below_ref, above_ref, inside_ref, w1_ref, b1_ref, w2_ref, b2_ref,
    inner_first, inner_high, inner_low, inner_second,
    first_ref, second_ref, wind_ref,
    stack_ref, wind_high, wind_low, high_ref, low_ref,
):
    count, rows, width = wind_ref.shape
    tile, cols = own_ref.shape[1:]
    channels = below_ref.shape[0] - 3
    side, side_rows = sides_of(side_ref.shape[0] // 2 - 1, side_ref, below_ref, above_ref, channels)
    for i in range(count):
        wind_ref[i, HALO : HALO + tile, :cols] = own_ref[i]
        wide = [jnp.zeros((tile, LANES), F32), jnp.zeros((tile, LANES), F32)]
        strip = jnp.zeros((2 * HALO, cols), F32)
        for part in range(3):
            j = part * count + i
            wide[0] = wide[0] + placed(side, j)
            wide[1] = wide[1] + placed(side_rows, j)
            index = channels - 3 * count + j
            strip = strip + rows_of(below_ref[index], above_ref[index])
        wind_ref[i, HALO : HALO + tile, cols:] = wide[0]
        for value, where in ((strip, slice(0, cols)), (wide[1], slice(cols, width))):
            wind_ref[i, HALO + tile :, where] = value[:HALO]
            wind_ref[i, :HALO, where] = value[HALO:]
    stack_ref[...] = jnp.zeros(stack_ref.shape, F32)
    edge = HALO + 2
    put_winds(wind_ref, stack_ref, [(row, row) for row in range(rows) if row < edge or row >= rows - edge], width)
    wind_high[...], wind_low[...] = halves(stack_ref[...])
    bias1, bias2 = b1_ref[...], b2_ref[...]
    inside = jnp.concatenate([inside_ref[...]] * 2, axis=1)
    first_ref[:, HALO * width : (rows - 2 - HALO) * width] = inner_first[...]
    for row in list(range(2)) + list(range(tile - 4, tile - 2)):
        source = slice(row * width, (row + 1) * width)
        target = slice((HALO + row) * width, (HALO + row + 1) * width)
        high_ref[:, target] = inner_high[:, source]
        low_ref[:, target] = inner_low[:, source]
    for row in range(0, rows - 2, 2):
        if HALO <= row < rows - 2 - HALO:
            continue
        value = network_rows(w1_ref[...], bias1, wind_high, wind_low, row, width) * inside
        first_ref[:, row * width : (row + 2) * width] = value
        for part in range(2):
            put_moved(high_ref, low_ref, row + part, value[:, part * width : (part + 1) * width], 1)
    for row in range(0, rows - 4, 2):
        if HALO <= row < rows - 4 - HALO:
            value = inner_second[:, (row - HALO) * width : (row - HALO + 2) * width]
        else:
            value = network_rows(w2_ref[...], bias2, high_ref, low_ref, row, width)
        second_ref[:, row * width : (row + 2) * width] = value


def backward_kernel(
    inner_ref, inner_other, border_ref, border_other, wind_ref, inside_ref, first_ref, second_ref, headt_ref, w2b_ref,
    par_ref, d1_ref,
    sum_ref, g_ref, d2_high, d2_low, own2_ref, act_ref, own1_ref, wind_stack,
):
    cells = g_ref.shape[1]
    width = wind_ref.shape[2]
    cols = width - LANES
    ring = cells // width
    tile = ring - 4
    wrap = sum_ref.shape[1]
    nine = sum_ref.shape[0]
    for index in range(nine):
        inner, border = inner_ref[index] + inner_other[index], border_ref[index] + border_other[index]
        sum_ref[index, :tile], sum_ref[index, tile:] = merged(inner, border, index % 9)
    g_ref[...] = jnp.zeros(g_ref.shape, F32)
    for row in range(ring):
        g_ref[:nine, row * width : (row + 1) * width] = sum_ref[:, (row - 2) % wrap, :]
    inside = inside_ref[...]
    for ref in (own2_ref, own1_ref):
        ref[...] = jnp.zeros(ref.shape, BF16)
    wind_stack[...] = jnp.zeros(wind_stack.shape, F32)
    put_winds(wind_ref, wind_stack, [(row + 3, row) for row in range(tile + 2)], cols)
    wind_stack[12:13, :] = jnp.ones((1, wind_stack.shape[1]), F32)
    bias2 = jnp.zeros((CH, cols), F32)

    def put_own(ref, x, value):
        for half, part in enumerate(halves(value[:, :cols])):
            for a in range(3):
                start = (3 * half + a) * CH
                ref[start : start + CH, (x + a) * cols : (x + a + 1) * cols] = part

    for row in range(0, ring, 2):
        where = slice(row * width, (row + 2) * width)
        high, low = halves(g_ref[:, where])
        hidden = dot3(headt_ref[...], high, low)
        second = second_ref[:, where]
        delta = hidden * (1.0 - second * second)
        for part in range(2):
            value = delta[:, part * width : (part + 1) * width]
            put_moved(d2_high, d2_low, row + part, value, -1)
            x = row + part - 2
            if 0 <= x < tile:
                put_own(own2_ref, x, value)
                bias2 = bias2 + value[:, :cols]
    for row in range(tile + 2):
        for half, part in enumerate(halves(first_ref[:, (row + 2) * width : (row + 3) * width])):
            for b in range(3):
                start = (3 * half + b) * CH
                act_ref[start : start + CH, row * cols : (row + 1) * cols] = turn(part, STEPS[b], 1)[:, :cols]
    par_ref[...] = jnp.zeros(par_ref.shape, F32)
    par_ref[:, : 3 * CH] = dot3_nt(act_ref[...], own2_ref[...])
    par_ref[:CH, 3 * CH + 16 : 3 * CH + 17] = jnp.sum(bias2, axis=1, keepdims=True)
    inside2 = jnp.concatenate([inside] * 2, axis=1)
    for row in range(0, tile + 2, 2):
        total = convolved(w2b_ref[...], d2_high, d2_low, (row + 2, row + 1, row), width)
        first = first_ref[:, (row + 2) * width : (row + 4) * width]
        delta = total * (1.0 - first * first) * inside2
        d1_ref[:, row * width : (row + 2) * width] = delta
        for part in range(2):
            value = delta[:, part * width : (part + 1) * width]
            x = row + part - 1
            if 0 <= x < tile:
                put_own(own1_ref, x, value)
    par_ref[:, 3 * CH : 3 * CH + 16] = dot3_nt(own1_ref[...], jnp.concatenate(halves(wind_stack[...]), axis=0))

    def own_cells(ref):
        rows = [ref[:, row * width : row * width + cols] for row in range(2, 2 + tile)]
        return jnp.concatenate(halves(jnp.concatenate(rows, axis=1)), axis=0)

    raw = dot3_nt(own_cells(second_ref), own_cells(g_ref))
    for level in range(LEVELS):
        rows = slice((level + 1) * CH, (level + 2) * CH)
        par_ref[rows, 3 * CH + 16 : 3 * CH + 25] = raw[:, 9 * level : 9 * level + 9]


def wind_kernel(inner_ref, inner_other, border_ref, border_other, wind_ref, d1_ref, w1b_ref, wgrad_ref, pick2_ref, pick1_ref, d1_high, d1_low, net_ref):
    n_wind = wgrad_ref.shape[0]
    def wanted2(row):
        r = row & (LANES - 1)
        return jnp.where(r < 3 * CH, 9 * (r & (CH - 1)) + 3 * (row >> 7) + (r >> 5), -1)

    pick2_ref[...] = picker(pick2_ref.shape, 1, wanted2)

    def wanted1(row):
        a, r = row >> 7, (row & (LANES - 1)) - 3 * CH
        b = (r >= n_wind).astype(jnp.int32) + (r >= 2 * n_wind).astype(jnp.int32)
        return jnp.where((r >= 0) & (r < 3 * n_wind), 9 * (r - n_wind * b) + 3 * a + b, -1)

    pick1_ref[...] = picker(pick1_ref.shape, 1, wanted1)
    tile, cols = wgrad_ref.shape[1:]
    width = wind_ref.shape[2]
    for row in range(tile + 2):
        put_moved(d1_high, d1_low, row, d1_ref[:, row * width : (row + 1) * width], -1)
    for row in range(0, tile, 2):
        total = convolved(w1b_ref[...], d1_high, d1_low, (row + 2, row + 1, row), width)
        for part in range(2):
            net_ref[:, row + part, :] = total[:4, part * width : part * width + cols]
    for level in range(LEVELS):
        cx = COURANT * wind_ref[2 * level, HALO : HALO + tile, :cols]
        cy = COURANT * wind_ref[2 * level + 1, HALO : HALO + tile, :cols]
        px, py = lax_wendroff(cx), lax_wendroff(cy)
        dx, dy = (0.5 + cx, -2.0 * cx, cx - 0.5), (0.5 + cy, -2.0 * cy, cy - 0.5)
        gx_sum = jnp.zeros((tile, cols), F32)
        gy_sum = jnp.zeros((tile, cols), F32)
        for a in range(3):
            for b in range(3):
                k = 9 * level + 3 * a + b
                inner = inner_ref[k, :, :cols] + inner_other[k, :, :cols]
                border = border_ref[k, :, :cols] + border_other[k, :, :cols]
                grad = merged(inner, border, k % 9)[0]
                gx_sum = gx_sum + grad * (dx[a] * py[b])
                gy_sum = gy_sum + grad * (px[a] * dy[b])
        wgrad_ref[2 * level] = COURANT * gx_sum + net_ref[2 * level]
        wgrad_ref[2 * level + 1] = COURANT * gy_sum + net_ref[2 * level + 1]


def final_kernel(mine_ref, other_ref, pick2_ref, pick1_ref, c1_ref, b1_ref, c2_ref, b2_ref, head_ref):
    total = mine_ref[...] + other_ref[...]
    across = jnp.concatenate([total, jnp.zeros((LANES - total.shape[0], LANES), F32)], axis=0).T
    n_wind = c1_ref.shape[1] // 9

    def moved(value, pick_ref):
        parts = []
        for _ in range(3):
            high = value.astype(BF16)
            parts.append(jnp.concatenate([high[a * CH : (a + 1) * CH] for a in range(3)], axis=1))
            value = value - high.astype(F32)
        out = jnp.dot(jnp.concatenate(parts, axis=0), pick_ref[...], preferred_element_type=F32)
        return out[:CH] + out[CH : 2 * CH] + out[2 * CH :]

    c2_ref[...] = moved(across[: 3 * CH], pick2_ref)
    c1_ref[...] = moved(total, pick1_ref)
    b1_ref[...] = across[3 * CH + 3 * n_wind : 3 * CH + 3 * n_wind + 1, CH : 2 * CH]
    b2_ref[...] = across[3 * CH + 16 : 3 * CH + 17, :CH]
    for level in range(LEVELS):
        raw = across[3 * CH + 16 : 3 * CH + 25, (level + 1) * CH : (level + 2) * CH]
        mean = jnp.sum(raw, axis=0, keepdims=True) / 9.0
        head_ref[9 * level : 9 * level + 9, :] = CORRECTION * (raw - mean)


def lax_wendroff(courant):
    return (
        0.5 * courant + 0.5 * courant * courant,
        1.0 - courant * courant,
        0.5 * courant * courant - 0.5 * courant,
    )


def tracer_kernel(levels_ref, wind_ref, second_ref, head_ref, cot_ref, side_ref, below_ref, above_ref, out_ref, coef_ref, corr_ref):
    count, tile, cols = out_ref.shape
    width = wind_ref.shape[2]
    for row in range(0, tile + 4, 2):
        high, low = halves(second_ref[:, row * width : (row + 2) * width])
        corr = dot3(head_ref[...], high, low)
        for part in range(2):
            corr_ref[:, 2 + row + part, :] = corr[: corr_ref.shape[0], part * width : (part + 1) * width]
    for level in range(LEVELS):
        px = lax_wendroff(COURANT * wind_ref[2 * level])
        py = lax_wendroff(COURANT * wind_ref[2 * level + 1])
        for a in range(3):
            for b in range(3):
                coef = corr_ref[9 * level + 3 * a + b] + px[a] * py[b]
                coef = turn(turn(coef, -STEPS[b], 1), HALO - STEPS[a], 0)
                coef_ref[level, 3 * a + b] = coef[:tile, :cols]

    channels = below_ref.shape[0] - 3
    groups = count // GROUP
    for group in range(groups):
        sides = sides_of(groups + 1 + group, side_ref, below_ref, above_ref, channels)

        def step(entry, carry):
            spare = count + group * (GROUP // 4) + entry
            spare = rows_of(below_ref[spare], above_ref[spare])
            for part in range(4):
                j = 4 * entry + part
                t = group * GROUP + j
                level = levels_ref[t]
                strip = cot_strip(rows_of(below_ref[t], above_ref[t]), spare, part)
                field = joined(cot_ref[t], sides[0], strip, sides[1], j)
                total = jnp.zeros((tile, cols), F32)
                for b in range(3):
                    moved = turn(field, -STEPS[b], 1)
                    for a in range(3):
                        total = total + coef_ref[level, 3 * a + b] * turn(moved, -STEPS[a], 0)[:tile, :cols]
                out_ref[t] = total.astype(BF16)
            return carry

        lax.fori_loop(0, GROUP // 4, step, 0)


def call(kernel, outs, scratch, operands, spaces=None, flops=2_000_000, vmem=40):
    specs = [pl.BlockSpec(memory_space=(spaces or {}).get(i, pltpu.VMEM)) for i in range(len(operands))]
    whole = pl.BlockSpec(memory_space=pltpu.VMEM)
    return pl.pallas_call(
        kernel,
        out_shape=outs,
        in_specs=specs,
        out_specs=[whole] * len(outs) if isinstance(outs, (list, tuple)) else whole,
        scratch_shapes=scratch,
        compiler_params=pltpu.CompilerParams(vmem_limit_bytes=vmem * 1024 * 1024),
        cost_estimate=pl.CostEstimate(flops=flops, bytes_accessed=2_000_000, transcendentals=0),
    )(*operands)


def ring_pairs(size, wrap):
    up = [(i, (i + 1) % size) for i in range(size if wrap else size - 1)]
    return up, [(j, i) for i, j in up]


def sum_rounds(value, axes, early, late):
    sizes = [lax.axis_size(axis) for axis in axes]
    other = jnp.zeros_like(value)
    if any(size & (size - 1) for size in sizes):
        return lax.psum(value, axes), other, early, late
    rounds = [(axis, 1 << bit) for axis, size in zip(axes, sizes) for bit in range(size.bit_length() - 1)]
    for index, (axis, step) in enumerate(rounds):
        value = value + other
        if index == 1:
            value, early = lax.optimization_barrier((value, early))
        if index == len(rounds) - 1:
            value, late = lax.optimization_barrier((value, late))
        other = lax.ppermute(value, axis, [(i, i ^ step) for i in range(lax.axis_size(axis))])
    return value, other, early, late


def body(tracers, cotangent, winds, levels, conv1, bias1, conv2, bias2, head):
    count, tile, cols = tracers.shape
    n_wind = winds.shape[0]
    width = cols + LANES
    rows = tile + 2 * HALO
    vmem, spec = pltpu.VMEM, jax.ShapeDtypeStruct
    gy, gy_size = lax.axis_index("gy"), lax.axis_size("gy")
    gx, gx_size = lax.axis_index("gx"), lax.axis_size("gx")
    paired = gx_size % 2 == 0
    odd = (gx % 2 if paired else 0 * gx).astype(jnp.int32)
    strip = spec((count + count // 4 + 3 * n_wind, HALO, cols), BF16)
    packed, one, two = call(
        pack_kernel,
        [spec((2 * (count // GROUP) + 2, tile, LANES), BF16), strip, strip],
        [vmem((count, tile, cols), BF16)] * 2
        + [vmem((n_wind, tile, cols), F32), pltpu.SemaphoreType.DMA((3,))],
        (odd[None], tracers, cotangent, winds),
        {0: pltpu.SMEM} | {i: pltpu.HBM for i in range(1, 4)},
        vmem=60,
    )
    spare = ((0, packed.shape[0] // 2), (0, 0), (0, 0))
    one, two = lax.optimization_barrier((jnp.pad(one, spare), jnp.pad(two, spare)))
    up, down = ring_pairs(gy_size, False)
    lane = lax.broadcasted_iota(jnp.int32, (1, 1, LANES), 2) % (2 * HALO)
    if gy_size == 2:
        got = lax.ppermute(packed, "gy", up + down)
        side = jnp.where(jnp.where(gy == 0, lane >= HALO, lane < HALO), got, 0)
    else:
        right = lax.ppermute(packed, "gy", down)
        left = lax.ppermute(packed, "gy", up)
        side = jnp.where(lane >= HALO, right, left)
    side = side.astype(BF16)
    w1, w2, w2b, w1b, head_w, head_t, bias1_col, bias2_col = call(
        prep_kernel,
        [
            spec((2 * CH, 96), BF16),
            spec((2 * CH, 18 * CH), BF16),
            spec((2 * CH, 18 * CH), BF16),
            spec((32, 18 * CH), BF16),
            spec((2 * CH, 2 * CH), BF16),
            spec((2 * CH, 2 * CH), BF16),
            spec((CH, 1), F32),
            spec((CH, 1), F32),
        ],
        [
            vmem(conv1.shape, F32),
            vmem((1, CH), F32),
            vmem(conv2.shape, F32),
            vmem((1, CH), F32),
            vmem(head.shape, F32),
            vmem((2 * CH, 9 * CH), F32),
            vmem((32, 9 * CH), F32),
            vmem((2 * CH, CH), F32),
            vmem((2 * CH, 18 * CH), F32),
            pltpu.SemaphoreType.DMA((5,)),
        ],
        lax.optimization_barrier((conv1, bias1[None], conv2, bias2[None], head, side))[:5],
        {i: pltpu.HBM for i in range(5)},
    )
    half = side.shape[0] // 2
    wide = jnp.concatenate([side[:half], side[half:]], axis=2)
    first_rows, last_rows = wide[:, :HALO], wide[:, tile - HALO :]
    is_odd = odd == 1
    one = lax.dynamic_update_slice(one, jnp.where(is_odd, first_rows, last_rows), (one.shape[0] - half, 0, 0))
    two = lax.dynamic_update_slice(two, jnp.where(is_odd, last_rows, first_rows), (two.shape[0] - half, 0, 0))
    if paired:
        ahead = [(i, i ^ 1) for i in range(gx_size)]
        behind = [(i, (i + 1) % gx_size if i % 2 else (i - 1) % gx_size) for i in range(gx_size)]
        one, two = lax.ppermute(one, "gx", ahead), lax.ppermute(two, "gx", behind)
        below, above = jnp.where(is_odd, two, one), jnp.where(is_odd, one, two)
    else:
        up, down = ring_pairs(gx_size, True)
        above, below = lax.ppermute(one, "gx", up), lax.ppermute(two, "gx", down)
    place = lax.broadcasted_iota(jnp.int32, (1, width), 1)
    has_right, has_left = gy < gy_size - 1, gy > 0
    inside = jnp.where(place < cols, True, jnp.where(place < cols + LANES // 2, has_right, has_left)).astype(F32)

    levels = jnp.clip(levels, 0, LEVELS - 1)
    inner, edge = call(
        inner_kernel,
        [spec((9 * LEVELS, tile, width), F32), spec((2, count, tile, width), F32)],
        [vmem((3, count + 8, tile, width), F32)] * 2,
        (levels, tracers, cotangent, side),
        {0: pltpu.SMEM},
    )
    inner_net = call(
        inner_forward_kernel,
        [
            spec((CH, (tile - 2) * width), F32),
            spec((3 * CH, (tile - 2) * width), BF16),
            spec((3 * CH, (tile - 2) * width), BF16),
            spec((CH, (tile - 4) * width), F32),
        ],
        [vmem((n_wind, tile, width), F32), vmem((16, tile * width), F32)] + [vmem((16, tile * width), BF16)] * 2,
        (winds, side, inside, w1, bias1_col, w2, bias2_col),
    )
    cores = [(i, i ^ 1) for i in range(lax.axis_size("tracer"))]
    inner_other = lax.ppermute(inner, "tracer", cores)
    above, below, inner_net, inner, inner_other = lax.optimization_barrier((above, below, inner_net, inner, inner_other))
    border = call(
        border_kernel,
        spec((9 * LEVELS, 2 * HALO, width), F32),
        [vmem((3, count + 8, 2 * HALO, width), F32)] * 2,
        (levels, edge, side, below, above),
        {0: pltpu.SMEM},
    )
    totals = (inner, inner_other, border, lax.ppermute(border, "tracer", cores))
    first, second, wind_ext = call(
        forward_kernel,
        [
            spec((CH, (rows - 2) * width), F32),
            spec((CH, (rows - 4) * width), F32),
            spec((n_wind, rows, width), F32),
        ],
        [vmem((16, rows * width), F32)]
        + [vmem((16, rows * width), BF16)] * 2
        + [vmem((3 * CH, (rows - 2) * width), BF16)] * 2,
        (winds, side, below, above, inside, w1, bias1_col, w2, bias2_col) + tuple(inner_net),
    )
    ring, own = (tile + 4) * width, (tile + 2) * width
    params, delta = call(
        backward_kernel,
        [spec((3 * CH, LANES), F32), spec((CH, own), F32)],
        [vmem((9 * LEVELS, rows, width), F32), vmem((CH, ring), F32)]
        + [vmem((3 * CH, ring), BF16)] * 2
        + [vmem((6 * CH, (tile + 2) * cols), BF16)] * 3
        + [vmem((16, (tile + 2) * cols), F32)],
        totals + (wind_ext, inside, first, second, head_t, w2b),
    )
    early = call(
        wind_kernel,
        [spec((n_wind, tile, cols), F32), spec((3 * LANES, 9 * CH), BF16), spec((3 * LANES, conv1.shape[1]), BF16)],
        [vmem((3 * CH, own), BF16)] * 2 + [vmem((n_wind, tile, cols), F32)],
        totals + (wind_ext, delta, w1b),
    )
    mine, other, early, second = sum_rounds(params, ("gy", "gx"), early, second)
    wind_grad, pick2, pick1 = early
    tracer_grad = call(
        tracer_kernel,
        spec((count, tile, cols), BF16),
        [vmem((LEVELS, 9, tile, cols), F32), vmem((9 * LEVELS, rows, width), F32)],
        (levels, wind_ext, second, head_w, cotangent, side, below, above),
        {0: pltpu.SMEM},
    )
    conv1_grad, bias1_grad, conv2_grad, bias2_grad, head_grad = call(
        final_kernel,
        [spec(conv1.shape, F32), spec((1, CH), F32), spec(conv2.shape, F32), spec((1, CH), F32), spec(head.shape, F32)],
        [],
        (mine, other, pick2, pick1),
        flops=200_000,
    )
    return (tracer_grad, wind_grad, conv1_grad, bias1_grad[0], conv2_grad, bias2_grad[0], head_grad)


def solution(mesh):
    return jax.shard_map(
        body,
        mesh=mesh,
        in_specs=(
            P(("member", "tracer"), "gx", "gy"),
            P(("member", "tracer"), "gx", "gy"),
            P("member", "gx", "gy"),
            P(("member", "tracer")),
            P(),
            P(),
            P(),
            P(),
            P(),
        ),
        out_specs=(
            P(("member", "tracer"), "gx", "gy"),
            P("member", "gx", "gy"),
            P("member", None),
            P("member"),
            P("member", None),
            P("member"),
            P("member", None),
        ),
        check_vma=False,
    )
```
